32 devices in a mesh: seq: 4 (over z), fsdp: 8 (over y, x, core).
Axes of the slice: x: 2, y: 2, z: 4, core: 2. Of those that a mesh axis runs over, the one named last changes fastest.
Arguments:
- hidden_in: bfloat16 [8, 2048, 1024], P('fsdp', 'seq'), may hold values from -6 to 6
- cotangent: bfloat16 [8, 2048, 1024], P('fsdp', 'seq'), may hold values from -6 to 6
- norm_gain: bfloat16 [2, 1024], P(None, 'fsdp'), may hold values from 0.25 to 1.75
- input_projection_weight: bfloat16 [2, 1024, 4384], P(None, 'fsdp'), may hold values from -0.1875 to 0.1875
- conv_weight: bfloat16 [2, 4, 2304], P(None, None, 'fsdp'), may hold values from -3 to 3
- conv_bias: bfloat16 [2, 2304], P(None, 'fsdp'), may hold values from -1 to 1
- dt_bias: bfloat16 [2, 32], P(None, 'fsdp'), may hold values from -9 to -4
- a_log: bfloat16 [2, 32], P(None, 'fsdp'), may hold values from 0 to 2.5
- skip: bfloat16 [2, 32], P(None, 'fsdp'), may hold values from 0.5 to 1.5
- gate_gain: bfloat16 [2, 2048], P(None, 'fsdp'), may hold values from 0.25 to 1.75
- output_projection_weight: bfloat16 [2, 2048, 1024], P(None, 'fsdp'), may hold values from -0.125 to 0.125
Outputs:
- block_out: bfloat16 [8, 2048, 1024], P('fsdp', 'seq')
- input_grad: float32 [8, 2048, 1024], P('fsdp', 'seq')
- norm_gain_grad: float32 [2, 1024], P(None, 'fsdp')
- in_weight_grad: float32 [2, 1024, 4384], P(None, 'fsdp')
- conv_weight_grad: float32 [2, 4, 2304], P(None, None, 'fsdp')
- conv_bias_grad: float32 [2, 2304], P(None, 'fsdp')
- dt_bias_grad: float32 [2, 32], P(None, 'fsdp')
- a_log_grad: float32 [2, 32], P(None, 'fsdp')
- skip_grad: float32 [2, 32], P(None, 'fsdp')
- gate_gain_grad: float32 [2, 2048], P(None, 'fsdp')
- out_weight_grad: float32 [2, 2048, 1024], P(None, 'fsdp')
The draws below stay inside these ranges and needn't reach their ends.
All inputs are finite; a program needn't handle non-finite values.
Results may differ from the reference program's by a relative error of at most 0.019.
Values may be sent and summed in bfloat16 or wider, within the bound.
No kernel may reach another device: no remote copies, remote signals or barrier semaphores. Data moves between devices by JAX's collectives and lax.ppermute only.
A program may use at most 320 MiB of HBM per device.

```python
import jax
import jax.numpy as jnp
from jax import lax

D = 1024
H = 32
P_SIZE = 64
N = 128
GROUP = 256
KERNEL = 4
LAYERS = 2
DI = 2048
CC = 2304
PROJ = 4384
LENGTH = 2048
SEQS = 8


def steps_of(rng, extent, split, smallest, top_value):
    def one(dim, shards_of):
        heights = jax.random.uniform(jax.random.fold_in(jax.random.fold_in(rng, 6), dim), (shards_of,), jnp.float32, smallest / len(split), top_value / len(split))
        return jnp.repeat(jnp.exp(heights), extent[dim] // shards_of).reshape((-1,) + (1,) * (len(extent) - dim - 1))

    gain = one(*split[0])
    for cut in split[1:]:
        gain = gain * one(*cut)
    return gain


def scatter_about(stream_key, extent, spread, most, shards=(), held_as=jnp.bfloat16):
    loudness = steps_of(stream_key, extent, shards, -0.22, 0.18) if shards else 1.0
    values = jax.random.normal(stream_key, extent, jnp.float32) * spread * loudness
    return jnp.minimum(jnp.maximum(values, -most), most).astype(held_as)


def setup_inputs(seed: int = 0) -> dict:
    arg_keys = jax.random.split(jax.random.key(seed), 12)
    return {
        "hidden_in": scatter_about(arg_keys[0], (SEQS, LENGTH, D), 1.0, 6.0, ((0, 8), (1, 4))),
        "cotangent": scatter_about(arg_keys[1], (SEQS, LENGTH, D), 1.0, 6.0, ((0, 8), (1, 4))),
        "norm_gain": jnp.clip(1.0 + 0.15 * jax.random.normal(arg_keys[2], (LAYERS, D), jnp.float32), 0.25, 1.75).astype(jnp.bfloat16),
        "input_projection_weight": scatter_about(arg_keys[3], (LAYERS, D, PROJ), D ** -0.5, 0.1875, ((1, 8),)),
        "conv_weight": scatter_about(arg_keys[4], (LAYERS, KERNEL, CC), KERNEL ** -0.5, 3.0, ((2, 8),)),
        "conv_bias": jnp.clip(jax.random.uniform(arg_keys[5], (LAYERS, CC), jnp.float32, -1.0, 1.0) * steps_of(arg_keys[5], (LAYERS, CC), ((1, 8),), -0.4, 0.0), -1.0, 1.0).astype(jnp.bfloat16),
        "dt_bias": jnp.clip(-9.0 + 5.0 * jax.random.uniform(arg_keys[6], (LAYERS, H), jnp.float32) ** steps_of(arg_keys[6], (LAYERS, H), ((1, 8),), -0.2, 0.2), -9.0, -4.0).astype(jnp.bfloat16),
        "a_log": jnp.clip(2.5 * jax.random.uniform(arg_keys[7], (LAYERS, H), jnp.float32) ** steps_of(arg_keys[7], (LAYERS, H), ((1, 8),), -0.2, 0.2), 0.0, 2.5).astype(jnp.bfloat16),
        "skip": jnp.clip(0.5 + 1.0 * jax.random.uniform(arg_keys[8], (LAYERS, H), jnp.float32) ** steps_of(arg_keys[8], (LAYERS, H), ((1, 8),), -0.2, 0.2), 0.5, 1.5).astype(jnp.bfloat16),
        "gate_gain": jnp.clip(1.0 + 0.15 * jax.random.normal(arg_keys[9], (LAYERS, DI), jnp.float32), 0.25, 1.75).astype(jnp.bfloat16),
        "output_projection_weight": scatter_about(arg_keys[10], (LAYERS, DI, D), DI ** -0.5, 0.125, ((1, 8),)),
    }


epsilon = 1e-05
highest_precision = lax.Precision.HIGHEST

@jax.custom_vjp
def low(v):
    return lax.optimization_barrier(v.astype(jnp.bfloat16)).astype(jnp.float32)

@jax.custom_vjp
def low_back(v):
    return v

def low_keep(v):
    return (low(v), None)

def low_pass(kept, grad):
    return (grad,)

def back_keep(v):
    return (v, None)

def back_low(kept, grad):
    return (low(grad),)
low.defvjp(low_keep, low_pass)
low_back.defvjp(back_keep, back_low)

def rms_scale(values):
    return lax.rsqrt(lax.optimization_barrier(jnp.mean(values * values, axis=-1, keepdims=True)) + epsilon)

def causal_conv(values, taps, shift):
    length = values.shape[0]
    reach = taps.shape[0]
    padded = jnp.pad(values, ((reach - 1, 0), (0, 0)))
    total = shift[None, :] + jnp.zeros_like(values)
    for offset in range(reach):
        total = total + taps[offset][None, :] * padded[offset:offset + length]
    return total

def block_scan(values, steps_dt, decay_rate, bmatrix, cmatrix):
    length, head_count, head_width = values.shape
    blocks = length // GROUP
    causal_mask = jnp.tril(jnp.ones((GROUP, GROUP), jnp.float32))

    def one_block(carry_state, pieces):
        xblock, dblock, bblock, cblock = pieces
        cumulative = jnp.cumsum(dblock * decay_rate[None, :], axis=0)
        across = jnp.transpose(cumulative)
        scores = jnp.dot(cblock, jnp.transpose(bblock), precision=highest_precision) * causal_mask
        decays = jnp.exp(jnp.minimum(across[:, :, None] - across[:, None, :], 0.0))
        weights = decays * scores[None, :, :] * jnp.transpose(dblock)[:, None, :]
        inside = jnp.einsum('hts,shp->thp', weights, xblock, precision=highest_precision)
        carried = jnp.einsum('tn,hpn->thp', cblock, carry_state, precision=highest_precision) * jnp.exp(cumulative)[:, :, None]
        tail_weight = jnp.exp(cumulative[-1][None, :] - cumulative) * dblock
        fresh_state = jnp.einsum('sh,shp,sn->hpn', tail_weight, xblock, bblock, precision=highest_precision)
        carry_state = carry_state * jnp.exp(cumulative[-1])[:, None, None] + fresh_state
        return (carry_state, inside + carried)
    initial = jnp.zeros((head_count, head_width, bmatrix.shape[1]), jnp.float32)
    pieces = (values.reshape(blocks, GROUP, head_count, head_width), steps_dt.reshape(blocks, GROUP, head_count), bmatrix.reshape(blocks, GROUP, bmatrix.shape[1]), cmatrix.reshape(blocks, GROUP, cmatrix.shape[1]))
    final_state, outputs = lax.scan(jax.checkpoint(one_block), initial, pieces)
    return outputs.reshape(length, head_count, head_width)

def mix_layer(x_part, dt_part, bc_part, x_taps, bc_taps, x_shift, bc_shift, bias_dt, log_rate, skip_gain):
    length, head_count, head_width = x_part.shape
    states = bc_part.shape[1] // 2
    xs_conv = causal_conv(x_part.reshape(length, head_count * head_width), x_taps, x_shift)
    xs_act = jax.nn.silu(xs_conv).reshape(length, head_count, head_width)
    bc_act = jax.nn.silu(causal_conv(bc_part, bc_taps, bc_shift))
    steps_dt = jax.nn.softplus(dt_part + bias_dt[None, :])
    decay_rate = -jnp.exp(log_rate)
    scanned = block_scan(xs_act, steps_dt, decay_rate, bc_act[:, :states], bc_act[:, states:])
    return scanned + skip_gain[None, :, None] * xs_act

def forward(hidden, norm_gain, input_projection_weight, conv_weight, conv_bias, dt_bias, a_log, skip, gate_gain, output_projection_weight):
    seq_count, length, model_width = hidden.shape
    for current_layer_index in range(LAYERS):
        normed_layer_input = low(hidden * rms_scale(hidden) * norm_gain[current_layer_index])
        projected_input = low_back(jnp.einsum('gvm,mu->gvu', normed_layer_input, input_projection_weight[current_layer_index], precision=highest_precision))
        gate_part = projected_input[:, :, :DI]
        x_part = low(projected_input[:, :, DI:2 * DI]).reshape(seq_count, length, H, P_SIZE)
        bc_part = low(projected_input[:, :, 2 * DI:2 * DI + 2 * N])
        dt_part = low(projected_input[:, :, 2 * DI + 2 * N:])
        layer_taps = conv_weight[current_layer_index]
        layer_shift = conv_bias[current_layer_index]
        layer_bias = dt_bias[current_layer_index]
        layer_rate = a_log[current_layer_index]
        layer_skip = skip[current_layer_index]

        def one_sequence(pieces):
            return mix_layer(pieces[0], pieces[1], pieces[2], layer_taps[:, :DI], layer_taps[:, DI:], layer_shift[:DI], layer_shift[DI:], layer_bias, layer_rate, layer_skip)
        mixed = lax.map(jax.checkpoint(one_sequence), (x_part, dt_part, bc_part))
        mixed = low_back(low(mixed.reshape(seq_count, length, DI)))
        gated = mixed * jax.nn.silu(gate_part)
        normed_gate_value = low(gated * rms_scale(gated) * gate_gain[current_layer_index])
        branch_output = low_back(jnp.einsum('itj,jy->ity', normed_gate_value, output_projection_weight[current_layer_index], precision=highest_precision))
        hidden = hidden + branch_output
    return hidden

def reference(hidden_in, cotangent, norm_gain, input_projection_weight, conv_weight, conv_bias, dt_bias, a_log, skip, gate_gain, output_projection_weight):
    params = [p.astype(jnp.float32) for p in (norm_gain, input_projection_weight, conv_weight, conv_bias, dt_bias, a_log, skip, gate_gain, output_projection_weight)]
    result, pullback = jax.vjp(forward, hidden_in.astype(jnp.float32), params[0], params[1], params[2], params[3], params[4], params[5], params[6], params[7], params[8])
    grads = pullback(cotangent.astype(jnp.float32))
    return (result.astype(jnp.bfloat16), grads[0], grads[1], grads[2], grads[3], grads[4], grads[5], grads[6], grads[7], grads[8], grads[9])
```

```python
import jax
import jax.numpy as jnp
from jax import lax
from jax.experimental import pallas as pl
from jax.experimental.pallas import tpu as pltpu
from jax.sharding import PartitionSpec as P

H = 32
P_SIZE = 64
N = 128
DI = 2048
CC = DI + 2 * N
T = 128
WB = 256
HB = WB // P_SIZE
STEPS = DI // WB
HALO = 16
F32 = jnp.float32
BF16 = jnp.bfloat16
EPS = 1e-05
VMEM_LIMIT = 50 * 1024 * 1024

L_STEP, L_CUM, L_CUMF, L_SIG = 0, 32, 64, 96


def dot(a, b):
    return jnp.dot(a, b, preferred_element_type=F32)


def dot_nt(a, b):
    return lax.dot_general(a, b, (((1,), (1,)), ((), ())), preferred_element_type=F32)


def dot_tn(a, b):
    return lax.dot_general(a, b, (((0,), (0,)), ((), ())), preferred_element_type=F32)


def sigmoid(v):
    return 1.0 / (1.0 + jnp.exp(-v))


def lane_iota(rows, lanes=128):
    return lax.broadcasted_iota(jnp.int32, (rows, lanes), 1)


def row_iota(rows, lanes=128):
    return lax.broadcasted_iota(jnp.int32, (rows, lanes), 0)


def column(cols, lane):
    return jnp.broadcast_to(cols[:, lane : lane + 1], (cols.shape[0], 128))


def widen(columns):
    left = lane_iota(columns[0].shape[0]) < P_SIZE
    tiles = [
        jnp.where(left, columns[2 * p], columns[2 * p + 1]) for p in range(len(columns) // 2)
    ]
    return jnp.concatenate(tiles, axis=1)


def spread(cols, lane, heads):
    return widen([column(cols, lane + h) for h in range(heads)])


def halves(tile, axis_rows=True):
    left = lane_iota(tile.shape[0]) < P_SIZE
    zero = jnp.zeros_like(tile)
    return jnp.concatenate([jnp.where(left, tile, zero), jnp.where(left, zero, tile)], axis=0)


def head_columns(cols, i):
    return pltpu.roll(cols, lax.rem(128 - HB * i, 128), 1)


def head_row(pt_ref, i, h, tokens):
    eight = pl.multiple_of(L_CUM + 8 * lax.shift_right_logical(i, 1), 8)
    block = pt_ref[pl.ds(eight, 8), tokens]
    odd = jnp.full((1, T), lax.rem(i, 2), jnp.int32) == 1
    return jnp.where(odd, block[HB + h : HB + h + 1, :], block[h : h + 1, :])


def fill(ext, halo_ref, v_ref):
    ext[0:HALO, :] = halo_ref[...].astype(F32)
    ext[HALO:, :] = v_ref[...].astype(F32)


def conv_block(ext, taps_ref, shift_ref, c):
    total = shift_ref[0:1, :] + taps_ref[0:1, :] * ext[pl.ds(HALO - 3 + c * T, T), :]
    for k in range(1, 4):
        total = total + taps_ref[k : k + 1, :] * ext[pl.ds(HALO - 3 + k + c * T, T), :]
    return total


def state_kernel(
    v_ref, halo_ref, bc_ref, bchalo_ref, dt_ref, taps_ref, shift_ref, bctaps_ref, bcshift_ref,
    prm_ref, f_ref, tot_ref, p_ref, pt_ref, b_ref, c_ref, bt_ref, ct_ref, ext,
):
    i = pl.program_id(0)
    blocks = v_ref.shape[0] // T

    @pl.when(i == 0)
    def _():
        fill(ext, bchalo_ref, bc_ref)
        lane = lane_iota(T)
        tril = (row_iota(T) >= lane).astype(F32)
        offset = jnp.zeros((1, 128), F32)
        for c in range(blocks):
            rows = pl.ds(c * T, T)
            conv = conv_block(ext, bctaps_ref, bcshift_ref, c)
            act = conv * sigmoid(conv)
            b_ref[rows, :] = act[:, :N].astype(BF16)
            c_ref[rows, :] = act[:, N:].astype(BF16)
            bt_ref[:, rows] = act[:, :N].T.astype(BF16)
            ct_ref[:, rows] = act[:, N:].T.astype(BF16)
            z = dt_ref[rows, :].astype(F32) + prm_ref[0:1, :]
            step = jnp.maximum(z, 0.0) + jnp.log1p(jnp.exp(-jnp.abs(z)))
            decay = step * prm_ref[1:2, :]
            cum = lax.dot_general(
                tril, decay, (((1,), (0,)), ((), ())),
                precision=lax.Precision.HIGHEST, preferred_element_type=F32,
            )
            cumf = cum + offset
            offset = cumf[T - 1 : T, :]
            packed = jnp.where(
                lane < L_CUM, step,
                jnp.where(lane < L_CUMF, cum, jnp.where(lane < L_SIG, cumf, sigmoid(z))),
            )
            p_ref[rows, :] = packed
            pt_ref[:, rows] = packed.T

    fill(ext, halo_ref, v_ref)
    last = head_columns(p_ref[pl.ds(blocks * T - 8, 8), :], i)
    tot = spread(last, L_CUMF, HB)[7:8, :]
    total = jnp.zeros((N, WB), F32)
    for c in range(blocks):
        rows = pl.ds(c * T, T)
        conv = conv_block(ext, taps_ref, shift_ref, c)
        cols = head_columns(p_ref[rows, :], i)
        w = jnp.exp(tot - spread(cols, L_CUMF, HB)) * spread(cols, L_STEP, HB)
        wx = (conv * sigmoid(conv) * w).astype(BF16)
        total = total + dot(bt_ref[:, rows], wx)
    f_ref[...] = total.astype(BF16)
    tot_ref[...] = jnp.broadcast_to(jnp.exp(tot), (8, WB))


def scan_kernel(
    v_ref, halo_ref, taps_ref, shift_ref, skip_ref, p_ref, pt_ref, b_ref, c_ref, bt_ref,
    y_ref, ext, cb,
):
    i = pl.program_id(0)
    blocks = v_ref.shape[0] // T

    @pl.when(i == 0)
    def _():
        causal = row_iota(T) >= lane_iota(T)
        for c in range(blocks):
            rows = pl.ds(c * T, T)
            cb[c] = jnp.where(causal, dot_nt(c_ref[rows, :], b_ref[rows, :]), 0.0)

    fill(ext, halo_ref, v_ref)
    state = None
    for c in range(blocks):
        rows = pl.ds(c * T, T)
        conv = conv_block(ext, taps_ref, shift_ref, c)
        x = conv * sigmoid(conv)
        cols = head_columns(p_ref[rows, :], i)
        cums = [column(cols, L_CUM + h) for h in range(HB)]
        xd = x * spread(cols, L_STEP, HB)
        parts = []
        for p in range(HB // 2):
            weights = []
            for h in (2 * p, 2 * p + 1):
                across = head_row(pt_ref, i, h, rows)
                weights.append(
                    (jnp.exp(jnp.minimum(cums[h] - across, 0.0)) * cb[c]).astype(BF16)
                )
            parts.append(
                dot(
                    jnp.concatenate(weights, axis=1),
                    halves(xd[:, p * 128 : (p + 1) * 128]).astype(BF16),
                )
            )
        y = jnp.concatenate(parts, axis=1) + skip_ref[0:1, :] * x
        cumx = widen(cums)
        if state is not None:
            y = y + jnp.exp(cumx) * dot(c_ref[rows, :], state.astype(BF16))
        y_ref[rows, :] = y
        if c < blocks - 1:
            tot = cumx[T - 1 : T, :]
            fresh = dot(bt_ref[:, rows], (jnp.exp(tot - cumx) * xd).astype(BF16))
            state = fresh if state is None else state * jnp.exp(tot) + fresh


def gate_kernel(y_ref, gate_ref, p_ref, c_ref, s_ref, gain_ref, out_y_ref, out_ref):
    grow = spread(jnp.exp(p_ref[...]), L_CUMF, H)
    y = y_ref[...] + grow * dot(c_ref[...], s_ref[...])
    out_y_ref[...] = y
    mixed = y.astype(BF16).astype(F32)
    gate = gate_ref[...]
    gated = mixed * (gate * sigmoid(gate))
    r = lax.rsqrt(jnp.mean(gated * gated, axis=1, keepdims=True) + EPS)
    out_ref[...] = (gated * r * gain_ref[0:1, :]).astype(BF16)


def gate_back_kernel(
    y_ref, gate_ref, dgn_ref, p_ref, ct_ref, gain_ref, dgate_ref, dmix_ref, gg_ref, g_ref, acc
):
    i = pl.program_id(0)

    @pl.when(i == 0)
    def _():
        acc[...] = jnp.zeros_like(acc)
        gg_ref[...] = jnp.zeros_like(gg_ref)

    mixed = y_ref[...].astype(BF16).astype(F32)
    gate = gate_ref[...]
    sig = sigmoid(gate)
    silu = gate * sig
    gated = mixed * silu
    r = lax.rsqrt(jnp.mean(gated * gated, axis=1, keepdims=True) + EPS)
    q = gated * r
    dgn = dgn_ref[...]
    gg_ref[...] += jnp.broadcast_to(jnp.sum(dgn * q, axis=0, keepdims=True), gg_ref.shape)
    dq = dgn * gain_ref[0:1, :]
    dgated = r * (dq - q * jnp.mean(dq * q, axis=1, keepdims=True))
    dgate_ref[...] = (dgated * mixed * (sig * (1.0 + gate * (1.0 - sig)))).astype(BF16)
    dmix = (dgated * silu).astype(BF16)
    dmix_ref[...] = dmix
    grow = spread(jnp.exp(p_ref[...]), L_CUMF, H)
    acc[...] += dot(ct_ref[...], (grow * dmix.astype(F32)).astype(BF16))

    @pl.when(i == pl.num_programs(0) - 1)
    def _():
        g_ref[...] = acc[...].astype(BF16)


def conv_back(ext, dext, taps_ref, dv_ref, tail_ref, head_ref, stats_ref, blocks):
    sums = [jnp.zeros((1, WB), F32) for _ in range(5)]
    for c in range(blocks):
        d = dext[pl.ds(c * T, T), :]
        total = taps_ref[3:4, :] * d
        for k in range(3):
            total = total + taps_ref[k : k + 1, :] * dext[pl.ds(c * T + 3 - k, T), :]
        dv_ref[pl.ds(c * T, T), :] = total.astype(BF16)
        if c == blocks - 1:
            tail_ref[...] = total[T - 8 :, :]
        for k in range(4):
            v = ext[pl.ds(HALO - 3 + k + c * T, T), :]
            sums[k] = sums[k] + jnp.sum(d * v, axis=0, keepdims=True)
        sums[4] = sums[4] + jnp.sum(d, axis=0, keepdims=True)
    head_ref[...] = dext[0:8, :]
    for k in range(5):
        stats_ref[k : k + 1, :] = sums[k]


def back_kernel(
    v_ref, halo_ref, bc_ref, bchalo_ref, taps_ref, shift_ref, bctaps_ref, bcshift_ref, skip_ref,
    prm_ref, p_ref, pt_ref, b_ref, c_ref, bt_ref, ct_ref, s_ref, gin_ref, dy_ref, y_ref,
    dv_ref, tail_ref, head_ref, stats_ref, bdv_ref, btail_ref, bhead_ref, bstats_ref,
    ddt_ref, dtstats_ref,
    ext, dext, convs, sigs, cbt, dcbt, acc, dbacc, dcacc,
):
    i = pl.program_id(0)
    blocks = v_ref.shape[0] // T
    length = blocks * T

    @pl.when(i == 0)
    def _():
        causal = row_iota(T) <= lane_iota(T)
        for c in range(blocks):
            rows = pl.ds(c * T, T)
            cbt[c] = jnp.where(causal, dot_nt(b_ref[rows, :], c_ref[rows, :]), 0.0)
        dcbt[...] = jnp.zeros_like(dcbt)
        acc[...] = jnp.zeros_like(acc)
        dbacc[...] = jnp.zeros_like(dbacc)
        dcacc[...] = jnp.zeros_like(dcacc)

    fill(ext, halo_ref, v_ref)
    dext[length:, :] = jnp.zeros((8, WB), F32)
    states = [s_ref[...].astype(F32)]
    for c in range(blocks):
        rows = pl.ds(c * T, T)
        conv = conv_block(ext, taps_ref, shift_ref, c)
        sig = sigmoid(conv)
        convs[rows, :] = conv
        sigs[rows, :] = sig
        cols = head_columns(p_ref[rows, :], i)
        cumx = spread(cols, L_CUM, HB)
        tot = cumx[T - 1 : T, :]
        wx = (jnp.exp(tot - cumx) * (conv * sig * spread(cols, L_STEP, HB))).astype(BF16)
        states.append(states[-1] * jnp.exp(tot) + dot(bt_ref[:, rows], wx))

    ch = lax.shift_right_logical(row_iota(WB), 6)
    seg1 = (lane_iota(WB) == HB * i + ch).astype(BF16)
    seg2 = (lane_iota(WB) == 32 + HB * i + ch).astype(BF16)
    final = row_iota(T, WB) == T - 1
    grad = gin_ref[...].astype(F32)
    skip_sum = jnp.zeros((1, WB), F32)
    for c in reversed(range(blocks)):
        rows = pl.ds(c * T, T)
        conv, sig = convs[rows, :], sigs[rows, :]
        x = conv * sig
        cols = head_columns(p_ref[rows, :], i)
        cums = [column(cols, L_CUM + h) for h in range(HB)]
        cumx = widen(cums)
        dt = spread(cols, L_STEP, HB)
        tot = cumx[T - 1 : T, :]
        xd = x * dt
        xdb = xd.astype(BF16)
        dyb = dy_ref[rows, :]
        dy = dyb.astype(F32)
        parts = []
        for p in range(HB // 2):
            lanes = slice(p * 128, (p + 1) * 128)
            dm = dot_nt(halves(xd[:, lanes]).astype(BF16), dyb[:, lanes])
            weights = []
            for j in range(2):
                h = 2 * p + j
                across = head_row(pt_ref, i, h, rows)
                e = jnp.exp(jnp.minimum(across - cums[h], 0.0))
                weights.append((e * cbt[c]).astype(BF16))
                dcbt[c] += dm[j * T : (j + 1) * T, :] * e
            parts.append(
                dot(jnp.concatenate(weights, axis=1), halves(dy[:, lanes]).astype(BF16))
            )
        gb = grad.astype(BF16)
        w = jnp.exp(tot - cumx)
        dxd = jnp.concatenate(parts, axis=1) + w * dot(b_ref[rows, :], gb)
        ey = (jnp.exp(cumx) * dy).astype(BF16)
        wx = (w * xd).astype(BF16)
        dcacc[rows, :] += dot_nt(ey, states[c].astype(BF16))
        dbacc[rows, :] += dot_nt(wx, gb)
        bound = jnp.sum(grad * states[c + 1], axis=0, keepdims=True)
        skip = skip_ref[0:1, :]
        p1 = dy * (y_ref[rows, :] - skip * x) - xdb.astype(F32) * dxd
        p1 = p1 + jnp.where(final, bound, 0.0)
        p2 = x * dxd
        p1h = p1.astype(BF16)
        p2h = p2.astype(BF16)
        acc[rows, :] += (
            dot(p1h, seg1) + dot((p1 - p1h.astype(F32)).astype(BF16), seg1)
        ) + (dot(p2h, seg2) + dot((p2 - p2h.astype(F32)).astype(BF16), seg2))
        skip_sum = skip_sum + jnp.sum(x * dy, axis=0, keepdims=True)
        dx = dt * dxd + skip * dy
        dext[rows, :] = dx * (sig * (1.0 + conv * (1.0 - sig)))
        grad = grad * jnp.exp(tot) + dot(ct_ref[:, rows], ey)
    conv_back(ext, dext, taps_ref, dv_ref, tail_ref, head_ref, stats_ref, blocks)
    stats_ref[5:6, :] = skip_sum

    @pl.when(i == pl.num_programs(0) - 1)
    def _():
        fill(ext, bchalo_ref, bc_ref)
        triu = (row_iota(T) <= lane_iota(T)).astype(F32)
        rate = prm_ref[1:2, :]
        rate_sum = jnp.zeros((1, 128), F32)
        bias_sum = jnp.zeros((1, 128), F32)
        for c in range(blocks):
            rows = pl.ds(c * T, T)
            causal = row_iota(T) <= lane_iota(T)
            m = jnp.where(causal, dcbt[c], 0.0).astype(BF16)
            db = dbacc[rows, :] + dot(m, c_ref[rows, :])
            dc = dcacc[rows, :] + dot_tn(m, b_ref[rows, :])
            conv = conv_block(ext, bctaps_ref, bcshift_ref, c)
            sig = sigmoid(conv)
            dext[rows, :] = jnp.concatenate([db, dc], axis=1) * (
                sig * (1.0 + conv * (1.0 - sig))
            )
            a = acc[rows, :]
            ddecay = lax.dot_general(
                triu, a, (((1,), (0,)), ((), ())),
                precision=lax.Precision.HIGHEST, preferred_element_type=F32,
            )
            packed = p_ref[rows, :]
            rate_sum = rate_sum + jnp.sum(packed * ddecay, axis=0, keepdims=True)
            dz = (pltpu.roll(a, 96, 1) + rate * ddecay) * pltpu.roll(packed, 32, 1)
            ddt_ref[rows, :] = dz.astype(BF16)
            bias_sum = bias_sum + jnp.sum(dz, axis=0, keepdims=True)
        conv_back(ext, dext, bctaps_ref, bdv_ref, btail_ref, bhead_ref, bstats_ref, blocks)
        dtstats_ref[0:1, :] = rate_sum * rate
        dtstats_ref[1:2, :] = bias_sum


def whole(shape):
    return pl.BlockSpec(shape, lambda i: (0,) * len(shape))


def wide(rows):
    return pl.BlockSpec((rows, WB), lambda i: (0, i))


def bc_block(rows):
    return pl.BlockSpec((rows, WB), lambda i: (0, STEPS))


def shape_of(shape, dtype):
    return jax.ShapeDtypeStruct(shape, dtype)


def params():
    return pltpu.CompilerParams(vmem_limit_bytes=VMEM_LIMIT)


def cost(flops, moved):
    return pl.CostEstimate(flops=int(flops), bytes_accessed=int(moved), transcendentals=0)


def local_state(r_low, halo, dt_low, taps, shift, prm):
    length = r_low.shape[0]
    return pl.pallas_call(
        state_kernel,
        name="local_state",
        grid=(STEPS,),
        in_specs=[
            wide(length), wide(HALO), bc_block(length), bc_block(HALO), whole((length, 128)),
            wide(4), wide(1), bc_block(4), bc_block(1), whole((8, 128)),
        ],
        out_specs=[
            wide(N), wide(8), whole((length, 128)), whole((128, length)),
            whole((length, N)), whole((length, N)), whole((N, length)), whole((N, length)),
        ],
        out_shape=[
            shape_of((N, DI), BF16), shape_of((8, DI), F32), shape_of((length, 128), F32),
            shape_of((128, length), F32), shape_of((length, N), BF16),
            shape_of((length, N), BF16), shape_of((N, length), BF16), shape_of((N, length), BF16),
        ],
        scratch_shapes=[pltpu.VMEM((HALO + length, WB), F32)],
        compiler_params=params(),
        cost_estimate=cost(4e9, 8e6),
    )(r_low, halo, r_low, halo, dt_low, taps, shift, taps, shift, prm)


def local_scan(r_low, halo, taps, shift, skip, p, pt, b, c, bt):
    length = r_low.shape[0]
    return pl.pallas_call(
        scan_kernel,
        name="local_scan",
        grid=(STEPS,),
        in_specs=[
            wide(length), wide(HALO), wide(4), wide(1), wide(1), whole((length, 128)),
            whole((128, length)), whole((length, N)), whole((length, N)), whole((N, length)),
        ],
        out_specs=wide(length),
        out_shape=shape_of((length, DI), F32),
        scratch_shapes=[
            pltpu.VMEM((HALO + length, WB), F32), pltpu.VMEM((length // T, T, T), F32)
        ],
        compiler_params=params(),
        cost_estimate=cost(1.5e10, 8e6),
    )(r_low, halo, taps, shift, skip, p, pt, b, c, bt)


def gate_forward(y, gate, p, c, s_in, gain):
    length = y.shape[0]
    rows = lambda width: pl.BlockSpec((T, width), lambda i: (i, 0))
    return pl.pallas_call(
        gate_kernel,
        name="gate_forward",
        grid=(length // T,),
        in_specs=[rows(DI), rows(DI), rows(128), rows(N), whole((N, DI)), whole((1, DI))],
        out_specs=[rows(DI), rows(DI)],
        out_shape=[shape_of((length, DI), F32), shape_of((length, DI), BF16)],
        compiler_params=params(),
        cost_estimate=cost(5e9, 15e6),
    )(y, gate, p, c, s_in, gain)


def gate_backward(y, gate, dgn, p, ct, gain):
    length = y.shape[0]
    rows = lambda width: pl.BlockSpec((T, width), lambda i: (i, 0))
    return pl.pallas_call(
        gate_back_kernel,
        name="gate_backward",
        grid=(length // T,),
        in_specs=[
            rows(DI), rows(DI), rows(DI), rows(128),
            pl.BlockSpec((N, T), lambda i: (0, i)), whole((1, DI)),
        ],
        out_specs=[rows(DI), rows(DI), whole((8, DI)), whole((N, DI))],
        out_shape=[
            shape_of((length, DI), BF16), shape_of((length, DI), BF16),
            shape_of((8, DI), F32), shape_of((N, DI), BF16),
        ],
        scratch_shapes=[pltpu.VMEM((N, DI), F32)],
        compiler_params=params(),
        cost_estimate=cost(1e10, 17e6),
    )(y, gate, dgn, p, ct, gain)


def scan_backward(
    r_low, halo, taps, shift, skip, prm, p, pt, b, c, bt, ct, s_in, g_in, dy, y
):
    length = r_low.shape[0]
    blocks = length // T
    return pl.pallas_call(
        back_kernel,
        name="scan_backward",
        grid=(STEPS,),
        in_specs=[
            wide(length), wide(HALO), bc_block(length), bc_block(HALO),
            wide(4), wide(1), bc_block(4), bc_block(1), wide(1), whole((8, 128)),
            whole((length, 128)), whole((128, length)), whole((length, N)), whole((length, N)),
            whole((N, length)), whole((N, length)), wide(N), wide(N), wide(length), wide(length),
        ],
        out_specs=[
            wide(length), wide(8), wide(8), wide(8),
            whole((length, WB)), whole((8, WB)), whole((8, WB)), whole((8, WB)),
            whole((length, 128)), whole((8, 128)),
        ],
        out_shape=[
            shape_of((length, DI), BF16), shape_of((8, DI), F32), shape_of((8, DI), F32),
            shape_of((8, DI), F32),
            shape_of((length, WB), BF16), shape_of((8, WB), F32), shape_of((8, WB), F32),
            shape_of((8, WB), F32),
            shape_of((length, 128), BF16), shape_of((8, 128), F32),
        ],
        scratch_shapes=[
            pltpu.VMEM((HALO + length, WB), F32),
            pltpu.VMEM((length + 8, WB), F32),
            pltpu.VMEM((length, WB), F32),
            pltpu.VMEM((length, WB), F32),
            pltpu.VMEM((blocks, T, T), F32),
            pltpu.VMEM((blocks, T, T), F32),
            pltpu.VMEM((length, 128), F32),
            pltpu.VMEM((length, 128), F32),
            pltpu.VMEM((length, 128), F32),
        ],
        compiler_params=params(),
        cost_estimate=cost(3e10, 16e6),
    )(
        r_low, halo, r_low, halo, taps, shift, taps, shift, skip, prm, p, pt, b, c, bt, ct,
        s_in, g_in, dy, y,
    )


def pass_along(local, decay, order):
    hops = lax.axis_size("seq") - 1
    state = jnp.zeros_like(local)
    message = local
    for hop in range(hops):
        state = lax.ppermute(message, "seq", order)
        if hop < hops - 1:
            message = (local.astype(F32) + decay * state.astype(F32)).astype(BF16)
    return state


def on_device(
    hidden_in, cotangent, norm_gain, input_projection_weight, conv_weight, conv_bias, dt_bias,
    a_log, skip, gate_gain, output_projection_weight,
):
    layers = input_projection_weight.shape[0]
    seq_parts = lax.axis_size("seq")
    up = [(z, z + 1) for z in range(seq_parts - 1)]
    down = [(z + 1, z) for z in range(seq_parts - 1)]

    small = [norm_gain, conv_weight, conv_bias, dt_bias, a_log, skip, gate_gain]
    flat = jnp.concatenate([a.reshape(layers, -1) for a in small], axis=1)
    packed = lax.all_gather(flat, "fsdp", axis=0).astype(F32)
    shards = packed.shape[0]
    unpacked = []
    start = 0
    for a in small:
        width = a[0].size
        piece = packed[:, :, start : start + width].reshape((shards,) + a.shape)
        start += width
        piece = jnp.moveaxis(piece, 0, -2)
        unpacked.append(piece.reshape(a.shape[:-1] + (shards * a.shape[-1],)))
    gains, taps_all, shift_all, bias_all, rate_all, skip_all, gate_all = unpacked

    weights = []
    for layer in range(layers):
        w = input_projection_weight[layer]
        weights.append(
            (
                lax.all_gather(w[:, DI:], "fsdp", axis=0, tiled=True),
                lax.all_gather(w[:, :DI], "fsdp", axis=0, tiled=True),
                lax.all_gather(output_projection_weight[layer], "fsdp", axis=0, tiled=True),
            )
        )

    hidden = hidden_in[0].astype(F32)
    stored = []
    for layer in range(layers):
        w_rest, w_gate, w_out = weights[layer]
        r_in = lax.rsqrt(jnp.mean(hidden * hidden, axis=1, keepdims=True) + EPS)
        normed = (hidden * r_in * gains[layer][None, :]).astype(BF16)
        r_low = dot(normed, w_rest).astype(BF16)
        halo = lax.ppermute(r_low[-HALO:, :CC], "seq", up)
        gate = dot(normed, w_gate)
        taps = taps_all[layer]
        shift = shift_all[layer][None, :]
        skip_wide = jnp.repeat(skip_all[layer], P_SIZE)[None, :]
        prm = jnp.zeros((8, 128), F32)
        prm = prm.at[0].set(jnp.tile(bias_all[layer], 4))
        prm = prm.at[1].set(jnp.tile(-jnp.exp(rate_all[layer]), 4))
        dt_low = jnp.tile(r_low[:, CC:], (1, 4))
        f, decay, p, pt, b, c, bt, ct = local_state(r_low, halo, dt_low, taps, shift, prm)
        s_in = pass_along(f, decay[0:1], up)
        y = local_scan(r_low, halo, taps, shift, skip_wide, p, pt, b, c, bt)
        y, gate_low = gate_forward(y, gate, p, c, s_in, gate_all[layer][None, :])
        stored.append(
            (
                hidden, r_in, normed, r_low, halo, gate, taps, shift, skip_wide, prm, decay, p,
                pt, b, c, bt, ct, s_in, y, gate_low,
            )
        )
        hidden = hidden + dot(gate_low, w_out)
    block_out = hidden.astype(BF16)[None]

    grad = cotangent[0].astype(F32)
    big = [None] * layers
    vectors = [None] * layers
    for layer in reversed(range(layers)):
        (
            hidden, r_in, normed, r_low, halo, gate, taps, shift, skip_wide, prm, decay, p,
            pt, b, c, bt, ct, s_in, y, gate_low,
        ) = stored[layer]
        w_rest, w_gate, w_out = weights[layer]
        d_branch = grad.astype(BF16)
        dgn = dot_nt(d_branch, w_out)
        dgate, dmix, gain_out_grad, g_local = gate_backward(
            y, gate, dgn, p, ct, gate_all[layer][None, :]
        )
        g_in = pass_along(g_local, decay[0:1], down)
        out_grad = dot_tn(gate_low, d_branch).astype(BF16)
        gate_w_grad = dot_tn(normed, dgate).astype(BF16)
        dv, tail, head, stats, bdv, btail, bhead, bstats, ddt, dtstats = scan_backward(
            r_low, halo, taps, shift, skip_wide, prm, p, pt, b, c, bt, ct, s_in, g_in, dmix, y
        )
        heads_in = lax.ppermute(jnp.concatenate([head, bhead], axis=1), "seq", down)
        tail = jnp.concatenate([tail, btail], axis=1)
        fix = [tail[j : j + 1] for j in range(8)]
        for j in range(3):
            for k in range(j + 1):
                fix[5 + j] = fix[5 + j] + taps[k : k + 1] * heads_in[j - k : j - k + 1]
        d_rest = jnp.concatenate([dv, bdv, ddt[:, :H]], axis=1)
        d_rest = lax.dynamic_update_slice(
            d_rest, jnp.concatenate(fix, axis=0).astype(BF16), (d_rest.shape[0] - 8, 0)
        )
        rest_w_grad = dot_tn(normed, d_rest).astype(BF16)
        d_normed = dot_nt(dgate, w_gate) + dot_nt(d_rest, w_rest)
        q = hidden * r_in
        dq = d_normed * gains[layer][None, :]
        gain_in_grad = jnp.sum(d_normed * q, axis=0)
        grad = grad + r_in * (dq - q * jnp.mean(dq * q, axis=1, keepdims=True))
        big[layer] = [
            lax.psum(lax.psum_scatter(a, "fsdp", scatter_dimension=0, tiled=True), "seq")
            for a in (out_grad, gate_w_grad, rest_w_grad)
        ]
        stats = jnp.concatenate([stats, bstats], axis=1)
        vectors[layer] = [
            gain_in_grad,
            stats[0:4],
            stats[4],
            dtstats[1, :H],
            dtstats[0, :H],
            stats[5, :DI].reshape(H, P_SIZE).sum(axis=1),
            gain_out_grad[0],
        ]

    rows = []
    for a, member in zip(small, range(len(small))):
        full = jnp.stack([vectors[layer][member] for layer in range(layers)])
        full = full.reshape(a.shape[:-1] + (shards, a.shape[-1]))
        rows.append(jnp.moveaxis(full, -2, 0).reshape(shards, -1))
    summed = lax.psum(jnp.concatenate(rows, axis=1), ("fsdp", "seq"))
    mine = lax.dynamic_index_in_dim(summed, lax.axis_index("fsdp"), 0, keepdims=False)
    outs = []
    start = 0
    for a in small:
        outs.append(mine[start : start + a.size].reshape(a.shape))
        start += a.size
    in_w = jnp.stack(
        [jnp.concatenate([big[k][1], big[k][2]], axis=1) for k in range(layers)]
    ).astype(F32)
    out_w = jnp.stack([big[k][0] for k in range(layers)]).astype(F32)
    return (
        block_out, grad[None], outs[0], in_w, outs[1], outs[2], outs[3], outs[4], outs[5],
        outs[6], out_w,
    )


def solution(mesh):
    tokens = P("fsdp", "seq", None)
    vector = P(None, "fsdp")
    matrix = P(None, "fsdp", None)
    channels = P(None, None, "fsdp")
    return jax.shard_map(
        on_device,
        mesh=mesh,
        in_specs=(
            tokens, tokens, vector, matrix, channels, vector, vector, vector, vector, vector,
            matrix,
        ),
        out_specs=(
            tokens, tokens, vector, matrix, channels, vector, vector, vector, vector, vector,
            matrix,
        ),
        check_vma=False,
    )
```

```python
import functools

import jax
import jax.numpy as jnp
from jax import lax
from jax.experimental import pallas as pl
from jax.experimental.pallas import tpu as pltpu
from jax.sharding import PartitionSpec as P

H = 32
P_SIZE = 64
N = 128
D = 1024
DI = 2048
CC = DI + 2 * N
T = 128
WB = 256
HB = WB // P_SIZE
STEPS = DI // WB
HALO = 16
F32 = jnp.float32
BF16 = jnp.bfloat16
EPS = 1e-05
VMEM_LIMIT = 50 * 1024 * 1024

L_STEP, L_CUM, L_CUMF, L_SIG = 0, 32, 64, 96


def dot(a, b):
    return jnp.dot(a, b, preferred_element_type=F32)


def dot_nt(a, b):
    return lax.dot_general(a, b, (((1,), (1,)), ((), ())), preferred_element_type=F32)


def dot_tn(a, b):
    return lax.dot_general(a, b, (((0,), (0,)), ((), ())), preferred_element_type=F32)


def sigmoid(v):
    return 0.5 * jnp.tanh(0.5 * v) + 0.5


def lane_iota(rows, lanes=128):
    return lax.broadcasted_iota(jnp.int32, (rows, lanes), 1)


def row_iota(rows, lanes=128):
    return lax.broadcasted_iota(jnp.int32, (rows, lanes), 0)


def parts_of(packed):
    high = packed.astype(BF16)
    rest = packed - high.astype(F32)
    middle = rest.astype(BF16)
    return jnp.concatenate([high, middle, (rest - middle.astype(F32)).astype(BF16)], axis=1)


def pick(first, rows, lanes, shift):
    row = jnp.bitwise_and(row_iota(rows, lanes), 127)
    head = lax.shift_right_logical(lane_iota(rows, lanes), shift)
    return jnp.where(row == first + head, 1.0, 0.0).astype(BF16)


def head_lanes(first, i):
    return pick(first + HB * i, 384, WB, 6)


def head_tiles(first, i):
    return pick(first + HB * i, 384, HB * 128, 7)


def widen(tiles):
    left = lane_iota(tiles.shape[0]) < P_SIZE
    tile = lambda h: tiles[:, h * 128 : (h + 1) * 128]
    return jnp.concatenate(
        [jnp.where(left, tile(2 * p), tile(2 * p + 1)) for p in range(HB // 2)], axis=1
    )


def halves(tile, axis_rows=True):
    left = lane_iota(tile.shape[0]) < P_SIZE
    zero = jnp.zeros_like(tile)
    return jnp.concatenate([jnp.where(left, tile, zero), jnp.where(left, zero, tile)], axis=0)


def head_rows(heads, i):
    lane = jnp.bitwise_and(lane_iota(16, 384), 127)
    sel = jnp.where(lane == L_CUM + HB * i + row_iota(16, 384), 1.0, 0.0).astype(BF16)
    return dot_nt(sel, heads)


def fill(ext, halo_ref, v_ref):
    ext[0:HALO, :] = halo_ref[...].astype(F32)
    ext[HALO:, :] = v_ref[...].astype(F32)


def conv_block(ext, taps_ref, shift_ref, c):
    total = shift_ref[0:1, :] + taps_ref[0:1, :] * ext[pl.ds(HALO - 3 + c * T, T), :]
    for k in range(1, 4):
        total = total + taps_ref[k : k + 1, :] * ext[pl.ds(HALO - 3 + k + c * T, T), :]
    return total


def state_kernel(
    v_ref, halo_ref, bc_ref, bchalo_ref, dt_ref, taps_ref, shift_ref, bctaps_ref, bcshift_ref,
    prm_ref, f_ref, tot_ref, x_ref, p_ref, p3_ref, b_ref, c_ref, bt_ref, ct_ref, ext,
):
    i = pl.program_id(0)
    blocks = v_ref.shape[0] // T

    @pl.when(i == 0)
    def _():
        fill(ext, bchalo_ref, bc_ref)
        lane = lane_iota(T)
        tril = (row_iota(T) >= lane).astype(F32)
        offset = jnp.zeros((1, 128), F32)
        for c in range(blocks):
            rows = pl.ds(c * T, T)
            conv = conv_block(ext, bctaps_ref, bcshift_ref, c)
            act = conv * sigmoid(conv)
            b_ref[rows, :] = act[:, :N].astype(BF16)
            c_ref[rows, :] = act[:, N:].astype(BF16)
            bt_ref[:, rows] = act[:, :N].T.astype(BF16)
            ct_ref[:, rows] = act[:, N:].T.astype(BF16)
            z = dt_ref[rows, :].astype(F32) + prm_ref[0:1, :]
            step = jnp.maximum(z, 0.0) + jnp.log1p(jnp.exp(-jnp.abs(z)))
            decay = step * prm_ref[1:2, :]
            cum = lax.dot_general(
                tril, decay, (((1,), (0,)), ((), ())),
                precision=lax.Precision.HIGHEST, preferred_element_type=F32,
            )
            cumf = cum + offset
            offset = cumf[T - 1 : T, :]
            packed = jnp.where(
                lane < L_CUM, step,
                jnp.where(lane < L_CUMF, cum, jnp.where(lane < L_SIG, cumf, 1.0 / (1.0 + jnp.exp(-z)))),
            )
            p_ref[rows, :] = packed
            p3_ref[rows, :] = parts_of(packed)

    fill(ext, halo_ref, v_ref)
    steps = head_lanes(L_STEP, i)
    sums = head_lanes(L_CUMF, i)
    tot = dot(p3_ref[pl.ds(blocks * T - 16, 16), :], sums)[15:16, :]
    total = jnp.zeros((N, WB), F32)
    for c in range(blocks):
        rows = pl.ds(c * T, T)
        conv = conv_block(ext, taps_ref, shift_ref, c)
        x = conv * sigmoid(conv)
        x_ref[rows, :] = x
        heads = p3_ref[rows, :]
        wx = (x * (jnp.exp(tot - dot(heads, sums)) * dot(heads, steps))).astype(BF16)
        total = total + dot(bt_ref[:, rows], wx)
    f_ref[...] = total.astype(BF16)
    tot_ref[...] = jnp.broadcast_to(jnp.exp(tot), (8, WB))


def scan_kernel(
    x_ref, skip_ref, p3_ref, b_ref, c_ref, bt_ref, y_ref, cb,
):
    i = pl.program_id(0)
    blocks = x_ref.shape[0] // T

    @pl.when(i == 0)
    def _():
        causal = row_iota(T) >= lane_iota(T)
        for c in range(blocks):
            rows = pl.ds(c * T, T)
            cb[c] = jnp.where(causal, dot_nt(c_ref[rows, :], b_ref[rows, :]), 0.0)

    steps = head_lanes(L_STEP, i)
    sums = head_tiles(L_CUM, i)
    state = None
    for c in range(blocks):
        rows = pl.ds(c * T, T)
        x = x_ref[rows, :]
        heads = p3_ref[rows, :]
        cums = dot(heads, sums)
        turned = head_rows(heads, i)
        xd = x * dot(heads, steps)
        parts = []
        for p in range(HB // 2):
            weights = []
            for h in (2 * p, 2 * p + 1):
                across = turned[h : h + 1, :]
                e = jnp.exp(jnp.minimum(cums[:, h * 128 : (h + 1) * 128] - across, 0.0))
                weights.append((e * cb[c]).astype(BF16))
            parts.append(
                dot(
                    jnp.concatenate(weights, axis=1),
                    halves(xd[:, p * 128 : (p + 1) * 128]).astype(BF16),
                )
            )
        y = jnp.concatenate(parts, axis=1) + skip_ref[0:1, :] * x
        cumx = widen(cums)
        if state is not None:
            y = y + jnp.exp(cumx) * dot(c_ref[rows, :], state.astype(BF16))
        y_ref[rows, :] = y
        if c < blocks - 1:
            tot = cumx[T - 1 : T, :]
            fresh = dot(bt_ref[:, rows], (jnp.exp(tot - cumx) * xd).astype(BF16))
            state = fresh if state is None else state * jnp.exp(tot) + fresh


def grow_factors(p_ref, sel):
    lane = lane_iota(p_ref.shape[0])
    inside = jnp.logical_and(lane >= L_CUMF, lane < L_SIG)
    grow = jnp.where(inside, jnp.exp(jnp.where(inside, p_ref[...], 0.0)), 0.0)
    high = grow.astype(BF16)
    low = (grow - high.astype(F32)).astype(BF16)
    return dot(jnp.concatenate([high, low], axis=1), sel[...])


def gate_kernel(y_ref, gate_ref, p_ref, c_ref, s_ref, gain_ref, out_y_ref, out_ref, sel):
    @pl.when(pl.program_id(0) == 0)
    def _():
        sel[...] = pick(L_CUMF, 256, DI, 6)

    grow = grow_factors(p_ref, sel)
    y = y_ref[...] + grow * dot(c_ref[...], s_ref[...])
    out_y_ref[...] = y
    mixed = y.astype(BF16).astype(F32)
    gate = gate_ref[...]
    gated = mixed * (gate * sigmoid(gate))
    r = lax.rsqrt(jnp.mean(gated * gated, axis=1, keepdims=True) + EPS)
    out_ref[...] = (gated * r * gain_ref[0:1, :]).astype(BF16)


def gate_back_kernel(
    y_ref, gate_ref, dgn_ref, p_ref, ct_ref, gain_ref, dgate_ref, dmix_ref, gg_ref, g_ref, acc,
    sel,
):
    i = pl.program_id(0)

    @pl.when(i == 0)
    def _():
        sel[...] = pick(L_CUMF, 256, DI, 6)
        acc[...] = jnp.zeros_like(acc)
        gg_ref[...] = jnp.zeros_like(gg_ref)

    mixed = y_ref[...].astype(BF16).astype(F32)
    gate = gate_ref[...]
    sig = sigmoid(gate)
    silu = gate * sig
    gated = mixed * silu
    r = lax.rsqrt(jnp.mean(gated * gated, axis=1, keepdims=True) + EPS)
    q = gated * r
    dgn = dgn_ref[...]
    gg_ref[...] += jnp.broadcast_to(jnp.sum(dgn * q, axis=0, keepdims=True), gg_ref.shape)
    dq = dgn * gain_ref[0:1, :]
    dgated = r * (dq - q * jnp.mean(dq * q, axis=1, keepdims=True))
    dgate_ref[...] = (dgated * mixed * (sig * (1.0 + gate * (1.0 - sig)))).astype(BF16)
    dmix = (dgated * silu).astype(BF16)
    dmix_ref[...] = dmix
    grow = grow_factors(p_ref, sel)
    acc[...] += dot(ct_ref[...], (grow * dmix.astype(F32)).astype(BF16))

    @pl.when(i == pl.num_programs(0) - 1)
    def _():
        g_ref[...] = acc[...].astype(BF16)


def conv_back(ext, dext, taps_ref, dv_ref, tail_ref, head_ref, stats_ref, blocks):
    sums = [jnp.zeros((1, WB), F32) for _ in range(5)]
    for c in range(blocks):
        d = dext[pl.ds(c * T, T), :]
        total = taps_ref[3:4, :] * d
        for k in range(3):
            total = total + taps_ref[k : k + 1, :] * dext[pl.ds(c * T + 3 - k, T), :]
        dv_ref[pl.ds(c * T, T), :] = total.astype(BF16)
        if c == blocks - 1:
            tail_ref[...] = total[T - 8 :, :]
        for k in range(4):
            v = ext[pl.ds(HALO - 3 + k + c * T, T), :]
            sums[k] = sums[k] + jnp.sum(d * v, axis=0, keepdims=True)
        sums[4] = sums[4] + jnp.sum(d, axis=0, keepdims=True)
    head_ref[...] = dext[0:8, :]
    for k in range(5):
        stats_ref[k : k + 1, :] = sums[k]


def back_inside_kernel(
    x_ref, p3_ref, b_ref, c_ref, dy_ref, dxd_ref, dcbt_ref, cbt, first,
):
    i = pl.program_id(0) + first
    blocks = x_ref.shape[0] // T

    @pl.when(pl.program_id(0) == 0)
    def _():
        causal = row_iota(T) <= lane_iota(T)
        for c in range(blocks):
            rows = pl.ds(c * T, T)
            cbt[c] = jnp.where(causal, dot_nt(b_ref[rows, :], c_ref[rows, :]), 0.0)
        dcbt_ref[...] = jnp.zeros_like(dcbt_ref)

    steps = head_lanes(L_STEP, i)
    sums = head_tiles(L_CUM, i)
    for c in range(blocks):
        rows = pl.ds(c * T, T)
        heads = p3_ref[rows, :]
        cums = dot(heads, sums)
        turned = head_rows(heads, i)
        xd = x_ref[rows, :] * dot(heads, steps)
        dyb = dy_ref[rows, :]
        dy = dyb.astype(F32)
        dcb = jnp.zeros((T, T), F32)
        for p in range(HB // 2):
            lanes = slice(p * 128, (p + 1) * 128)
            dm = dot_nt(halves(xd[:, lanes]).astype(BF16), dyb[:, lanes])
            weights = []
            for j in range(2):
                h = 2 * p + j
                across = turned[h : h + 1, :]
                e = jnp.exp(jnp.minimum(across - cums[:, h * 128 : (h + 1) * 128], 0.0))
                weights.append((e * cbt[c]).astype(BF16))
                dcb = dcb + dm[j * T : (j + 1) * T, :] * e
            dxd_ref[rows, lanes] = dot(
                jnp.concatenate(weights, axis=1), halves(dy[:, lanes]).astype(BF16)
            )
        dcbt_ref[c] += dcb


def back_kernel(
    v_ref, halo_ref, bc_ref, bchalo_ref, taps_ref, shift_ref, bctaps_ref, bcshift_ref, skip_ref,
    prm_ref, p_ref, p3_ref, b_ref, c_ref, bt_ref, ct_ref, s_ref, gin_ref, dy_ref, y_ref,
    inside_ref,
    low_ref, high_ref,
    dv_ref, tail_ref, head_ref, stats_ref, bdv_ref, btail_ref, bhead_ref, bstats_ref,
    ddt_ref, dtstats_ref,
    ext, dext, convs, sigs, cumw, dtw, acc, dbacc, dcacc,
):
    i = pl.program_id(0)
    blocks = v_ref.shape[0] // T
    length = blocks * T

    @pl.when(i == 0)
    def _():
        acc[...] = jnp.zeros_like(acc)
        dbacc[...] = jnp.zeros_like(dbacc)
        dcacc[...] = jnp.zeros_like(dcacc)

    fill(ext, halo_ref, v_ref)
    dext[length:, :] = jnp.zeros((8, WB), F32)
    steps = head_lanes(L_STEP, i)
    sums = head_lanes(L_CUM, i)
    states = [s_ref[...].astype(F32)]
    for c in range(blocks):
        rows = pl.ds(c * T, T)
        conv = conv_block(ext, taps_ref, shift_ref, c)
        sig = sigmoid(conv)
        convs[rows, :] = conv
        sigs[rows, :] = sig
        heads = p3_ref[rows, :]
        cumx = dot(heads, sums)
        dt = dot(heads, steps)
        cumw[rows, :] = cumx
        dtw[rows, :] = dt
        tot = cumx[T - 1 : T, :]
        wx = (jnp.exp(tot - cumx) * (conv * sig * dt)).astype(BF16)
        states.append(states[-1] * jnp.exp(tot) + dot(bt_ref[:, rows], wx))

    ch = lax.shift_right_logical(row_iota(WB), 6)
    seg1 = (lane_iota(WB) == HB * i + ch).astype(BF16)
    seg2 = (lane_iota(WB) == 32 + HB * i + ch).astype(BF16)
    final = row_iota(T, WB) == T - 1
    grad = gin_ref[...].astype(F32)
    skip_sum = jnp.zeros((1, WB), F32)
    for c in reversed(range(blocks)):
        rows = pl.ds(c * T, T)
        conv, sig = convs[rows, :], sigs[rows, :]
        x = conv * sig
        cumx, dt = cumw[rows, :], dtw[rows, :]
        tot = cumx[T - 1 : T, :]
        xd = x * dt
        xdb = xd.astype(BF16)
        dyb = dy_ref[rows, :]
        dy = dyb.astype(F32)
        gb = grad.astype(BF16)
        w = jnp.exp(tot - cumx)
        dxd = inside_ref[rows, :] + w * dot(b_ref[rows, :], gb)
        ey = (jnp.exp(cumx) * dy).astype(BF16)
        wx = (w * xd).astype(BF16)
        dcacc[rows, :] += dot_nt(ey, states[c].astype(BF16))
        dbacc[rows, :] += dot_nt(wx, gb)
        bound = jnp.sum(grad * states[c + 1], axis=0, keepdims=True)
        skip = skip_ref[0:1, :]
        p1 = dy * (y_ref[rows, :] - skip * x) - xdb.astype(F32) * dxd
        p1 = p1 + jnp.where(final, bound, 0.0)
        p2 = x * dxd
        p1h = p1.astype(BF16)
        p2h = p2.astype(BF16)
        acc[rows, :] += (
            dot(p1h, seg1) + dot((p1 - p1h.astype(F32)).astype(BF16), seg1)
        ) + (dot(p2h, seg2) + dot((p2 - p2h.astype(F32)).astype(BF16), seg2))
        skip_sum = skip_sum + jnp.sum(x * dy, axis=0, keepdims=True)
        dx = dt * dxd + skip * dy
        dext[rows, :] = dx * (sig * (1.0 + conv * (1.0 - sig)))
        grad = grad * jnp.exp(tot) + dot(ct_ref[:, rows], ey)
    conv_back(ext, dext, taps_ref, dv_ref, tail_ref, head_ref, stats_ref, blocks)
    stats_ref[5:6, :] = skip_sum

    @pl.when(i == pl.num_programs(0) - 1)
    def _():
        fill(ext, bchalo_ref, bc_ref)
        triu = (row_iota(T) <= lane_iota(T)).astype(F32)
        rate = prm_ref[1:2, :]
        rate_sum = jnp.zeros((1, 128), F32)
        bias_sum = jnp.zeros((1, 128), F32)
        for c in range(blocks):
            rows = pl.ds(c * T, T)
            causal = row_iota(T) <= lane_iota(T)
            m = jnp.where(causal, low_ref[c] + high_ref[c], 0.0).astype(BF16)
            db = dbacc[rows, :] + dot(m, c_ref[rows, :])
            dc = dcacc[rows, :] + dot_tn(m, b_ref[rows, :])
            conv = conv_block(ext, bctaps_ref, bcshift_ref, c)
            sig = sigmoid(conv)
            dext[rows, :] = jnp.concatenate([db, dc], axis=1) * (
                sig * (1.0 + conv * (1.0 - sig))
            )
            a = acc[rows, :]
            ddecay = lax.dot_general(
                triu, a, (((1,), (0,)), ((), ())),
                precision=lax.Precision.HIGHEST, preferred_element_type=F32,
            )
            packed = p_ref[rows, :]
            rate_sum = rate_sum + jnp.sum(packed * ddecay, axis=0, keepdims=True)
            dz = (pltpu.roll(a, 96, 1) + rate * ddecay) * pltpu.roll(packed, 32, 1)
            ddt_ref[rows, :] = jnp.where(lane_iota(T) < H, dz, 0.0).astype(BF16)
            bias_sum = bias_sum + jnp.sum(dz, axis=0, keepdims=True)
        conv_back(ext, dext, bctaps_ref, bdv_ref, btail_ref, bhead_ref, bstats_ref, blocks)
        dtstats_ref[0:1, :] = rate_sum * rate
        dtstats_ref[1:2, :] = bias_sum


def whole(shape):
    return pl.BlockSpec(shape, lambda i: (0,) * len(shape))


def wide(rows):
    return pl.BlockSpec((rows, WB), lambda i: (0, i))


def bc_block(rows):
    return pl.BlockSpec((rows, WB), lambda i: (0, STEPS))


def shape_of(shape, dtype):
    return jax.ShapeDtypeStruct(shape, dtype)


def params():
    return pltpu.CompilerParams(vmem_limit_bytes=VMEM_LIMIT)


def cost(flops, moved):
    return pl.CostEstimate(flops=int(flops), bytes_accessed=int(moved), transcendentals=0)


def local_state(r_low, halo, taps, shift, prm):
    length = r_low.shape[0]
    return pl.pallas_call(
        state_kernel,
        name="local_state",
        grid=(STEPS,),
        in_specs=[
            wide(length), wide(HALO), bc_block(length), bc_block(HALO),
            pl.BlockSpec((length, 128), lambda i: (0, CC // 128)),
            wide(4), wide(1), bc_block(4), bc_block(1), whole((8, 128)),
        ],
        out_specs=[
            wide(N), wide(8), wide(length), whole((length, 128)), whole((length, 384)),
            whole((length, N)), whole((length, N)), whole((N, length)), whole((N, length)),
        ],
        out_shape=[
            shape_of((N, DI), BF16), shape_of((8, DI), F32), shape_of((length, DI), F32),
            shape_of((length, 128), F32), shape_of((length, 384), BF16),
            shape_of((length, N), BF16), shape_of((length, N), BF16),
            shape_of((N, length), BF16), shape_of((N, length), BF16),
        ],
        scratch_shapes=[pltpu.VMEM((HALO + length, WB), F32)],
        compiler_params=params(),
        cost_estimate=cost(4e9, 8e6),
    )(r_low, halo, r_low, halo, r_low, taps, shift, taps, shift, prm)


def local_scan(x, skip, p3, b, c, bt):
    length = x.shape[0]
    return pl.pallas_call(
        scan_kernel,
        name="local_scan",
        grid=(STEPS,),
        in_specs=[
            wide(length), wide(1), whole((length, 384)),
            whole((length, N)), whole((length, N)), whole((N, length)),
        ],
        out_specs=wide(length),
        out_shape=shape_of((length, DI), F32),
        scratch_shapes=[pltpu.VMEM((length // T, T, T), F32)],
        compiler_params=params(),
        cost_estimate=cost(1.5e10, 8e6),
    )(x, skip, p3, b, c, bt)


def gate_forward(y, gate, p, c, s_in, gain):
    length = y.shape[0]
    rows = lambda width: pl.BlockSpec((T, width), lambda i: (i, 0))
    return pl.pallas_call(
        gate_kernel,
        name="gate_forward",
        grid=(length // T,),
        in_specs=[rows(DI), rows(DI), rows(128), rows(N), whole((N, DI)), whole((1, DI))],
        out_specs=[rows(DI), rows(DI)],
        out_shape=[shape_of((length, DI), F32), shape_of((length, DI), BF16)],
        scratch_shapes=[pltpu.VMEM((256, DI), BF16)],
        compiler_params=params(),
        cost_estimate=cost(5e9, 15e6),
    )(y, gate, p, c, s_in, gain)


def gate_backward(y, gate, dgn, p, ct, gain):
    length = y.shape[0]
    rows = lambda width: pl.BlockSpec((T, width), lambda i: (i, 0))
    return pl.pallas_call(
        gate_back_kernel,
        name="gate_backward",
        grid=(length // T,),
        in_specs=[
            rows(DI), rows(DI), rows(DI), rows(128),
            pl.BlockSpec((N, T), lambda i: (0, i)), whole((1, DI)),
        ],
        out_specs=[rows(DI), rows(DI), whole((8, DI)), whole((N, DI))],
        out_shape=[
            shape_of((length, DI), BF16), shape_of((length, DI), BF16),
            shape_of((8, DI), F32), shape_of((N, DI), BF16),
        ],
        scratch_shapes=[pltpu.VMEM((N, DI), F32), pltpu.VMEM((256, DI), BF16)],
        compiler_params=params(),
        cost_estimate=cost(1e10, 17e6),
    )(y, gate, dgn, p, ct, gain)


def scan_inside(x, p3, b, c, dy, first):
    length = x.shape[0]
    blocks = length // T
    wide_from = lambda rows: pl.BlockSpec((rows, WB), lambda i: (0, i + first))
    return pl.pallas_call(
        functools.partial(back_inside_kernel, first=first),
        name="scan_inside",
        grid=(STEPS // 2,),
        in_specs=[
            wide_from(length), whole((length, 384)), whole((length, N)),
            whole((length, N)), wide_from(length),
        ],
        out_specs=[wide(length), whole((blocks, T, T))],
        out_shape=[shape_of((length, DI // 2), F32), shape_of((blocks, T, T), F32)],
        scratch_shapes=[pltpu.VMEM((blocks, T, T), F32)],
        compiler_params=params(),
        cost_estimate=cost(1e10, 6e6),
    )(x, p3, b, c, dy)


def scan_backward(
    r_low, halo, taps, shift, skip, prm, p, p3, b, c, bt, ct, s_in, g_in, dy, y, low, high
):
    length = r_low.shape[0]
    blocks = length // T
    inside = jnp.concatenate([low[0], high[0]], axis=1)
    return pl.pallas_call(
        back_kernel,
        name="scan_backward",
        grid=(STEPS,),
        in_specs=[
            wide(length), wide(HALO), bc_block(length), bc_block(HALO),
            wide(4), wide(1), bc_block(4), bc_block(1), wide(1), whole((8, 128)),
            whole((length, 128)), whole((length, 384)), whole((length, N)), whole((length, N)),
            whole((N, length)), whole((N, length)), wide(N), wide(N), wide(length), wide(length),
            wide(length), whole((blocks, T, T)), whole((blocks, T, T)),
        ],
        out_specs=[
            wide(length), wide(8), wide(8), wide(8),
            whole((length, WB)), whole((8, WB)), whole((8, WB)), whole((8, WB)),
            whole((length, 128)), whole((8, 128)),
        ],
        out_shape=[
            shape_of((length, DI), BF16), shape_of((8, DI), F32), shape_of((8, DI), F32),
            shape_of((8, DI), F32),
            shape_of((length, WB), BF16), shape_of((8, WB), F32), shape_of((8, WB), F32),
            shape_of((8, WB), F32),
            shape_of((length, 128), BF16), shape_of((8, 128), F32),
        ],
        scratch_shapes=[
            pltpu.VMEM((HALO + length, WB), F32),
            pltpu.VMEM((length + 8, WB), F32),
            pltpu.VMEM((length, WB), F32),
            pltpu.VMEM((length, WB), F32),
            pltpu.VMEM((length, WB), F32),
            pltpu.VMEM((length, WB), F32),
            pltpu.VMEM((length, 128), F32),
            pltpu.VMEM((length, 128), F32),
            pltpu.VMEM((length, 128), F32),
        ],
        compiler_params=params(),
        cost_estimate=cost(3e10, 16e6),
    )(
        r_low, halo, r_low, halo, taps, shift, taps, shift, skip, prm, p, p3, b, c, bt, ct,
        s_in, g_in, dy, y, inside, low[1], high[1],
    )


def add(a, b):
    return (a.astype(F32) + b.astype(F32)).astype(BF16)


def swap(a, axis, bit):
    return lax.ppermute(a, axis, [(k, k ^ bit) for k in range(lax.axis_size(axis))])


def hop_to(message, state, hop, upward):
    last = lax.axis_size("seq") - 1
    pair = (hop, hop + 1) if upward else (last - hop, last - hop - 1)
    got = lax.ppermute(message, "seq", [pair])
    return got if state is None else got + state


def message_of(local, decay, state):
    return (local.astype(F32) + decay * state.astype(F32)).astype(BF16)


def pass_along(local, decay, upward, work):
    hops = lax.axis_size("seq") - 1
    state = None
    done = []
    for hop in range(hops):
        message = local if hop == 0 else message_of(local, decay, state)
        state = hop_to(message, state, hop, upward)
        if work:
            item = work[0]()
            work = work[1:]
            state, item = lax.optimization_barrier((state, item))
            done.append(item)
    for item in work:
        done.append(item())
    return state, done


def gather_pieces(w):
    n = lax.axis_size("fsdp")
    pieces = [w, swap(w, "fsdp", 1)]
    for piece in [swap(w, "fsdp", 2 * d) for d in range(1, n // 2)]:
        pieces += [piece, swap(piece, "fsdp", 1)]
    return pieces


def pieces_kernel(order_ref, left_ref, base_ref, *refs):
    del order_ref
    for m, piece in enumerate(refs[:-1]):

        @pl.when(pl.program_id(0) == m)
        def _(m=m, piece=piece):
            total = base_ref[...] if m == 0 else refs[-1][...]
            refs[-1][...] = total + dot(left_ref[...], piece[...])


def pieces_back_kernel(order_ref, left_ref, *refs):
    del order_ref
    for m, piece in enumerate(refs[:-1]):

        @pl.when(pl.program_id(0) == m)
        def _(piece=piece):
            refs[-1][...] = dot_nt(left_ref[...], piece[...])


def xor_order():
    n = lax.axis_size("fsdp")
    return jnp.bitwise_xor(lax.axis_index("fsdp"), jnp.arange(n)).astype(jnp.int32)


def fixed(shape):
    return pl.BlockSpec(shape, lambda i, order: (0,) * len(shape))


def add_product(base, left, w):
    if not isinstance(w, list):
        return base + dot(left, w)
    return pl.pallas_call(
        pieces_kernel,
        name="add_product",
        grid_spec=pltpu.PrefetchScalarGridSpec(
            num_scalar_prefetch=1,
            grid=(len(w),),
            in_specs=[
                pl.BlockSpec((left.shape[0], w[0].shape[0]), lambda i, order: (0, order[i])),
                fixed(base.shape),
            ]
            + [fixed(w[0].shape)] * len(w),
            out_specs=fixed(base.shape),
        ),
        out_shape=shape_of(base.shape, F32),
        compiler_params=params(),
        cost_estimate=cost(2e9, 10e6),
    )(xor_order(), left, base, *w)


def product_back(left, w):
    if not isinstance(w, list):
        return dot_nt(left, w)
    length = left.shape[0]
    return pl.pallas_call(
        pieces_back_kernel,
        name="product_back",
        grid_spec=pltpu.PrefetchScalarGridSpec(
            num_scalar_prefetch=1,
            grid=(len(w),),
            in_specs=[fixed(left.shape)] + [fixed(w[0].shape)] * len(w),
            out_specs=pl.BlockSpec((length, w[0].shape[0]), lambda i, order: (0, order[i])),
        ),
        out_shape=shape_of((length, len(w) * w[0].shape[0]), F32),
        compiler_params=params(),
        cost_estimate=cost(2e9, 10e6),
    )(xor_order(), left, *w)


def give_kernel(left_ref, right_ref, out_ref):
    out_ref[...] = dot_tn(left_ref[...], right_ref[...]).astype(BF16)


def own_kernel(left_ref, right_ref, got_ref, *out_refs):
    value = dot_tn(left_ref[...], right_ref[...]) + got_ref[...].astype(F32)
    rows = out_refs[0].shape[0]
    for d, out_ref in enumerate(out_refs):
        out_ref[...] = value[d * rows : (d + 1) * rows].astype(BF16)


def shard_columns(left, core):
    n = lax.axis_size("fsdp")
    me = lax.axis_index("fsdp")
    width = left.shape[1] // n
    return jnp.concatenate(
        [
            lax.dynamic_slice_in_dim(left, jnp.bitwise_xor(me, 2 * d + core) * width, width, 1)
            for d in range(n // 2)
        ],
        axis=1,
    )


def product_give(left, right):
    length, rows = left.shape
    columns = right.shape[1]
    block = columns // 2 if columns % 256 == 0 else columns
    return pl.pallas_call(
        give_kernel,
        name="product_give",
        grid=(columns // block,),
        in_specs=[whole((length, rows)), pl.BlockSpec((length, block), lambda i: (0, i))],
        out_specs=pl.BlockSpec((rows, block), lambda i: (0, i)),
        out_shape=shape_of((rows, columns), BF16),
        compiler_params=params(),
        cost_estimate=cost(3e9, 8e6),
    )(left, right)


def product_own(left, right, got):
    chips = lax.axis_size("fsdp") // 2
    length, rows = left.shape
    columns = right.shape[1]
    block = columns // 2 if columns % 256 == 0 else columns
    blocks = lambda height: pl.BlockSpec((height, block), lambda i: (0, i))
    return pl.pallas_call(
        own_kernel,
        name="product_own",
        grid=(columns // block,),
        in_specs=[whole((length, rows)), blocks(length), blocks(rows)],
        out_specs=[blocks(rows // chips)] * chips,
        out_shape=[shape_of((rows // chips, columns), BF16)] * chips,
        compiler_params=params(),
        cost_estimate=cost(3e9, 10e6),
    )(left, right, got)


def send_chips(parts):
    return parts[0], [swap(part, "fsdp", 2 * d) for d, part in enumerate(parts) if d]


def gather_sum(own, got):
    total = own.astype(F32)
    for piece in got:
        total = total + piece.astype(F32)
    return total.astype(BF16)


def tie(*values):
    return lax.optimization_barrier(values)


def seq_first(a):
    odd = lax.axis_index("seq") % 2
    half = a.shape[0] // 2
    keep = lax.dynamic_slice_in_dim(a, odd * half, half, 0)
    give = lax.dynamic_slice_in_dim(a, (1 - odd) * half, half, 0)
    return keep, swap(give, "seq", 1)


def seq_across(keep, got):
    keep = add(keep, got)
    bit = 2
    while 2 * bit < lax.axis_size("seq"):
        keep = add(keep, swap(keep, "seq", bit))
        bit *= 2
    return keep, swap(keep, "seq", bit)


def seq_back(keep, got):
    keep = add(keep, got)
    return keep, swap(keep, "seq", 1)


def seq_join(keep, other):
    odd = lax.axis_index("seq") % 2
    return jnp.where(
        odd == 0, jnp.concatenate([keep, other]), jnp.concatenate([other, keep])
    )


def sum_over(a, *axes):
    for axis in axes:
        bit = 1
        while bit < lax.axis_size(axis):
            a = a + swap(a, axis, bit)
            bit *= 2
    return a


def on_device(
    hidden_in, cotangent, norm_gain, input_projection_weight, conv_weight, conv_bias, dt_bias,
    a_log, skip, gate_gain, output_projection_weight,
):
    layers, _, in_width = input_projection_weight.shape
    seq_parts = lax.axis_size("seq")
    up = [(z, z + 1) for z in range(seq_parts - 1)]
    down = [(z + 1, z) for z in range(seq_parts - 1)]

    small = [norm_gain, conv_weight, conv_bias, dt_bias, a_log, skip, gate_gain]
    flat = jnp.concatenate([a.reshape(layers, -1) for a in small], axis=1)
    shards = lax.axis_size("fsdp")
    packed = lax.all_gather(flat, "fsdp", axis=0)
    packed = packed.astype(F32)
    unpacked = []
    start = 0
    for a in small:
        width = a[0].size
        piece = packed[:, :, start : start + width].reshape((shards,) + a.shape)
        start += width
        piece = jnp.moveaxis(piece, 0, -2)
        unpacked.append(piece.reshape(a.shape[:-1] + (shards * a.shape[-1],)))
    gains, taps_all, shift_all, bias_all, rate_all, skip_all, gate_all = unpacked

    weights = []
    for layer in range(layers):
        w = input_projection_weight[layer]
        rest = jnp.concatenate([w[:, DI : DI + CC]] + [w[:, DI + CC :]] * 4, axis=1)
        rest = lax.all_gather(rest, "fsdp", axis=0, tiled=True)
        if layer == 0:
            rest, first_out = tie(rest, output_projection_weight[0])
        weights.append(
            (
                rest,
                lax.all_gather(w[:, :DI], "fsdp", axis=0, tiled=True),
                gather_pieces(first_out)
                if layer == 0 and first_out.shape[0] % 128 == 0
                else lax.all_gather(output_projection_weight[layer], "fsdp", axis=0, tiled=True),
            )
        )

    hidden = hidden_in[0].astype(F32)
    stored = []
    for layer in range(layers):
        w_rest, w_gate, w_out = weights[layer]
        r_in = lax.rsqrt(jnp.mean(hidden * hidden, axis=1, keepdims=True) + EPS)
        normed = (hidden * r_in * gains[layer][None, :]).astype(BF16)
        r_low = dot(normed, w_rest).astype(BF16)
        halo = lax.ppermute(r_low[-HALO:, :CC], "seq", up)
        taps = taps_all[layer]
        shift = shift_all[layer][None, :]
        skip_wide = jnp.repeat(skip_all[layer], P_SIZE)[None, :]
        prm = jnp.zeros((8, 128), F32)
        prm = prm.at[0].set(jnp.tile(bias_all[layer], 4))
        prm = prm.at[1].set(jnp.tile(-jnp.exp(rate_all[layer]), 4))
        f, decay, x, p, p3, b, c, bt, ct = local_state(r_low, halo, taps, shift, prm)
        s_in, (y, gate) = pass_along(
            f,
            decay[0:1],
            True,
            [
                lambda: local_scan(x, skip_wide, p3, b, c, bt),
                lambda: dot(normed, w_gate),
            ],
        )
        y, gate_low = gate_forward(y, gate, p, c, s_in, gate_all[layer][None, :])
        stored.append(
            (
                hidden, r_in, normed, r_low, halo, gate, taps, shift, skip_wide, prm, decay, x, p,
                p3, b, c, bt, ct, s_in, y, gate_low,
            )
        )
        hidden = add_product(hidden, gate_low, w_out)
    block_out = hidden.astype(BF16)[None]

    block_out, cotangent = tie(block_out, cotangent)
    grad = cotangent[0].astype(F32)
    big = [None] * layers
    vectors = [None] * layers
    waiting = None
    for layer in reversed(range(layers)):
        (
            hidden, r_in, normed, r_low, halo, gate, taps, shift, skip_wide, prm, decay, x, p,
            p3, b, c, bt, ct, s_in, y, gate_low,
        ) = stored[layer]
        w_rest, w_gate, w_out = weights[layer]
        d_branch = grad.astype(BF16)
        dgn = product_back(d_branch, w_out)
        dgate, dmix, gain_out_grad, g_local = gate_backward(
            y, gate, dgn, p, ct, gate_all[layer][None, :]
        )

        if waiting is not None:
            scattered, g_local = tie(scattered, g_local)
            big[layer + 1] = [lax.psum(a, "seq") for a in scattered]

        normed_give, normed_own = shard_columns(normed, 1), shard_columns(normed, 0)
        inside = lambda first: scan_inside(x, p3, b, c, dmix, first)
        if layer == 0:
            out_give = product_give(shard_columns(gate_low, 1), d_branch)
            state = hop_to(g_local, None, 0, False)
            low = inside(0)
            state, out_give, low, rest_sent = tie(state, out_give, low, rest_sent)
            above = seq_first(gather_sum(rest_mine, rest_sent))
            for hop in range(1, seq_parts - 1):
                state = hop_to(message_of(g_local, decay[0:1], state), state, hop, False)
                if hop == 1:
                    out_got = swap(out_give, "fsdp", 1)
                    gate_give = product_give(normed_give, dgate)
                    high = inside(STEPS // 2)
                    state, out_got, gate_give, high, above = tie(
                        state, out_got, gate_give, high, above
                    )
                    above = seq_across(*above)
                    gate_got = swap(gate_give, "fsdp", 1)
                    out_parts = product_own(shard_columns(gate_low, 0), d_branch, out_got)
                elif hop == 2:
                    out_parts, state = tie(out_parts, state)
                    out_mine, out_sent = send_chips(out_parts)
                    state, gate_got, above = tie(state, gate_got, above)
                    above = seq_back(*above)
                    gate_parts = product_own(normed_own, dgate, gate_got)
                    state, gate_parts = tie(state, gate_parts)
                    gate_mine, gate_sent = send_chips(gate_parts)
        else:
            state, ((out_grad, gate_w_grad), low, high) = pass_along(
                g_local,
                decay[0:1],
                False,
                [
                    lambda: (
                        dot_tn(gate_low, d_branch).astype(BF16),
                        dot_tn(normed, dgate).astype(BF16),
                    ),
                    lambda: inside(0),
                    lambda: inside(STEPS // 2),
                ],
            )
            scattered = [
                lax.psum_scatter(a, "fsdp", scatter_dimension=0, tiled=True)
                for a in (out_grad, gate_w_grad)
            ]
        back = scan_backward(
            r_low, halo, taps, shift, skip_wide, prm, p, p3, b, c, bt, ct, s_in, state, dmix, y,
            low, high,
        )
        if layer == 0:
            back, out_sent, above = tie(back, out_sent, above)
            big[layer + 1].append(seq_join(*above))
            out_seq = seq_first(gather_sum(out_mine, out_sent))
        dv, tail, head, stats, bdv, btail, bhead, bstats, ddt, dtstats = back
        heads_in = lax.ppermute(jnp.concatenate([head, bhead], axis=1), "seq", down)
        tail = jnp.concatenate([tail, btail], axis=1)
        fix = [tail[j : j + 1] for j in range(8)]
        for j in range(3):
            for k in range(j + 1):
                fix[5 + j] = fix[5 + j] + taps[k : k + 1] * heads_in[j - k : j - k + 1]
        d_rest = jnp.concatenate([dv, bdv, ddt], axis=1)
        d_rest = lax.dynamic_update_slice(
            d_rest, jnp.concatenate(fix, axis=0).astype(BF16), (d_rest.shape[0] - 8, 0)
        )
        got = swap(product_give(normed_give, d_rest), "fsdp", 1)
        d_normed = dot_nt(dgate, w_gate)
        got, d_normed = tie(got, d_normed)
        if layer == 0:
            got, out_seq, gate_sent = tie(got, out_seq, gate_sent)
            out_seq = seq_across(*out_seq)
            gate_seq = seq_first(gather_sum(gate_mine, gate_sent))
        parts = product_own(normed_own, d_rest, got)
        parts, d_rest = tie(parts, d_rest)
        rest_mine, rest_sent = send_chips(parts)
        d_normed = d_normed + dot_nt(d_rest, w_rest)
        q = hidden * r_in
        dq = d_normed * gains[layer][None, :]
        gain_in_grad = jnp.sum(d_normed * q, axis=0)
        grad = grad + r_in * (dq - q * jnp.mean(dq * q, axis=1, keepdims=True))
        if layer == 0:
            grad, gain_in_grad, out_seq, gate_seq, rest_sent = tie(
                grad, gain_in_grad, out_seq, gate_seq, rest_sent
            )
            out_seq = seq_back(*out_seq)
            gate_seq = seq_across(*gate_seq)
            rest_seq = seq_first(gather_sum(rest_mine, rest_sent))
            out_seq, gate_seq, rest_seq = tie(out_seq, gate_seq, rest_seq)
            gate_seq = seq_back(*gate_seq)
            rest_seq = seq_back(*seq_across(*rest_seq))
            big[layer] = [seq_join(*out_seq), seq_join(*gate_seq), seq_join(*rest_seq)]
        waiting = layer
        stats = jnp.concatenate([stats, bstats], axis=1)
        vectors[layer] = [
            gain_in_grad,
            stats[0:4],
            stats[4],
            dtstats[1, :H],
            dtstats[0, :H],
            stats[5, :DI].reshape(H, P_SIZE).sum(axis=1),
            gain_out_grad[0],
        ]

    rows = []
    for a, member in zip(small, range(len(small))):
        full = jnp.stack([vectors[layer][member] for layer in range(layers)])
        full = full.reshape(a.shape[:-1] + (shards, a.shape[-1]))
        rows.append(jnp.moveaxis(full, -2, 0).reshape(shards, -1))
    summed = sum_over(jnp.concatenate(rows, axis=1), "fsdp", "seq")
    mine = lax.dynamic_index_in_dim(summed, lax.axis_index("fsdp"), 0, keepdims=False)
    outs = []
    start = 0
    for a in small:
        outs.append(mine[start : start + a.size].reshape(a.shape))
        start += a.size
    rest_width = in_width - DI
    in_w = jnp.stack(
        [jnp.concatenate([big[k][1], big[k][2][:, :rest_width]], axis=1) for k in range(layers)]
    ).astype(F32)
    out_w = jnp.stack([big[k][0] for k in range(layers)]).astype(F32)
    return (
        block_out, grad[None], outs[0], in_w, outs[1], outs[2], outs[3], outs[4], outs[5],
        outs[6], out_w,
    )


def solution(mesh):
    tokens = P("fsdp", "seq", None)
    vector = P(None, "fsdp")
    matrix = P(None, "fsdp", None)
    channels = P(None, None, "fsdp")
    return jax.shard_map(
        on_device,
        mesh=mesh,
        in_specs=(
            tokens, tokens, vector, matrix, channels, vector, vector, vector, vector, vector,
            matrix,
        ),
        out_specs=(
            tokens, tokens, vector, matrix, channels, vector, vector, vector, vector, vector,
            matrix,
        ),
        check_vma=False,
    )
```

```python
import functools

import jax
import jax.numpy as jnp
from jax import lax
from jax.experimental import pallas as pl
from jax.experimental.pallas import tpu as pltpu
from jax.sharding import PartitionSpec as P

H = 32
P_SIZE = 64
N = 128
D = 1024
DI = 2048
CC = DI + 2 * N
T = 128
WB = 256
HB = WB // P_SIZE
STEPS = DI // WB
HALO = 16
F32 = jnp.float32
BF16 = jnp.bfloat16
EPS = 1e-05
VMEM_LIMIT = 50 * 1024 * 1024

L_STEP, L_CUM, L_CUMF, L_SIG = 0, 32, 64, 96


def dot(a, b):
    return jnp.dot(a, b, preferred_element_type=F32)


def dot_nt(a, b):
    return lax.dot_general(a, b, (((1,), (1,)), ((), ())), preferred_element_type=F32)


def dot_tn(a, b):
    return lax.dot_general(a, b, (((0,), (0,)), ((), ())), preferred_element_type=F32)


def sigmoid(v):
    return 0.5 * jnp.tanh(0.5 * v) + 0.5


def lane_iota(rows, lanes=128):
    return lax.broadcasted_iota(jnp.int32, (rows, lanes), 1)


def row_iota(rows, lanes=128):
    return lax.broadcasted_iota(jnp.int32, (rows, lanes), 0)


def parts_of(packed):
    high = packed.astype(BF16)
    rest = packed - high.astype(F32)
    middle = rest.astype(BF16)
    return jnp.concatenate([high, middle, (rest - middle.astype(F32)).astype(BF16)], axis=1)


def pick(first, rows, lanes, shift):
    row = jnp.bitwise_and(row_iota(rows, lanes), 127)
    head = lax.shift_right_logical(lane_iota(rows, lanes), shift)
    return jnp.where(row == first + head, 1.0, 0.0).astype(BF16)


def head_lanes(first, i):
    return pick(first + HB * i, 384, WB, 6)


def head_tiles(first, i):
    return pick(first + HB * i, 384, HB * 128, 7)


def widen(tiles):
    left = lane_iota(tiles.shape[0]) < P_SIZE
    tile = lambda h: tiles[:, h * 128 : (h + 1) * 128]
    return jnp.concatenate(
        [jnp.where(left, tile(2 * p), tile(2 * p + 1)) for p in range(HB // 2)], axis=1
    )


def halves(tile, axis_rows=True):
    left = lane_iota(tile.shape[0]) < P_SIZE
    zero = jnp.zeros_like(tile)
    return jnp.concatenate([jnp.where(left, tile, zero), jnp.where(left, zero, tile)], axis=0)


def head_rows(heads, i):
    lane = jnp.bitwise_and(lane_iota(16, 384), 127)
    sel = jnp.where(lane == L_CUM + HB * i + row_iota(16, 384), 1.0, 0.0).astype(BF16)
    return dot_nt(sel, heads)


def fill(ext, halo_ref, v_ref):
    ext[0:HALO, :] = halo_ref[...].astype(F32)
    ext[HALO:, :] = v_ref[...].astype(F32)


def conv_block(ext, taps_ref, shift_ref, c):
    total = shift_ref[0:1, :] + taps_ref[0:1, :] * ext[pl.ds(HALO - 3 + c * T, T), :]
    for k in range(1, 4):
        total = total + taps_ref[k : k + 1, :] * ext[pl.ds(HALO - 3 + k + c * T, T), :]
    return total


def state_kernel(
    v_ref, halo_ref, bc_ref, bchalo_ref, dt_ref, taps_ref, shift_ref, bctaps_ref, bcshift_ref,
    prm_ref, f_ref, tot_ref, x_ref, p_ref, p3_ref, b_ref, c_ref, bt_ref, ct_ref, ext, sumw,
    dtw, wxw,
):
    i = pl.program_id(0)
    blocks = v_ref.shape[0] // T

    @pl.when(i == 0)
    def _():
        fill(ext, bchalo_ref, bc_ref)
        lane = lane_iota(T)
        tril = (row_iota(T) >= lane).astype(F32)
        offset = jnp.zeros((1, 128), F32)
        for c in range(blocks):
            rows = pl.ds(c * T, T)
            conv = conv_block(ext, bctaps_ref, bcshift_ref, c)
            act = conv * sigmoid(conv)
            b_ref[rows, :] = act[:, :N].astype(BF16)
            c_ref[rows, :] = act[:, N:].astype(BF16)
            bt_ref[:, rows] = act[:, :N].T.astype(BF16)
            ct_ref[:, rows] = act[:, N:].T.astype(BF16)
            z = dt_ref[rows, :].astype(F32) + prm_ref[0:1, :]
            step = jnp.maximum(z, 0.0) + jnp.log1p(jnp.exp(-jnp.abs(z)))
            decay = step * prm_ref[1:2, :]
            cum = lax.dot_general(
                tril, decay, (((1,), (0,)), ((), ())),
                precision=lax.Precision.HIGHEST, preferred_element_type=F32,
            )
            cumf = cum + offset
            offset = cumf[T - 1 : T, :]
            packed = jnp.where(
                lane < L_CUM, step,
                jnp.where(lane < L_CUMF, cum, jnp.where(lane < L_SIG, cumf, 1.0 / (1.0 + jnp.exp(-z)))),
            )
            p_ref[rows, :] = packed
            p3_ref[rows, :] = parts_of(packed)

    fill(ext, halo_ref, v_ref)
    steps = head_lanes(L_STEP, i)
    sums = head_lanes(L_CUMF, i)
    heads = p3_ref[...]
    sumw[...] = dot(heads, sums)
    dtw[...] = dot(heads, steps)
    tot = sumw[blocks * T - 8 :, :][7:8, :]
    for c in range(blocks):
        rows = pl.ds(c * T, T)
        conv = conv_block(ext, taps_ref, shift_ref, c)
        x = conv * sigmoid(conv)
        x_ref[rows, :] = x
        wxw[rows, :] = (x * (jnp.exp(tot - sumw[rows, :]) * dtw[rows, :])).astype(BF16)
    f_ref[...] = dot(bt_ref[...], wxw[...]).astype(BF16)
    tot_ref[...] = jnp.broadcast_to(jnp.exp(tot), (8, WB))


def scan_kernel(
    x_ref, skip_ref, p3_ref, b_ref, c_ref, bt_ref, y_ref, cb, cumw, dtw,
):
    i = pl.program_id(0)
    blocks = x_ref.shape[0] // T

    @pl.when(i == 0)
    def _():
        causal = row_iota(T) >= lane_iota(T)
        for c in range(blocks):
            rows = pl.ds(c * T, T)
            cb[c] = jnp.where(causal, dot_nt(c_ref[rows, :], b_ref[rows, :]), 0.0)

    steps = head_lanes(L_STEP, i)
    sums = head_tiles(L_CUM, i)
    cumw[...] = dot(p3_ref[...], sums)
    dtw[...] = dot(p3_ref[...], steps)
    turned_all = head_rows(p3_ref[...], i)
    state = None
    for c in range(blocks):
        rows = pl.ds(c * T, T)
        x = x_ref[rows, :]
        cums = cumw[rows, :]
        turned = turned_all[:, c * T : (c + 1) * T]
        xd = x * dtw[rows, :]
        parts = []
        for p in range(HB // 2):
            weights = []
            for h in (2 * p, 2 * p + 1):
                across = turned[h : h + 1, :]
                e = jnp.exp(jnp.minimum(cums[:, h * 128 : (h + 1) * 128] - across, 0.0))
                weights.append((e * cb[c]).astype(BF16))
            parts.append(
                dot(
                    jnp.concatenate(weights, axis=1),
                    halves(xd[:, p * 128 : (p + 1) * 128]).astype(BF16),
                )
            )
        y = jnp.concatenate(parts, axis=1) + skip_ref[0:1, :] * x
        cumx = widen(cums)
        if state is not None:
            y = y + jnp.exp(cumx) * dot(c_ref[rows, :], state.astype(BF16))
        y_ref[rows, :] = y
        if c < blocks - 1:
            tot = cumx[T - 1 : T, :]
            fresh = dot(bt_ref[:, rows], (jnp.exp(tot - cumx) * xd).astype(BF16))
            state = fresh if state is None else state * jnp.exp(tot) + fresh


def grow_factors(p_ref, sel):
    lane = lane_iota(p_ref.shape[0])
    inside = jnp.logical_and(lane >= L_CUMF, lane < L_SIG)
    grow = jnp.where(inside, jnp.exp(jnp.where(inside, p_ref[...], 0.0)), 0.0)
    high = grow.astype(BF16)
    low = (grow - high.astype(F32)).astype(BF16)
    return dot(jnp.concatenate([high, low], axis=1), sel[...])


def gate_kernel(y_ref, gate_ref, p_ref, c_ref, s_ref, gain_ref, out_y_ref, out_ref, sel):
    @pl.when(pl.program_id(0) == 0)
    def _():
        sel[...] = pick(L_CUMF, 256, DI, 6)

    grow = grow_factors(p_ref, sel)
    y = y_ref[...] + grow * dot(c_ref[...], s_ref[...])
    out_y_ref[...] = y
    mixed = y.astype(BF16).astype(F32)
    gate = gate_ref[...]
    gated = mixed * (gate * sigmoid(gate))
    r = lax.rsqrt(jnp.mean(gated * gated, axis=1, keepdims=True) + EPS)
    out_ref[...] = (gated * r * gain_ref[0:1, :]).astype(BF16)


def gate_back_kernel(
    y_ref, gate_ref, dgn_ref, p_ref, ct_ref, gain_ref, dgate_ref, dmix_ref, gg_ref, g_ref, acc,
    sel,
):
    i = pl.program_id(0)

    @pl.when(i == 0)
    def _():
        sel[...] = pick(L_CUMF, 256, DI, 6)
        acc[...] = jnp.zeros_like(acc)
        gg_ref[...] = jnp.zeros_like(gg_ref)

    mixed = y_ref[...].astype(BF16).astype(F32)
    gate = gate_ref[...]
    sig = sigmoid(gate)
    silu = gate * sig
    gated = mixed * silu
    r = lax.rsqrt(jnp.mean(gated * gated, axis=1, keepdims=True) + EPS)
    q = gated * r
    dgn = dgn_ref[...]
    gg_ref[...] += jnp.broadcast_to(jnp.sum(dgn * q, axis=0, keepdims=True), gg_ref.shape)
    dq = dgn * gain_ref[0:1, :]
    dgated = r * (dq - q * jnp.mean(dq * q, axis=1, keepdims=True))
    dgate_ref[...] = (dgated * mixed * (sig * (1.0 + gate * (1.0 - sig)))).astype(BF16)
    dmix = (dgated * silu).astype(BF16)
    dmix_ref[...] = dmix
    grow = grow_factors(p_ref, sel)
    acc[...] += dot(ct_ref[...], (grow * dmix.astype(F32)).astype(BF16))

    @pl.when(i == pl.num_programs(0) - 1)
    def _():
        g_ref[...] = acc[...].astype(BF16)


def conv_back(ext, dext, taps_ref, dv_ref, tail_ref, head_ref, stats_ref, blocks):
    early = dext[0:8, :]
    before = ext[HALO - 8 : HALO, :]
    sums = []
    for k in range(5):
        sums.append(jnp.zeros((1, WB), F32))
        for j in range(3 - k):
            sums[k] = sums[k] + early[j : j + 1, :] * before[5 + k + j : 6 + k + j, :]
    for c in range(blocks):
        v = ext[pl.ds(HALO + c * T, T), :]
        total = None
        for k in (3, 2, 1, 0):
            d = dext[pl.ds(c * T + 3 - k, T), :]
            total = taps_ref[k : k + 1, :] * d if total is None else total + taps_ref[k : k + 1, :] * d
            sums[k] = sums[k] + jnp.sum(d * v, axis=0, keepdims=True)
            if k == 3:
                sums[4] = sums[4] + jnp.sum(d, axis=0, keepdims=True)
        dv_ref[pl.ds(c * T, T), :] = total.astype(BF16)
        if c == blocks - 1:
            tail_ref[...] = total[T - 8 :, :]
    head_ref[...] = dext[0:8, :]
    for k in range(5):
        stats_ref[k : k + 1, :] = sums[k]


def back_inside_kernel(
    x_ref, p3_ref, b_ref, c_ref, dy_ref, dxd_ref, dcbt_ref, cbt, cumw, dtw, first,
):
    i = pl.program_id(0) + first
    blocks = x_ref.shape[0] // T

    @pl.when(pl.program_id(0) == 0)
    def _():
        causal = row_iota(T) <= lane_iota(T)
        for c in range(blocks):
            rows = pl.ds(c * T, T)
            cbt[c] = jnp.where(causal, dot_nt(b_ref[rows, :], c_ref[rows, :]), 0.0)
        dcbt_ref[...] = jnp.zeros_like(dcbt_ref)

    steps = head_lanes(L_STEP, i)
    sums = head_tiles(L_CUM, i)
    cumw[...] = dot(p3_ref[...], sums)
    dtw[...] = dot(p3_ref[...], steps)
    turned_all = head_rows(p3_ref[...], i)
    for c in range(blocks):
        rows = pl.ds(c * T, T)
        cums = cumw[rows, :]
        turned = turned_all[:, c * T : (c + 1) * T]
        xd = x_ref[rows, :] * dtw[rows, :]
        dyb = dy_ref[rows, :]
        dy = dyb.astype(F32)
        dcb = jnp.zeros((T, T), F32)
        for p in range(HB // 2):
            lanes = slice(p * 128, (p + 1) * 128)
            dm = dot_nt(halves(xd[:, lanes]).astype(BF16), dyb[:, lanes])
            weights = []
            for j in range(2):
                h = 2 * p + j
                across = turned[h : h + 1, :]
                e = jnp.exp(jnp.minimum(across - cums[:, h * 128 : (h + 1) * 128], 0.0))
                weights.append((e * cbt[c]).astype(BF16))
                dcb = dcb + dm[j * T : (j + 1) * T, :] * e
            dxd_ref[rows, lanes] = dot(
                jnp.concatenate(weights, axis=1), halves(dy[:, lanes]).astype(BF16)
            )
        dcbt_ref[c] += dcb


def back_kernel(
    v_ref, halo_ref, bc_ref, bchalo_ref, taps_ref, shift_ref, bctaps_ref, bcshift_ref, skip_ref,
    prm_ref, p_ref, p3_ref, b_ref, c_ref, bt_ref, ct_ref, s_ref, gin_ref, dy_ref, y_ref,
    inside_low_ref, inside_high_ref, low_ref, high_ref,
    dv_ref, tail_ref, head_ref, stats_ref, bdv_ref, btail_ref, bhead_ref, bstats_ref,
    ddt_ref, dtstats_ref,
    ext, dext, convs, sigs, cumw, dtw, prods, acc, dbacc, dcacc,
):
    i = pl.program_id(0)
    blocks = v_ref.shape[0] // T
    length = blocks * T

    @pl.when(i == 0)
    def _():
        acc[...] = jnp.zeros_like(acc)
        dbacc[...] = jnp.zeros_like(dbacc)
        dcacc[...] = jnp.zeros_like(dcacc)

    fill(ext, halo_ref, v_ref)
    dext[length:, :] = jnp.zeros((8, WB), F32)
    steps = head_lanes(L_STEP, i)
    sums = head_lanes(L_CUM, i)
    cumw[...] = dot(p3_ref[...], sums)
    dtw[...] = dot(p3_ref[...], steps)
    states = [s_ref[...].astype(F32)]
    for c in range(blocks):
        rows = pl.ds(c * T, T)
        conv = conv_block(ext, taps_ref, shift_ref, c)
        sig = sigmoid(conv)
        convs[rows, :] = conv
        sigs[rows, :] = sig
        cumx, dt = cumw[rows, :], dtw[rows, :]
        tot = cumx[T - 1 : T, :]
        wx = (jnp.exp(tot - cumx) * (conv * sig * dt)).astype(BF16)
        states.append(states[-1] * jnp.exp(tot) + dot(bt_ref[:, rows], wx))

    ch = lax.shift_right_logical(row_iota(WB), 6)
    seg1 = (lane_iota(WB) == HB * i + ch).astype(BF16)
    seg2 = (lane_iota(WB) == 32 + HB * i + ch).astype(BF16)
    final = row_iota(T, WB) == T - 1
    lower = jnp.full((T, WB), i, jnp.int32) < STEPS // 2
    grad = gin_ref[...].astype(F32)
    skip_sum = jnp.zeros((1, WB), F32)
    for c in reversed(range(blocks)):
        rows = pl.ds(c * T, T)
        conv, sig = convs[rows, :], sigs[rows, :]
        x = conv * sig
        cumx, dt = cumw[rows, :], dtw[rows, :]
        tot = cumx[T - 1 : T, :]
        xd = x * dt
        xdb = xd.astype(BF16)
        dyb = dy_ref[rows, :]
        dy = dyb.astype(F32)
        gb = grad.astype(BF16)
        w = jnp.exp(tot - cumx)
        inside = jnp.where(lower, inside_low_ref[rows, :], inside_high_ref[rows, :])
        dxd = inside + w * dot(b_ref[rows, :], gb)
        ey = (jnp.exp(cumx) * dy).astype(BF16)
        wx = (w * xd).astype(BF16)
        dcacc[rows, :] += dot_nt(ey, states[c].astype(BF16))
        dbacc[rows, :] += dot_nt(wx, gb)
        bound = jnp.sum(grad * states[c + 1], axis=0, keepdims=True)
        skip = skip_ref[0:1, :]
        p1 = dy * (y_ref[rows, :] - skip * x) - xdb.astype(F32) * dxd
        p1 = p1 + jnp.where(final, bound, 0.0)
        p2 = x * dxd
        p1h = p1.astype(BF16)
        p2h = p2.astype(BF16)
        sides = (p1h, (p1 - p1h.astype(F32)).astype(BF16), p2h, (p2 - p2h.astype(F32)).astype(BF16))
        for k, side in enumerate(sides):
            prods[rows, k * WB : (k + 1) * WB] = side
        skip_sum = skip_sum + jnp.sum(x * dy, axis=0, keepdims=True)
        dx = dt * dxd + skip * dy
        dext[rows, :] = dx * (sig * (1.0 + conv * (1.0 - sig)))
        grad = grad * jnp.exp(tot) + dot(ct_ref[:, rows], ey)
    acc[...] += dot(prods[...], jnp.concatenate([seg1, seg1, seg2, seg2], axis=0))
    conv_back(ext, dext, taps_ref, dv_ref, tail_ref, head_ref, stats_ref, blocks)
    stats_ref[5:6, :] = skip_sum

    @pl.when(i == pl.num_programs(0) - 1)
    def _():
        fill(ext, bchalo_ref, bc_ref)
        triu = (row_iota(T) <= lane_iota(T)).astype(F32)
        rate = prm_ref[1:2, :]
        rate_sum = jnp.zeros((1, 128), F32)
        bias_sum = jnp.zeros((1, 128), F32)
        for c in range(blocks):
            rows = pl.ds(c * T, T)
            causal = row_iota(T) <= lane_iota(T)
            m = jnp.where(causal, low_ref[c] + high_ref[c], 0.0).astype(BF16)
            db = dbacc[rows, :] + dot(m, c_ref[rows, :])
            dc = dcacc[rows, :] + dot_tn(m, b_ref[rows, :])
            conv = conv_block(ext, bctaps_ref, bcshift_ref, c)
            sig = sigmoid(conv)
            dext[rows, :] = jnp.concatenate([db, dc], axis=1) * (
                sig * (1.0 + conv * (1.0 - sig))
            )
            a = acc[rows, :]
            ddecay = lax.dot_general(
                triu, a, (((1,), (0,)), ((), ())),
                precision=lax.Precision.HIGHEST, preferred_element_type=F32,
            )
            packed = p_ref[rows, :]
            rate_sum = rate_sum + jnp.sum(packed * ddecay, axis=0, keepdims=True)
            dz = (pltpu.roll(a, 96, 1) + rate * ddecay) * pltpu.roll(packed, 32, 1)
            ddt_ref[rows, :] = jnp.where(lane_iota(T) < H, dz, 0.0).astype(BF16)
            bias_sum = bias_sum + jnp.sum(dz, axis=0, keepdims=True)
        conv_back(ext, dext, bctaps_ref, bdv_ref, btail_ref, bhead_ref, bstats_ref, blocks)
        dtstats_ref[0:1, :] = rate_sum * rate
        dtstats_ref[1:2, :] = bias_sum


def whole(shape):
    return pl.BlockSpec(shape, lambda i: (0,) * len(shape))


def wide(rows):
    return pl.BlockSpec((rows, WB), lambda i: (0, i))


def bc_block(rows):
    return pl.BlockSpec((rows, WB), lambda i: (0, STEPS))


def shape_of(shape, dtype):
    return jax.ShapeDtypeStruct(shape, dtype)


def params():
    return pltpu.CompilerParams(vmem_limit_bytes=VMEM_LIMIT)


def cost(flops, moved):
    return pl.CostEstimate(flops=int(flops), bytes_accessed=int(moved), transcendentals=0)


def local_state(r_low, halo, taps, shift, prm):
    length = r_low.shape[0]
    return pl.pallas_call(
        state_kernel,
        name="local_state",
        grid=(STEPS,),
        in_specs=[
            wide(length), wide(HALO), bc_block(length), bc_block(HALO),
            pl.BlockSpec((length, 128), lambda i: (0, CC // 128)),
            wide(4), wide(1), bc_block(4), bc_block(1), whole((8, 128)),
        ],
        out_specs=[
            wide(N), wide(8), wide(length), whole((length, 128)), whole((length, 384)),
            whole((length, N)), whole((length, N)), whole((N, length)), whole((N, length)),
        ],
        out_shape=[
            shape_of((N, DI), BF16), shape_of((8, DI), F32), shape_of((length, DI), F32),
            shape_of((length, 128), F32), shape_of((length, 384), BF16),
            shape_of((length, N), BF16), shape_of((length, N), BF16),
            shape_of((N, length), BF16), shape_of((N, length), BF16),
        ],
        scratch_shapes=[
            pltpu.VMEM((HALO + length, WB), F32), pltpu.VMEM((length, WB), F32),
            pltpu.VMEM((length, WB), F32), pltpu.VMEM((length, WB), BF16),
        ],
        compiler_params=params(),
        cost_estimate=cost(4e9, 8e6),
    )(r_low, halo, r_low, halo, r_low, taps, shift, taps, shift, prm)


def local_scan(x, skip, p3, b, c, bt):
    length = x.shape[0]
    return pl.pallas_call(
        scan_kernel,
        name="local_scan",
        grid=(STEPS,),
        in_specs=[
            wide(length), wide(1), whole((length, 384)),
            whole((length, N)), whole((length, N)), whole((N, length)),
        ],
        out_specs=wide(length),
        out_shape=shape_of((length, DI), F32),
        scratch_shapes=[
            pltpu.VMEM((length // T, T, T), F32), pltpu.VMEM((length, HB * 128), F32),
            pltpu.VMEM((length, WB), F32),
        ],
        compiler_params=params(),
        cost_estimate=cost(1.5e10, 8e6),
    )(x, skip, p3, b, c, bt)


def gate_forward(y, gate, p, c, s_in, gain):
    length = y.shape[0]
    rows = lambda width: pl.BlockSpec((T, width), lambda i: (i, 0))
    return pl.pallas_call(
        gate_kernel,
        name="gate_forward",
        grid=(length // T,),
        in_specs=[rows(DI), rows(DI), rows(128), rows(N), whole((N, DI)), whole((1, DI))],
        out_specs=[rows(DI), rows(DI)],
        out_shape=[shape_of((length, DI), F32), shape_of((length, DI), BF16)],
        scratch_shapes=[pltpu.VMEM((256, DI), BF16)],
        compiler_params=params(),
        cost_estimate=cost(5e9, 15e6),
    )(y, gate, p, c, s_in, gain)


def gate_backward(y, gate, dgn, p, ct, gain):
    length = y.shape[0]
    rows = lambda width: pl.BlockSpec((T, width), lambda i: (i, 0))
    return pl.pallas_call(
        gate_back_kernel,
        name="gate_backward",
        grid=(length // T,),
        in_specs=[
            rows(DI), rows(DI), rows(DI), rows(128),
            pl.BlockSpec((N, T), lambda i: (0, i)), whole((1, DI)),
        ],
        out_specs=[rows(DI), rows(DI), whole((8, DI)), whole((N, DI))],
        out_shape=[
            shape_of((length, DI), BF16), shape_of((length, DI), BF16),
            shape_of((8, DI), F32), shape_of((N, DI), BF16),
        ],
        scratch_shapes=[pltpu.VMEM((N, DI), F32), pltpu.VMEM((256, DI), BF16)],
        compiler_params=params(),
        cost_estimate=cost(1e10, 17e6),
    )(y, gate, dgn, p, ct, gain)


def scan_inside(x, p3, b, c, dy, first):
    length = x.shape[0]
    blocks = length // T
    wide_from = lambda rows: pl.BlockSpec((rows, WB), lambda i: (0, i + first))
    return pl.pallas_call(
        functools.partial(back_inside_kernel, first=first),
        name="scan_inside",
        grid=(STEPS // 2,),
        in_specs=[
            wide_from(length), whole((length, 384)), whole((length, N)),
            whole((length, N)), wide_from(length),
        ],
        out_specs=[wide(length), whole((blocks, T, T))],
        out_shape=[shape_of((length, DI // 2), F32), shape_of((blocks, T, T), F32)],
        scratch_shapes=[
            pltpu.VMEM((blocks, T, T), F32), pltpu.VMEM((length, HB * 128), F32),
            pltpu.VMEM((length, WB), F32),
        ],
        compiler_params=params(),
        cost_estimate=cost(1e10, 6e6),
    )(x, p3, b, c, dy)


def scan_backward(
    r_low, halo, taps, shift, skip, prm, p, p3, b, c, bt, ct, s_in, g_in, dy, y, low, high
):
    length = r_low.shape[0]
    blocks = length // T
    return pl.pallas_call(
        back_kernel,
        name="scan_backward",
        grid=(STEPS,),
        in_specs=[
            wide(length), wide(HALO), bc_block(length), bc_block(HALO),
            wide(4), wide(1), bc_block(4), bc_block(1), wide(1), whole((8, 128)),
            whole((length, 128)), whole((length, 384)), whole((length, N)), whole((length, N)),
            whole((N, length)), whole((N, length)), wide(N), wide(N), wide(length), wide(length),
            pl.BlockSpec((length, WB), lambda i: (0, jnp.minimum(i, STEPS // 2 - 1))),
            pl.BlockSpec((length, WB), lambda i: (0, jnp.maximum(i - STEPS // 2, 0))),
            whole((blocks, T, T)), whole((blocks, T, T)),
        ],
        out_specs=[
            wide(length), wide(8), wide(8), wide(8),
            whole((length, WB)), whole((8, WB)), whole((8, WB)), whole((8, WB)),
            whole((length, 128)), whole((8, 128)),
        ],
        out_shape=[
            shape_of((length, DI), BF16), shape_of((8, DI), F32), shape_of((8, DI), F32),
            shape_of((8, DI), F32),
            shape_of((length, WB), BF16), shape_of((8, WB), F32), shape_of((8, WB), F32),
            shape_of((8, WB), F32),
            shape_of((length, 128), BF16), shape_of((8, 128), F32),
        ],
        scratch_shapes=[
            pltpu.VMEM((HALO + length, WB), F32),
            pltpu.VMEM((length + 8, WB), F32),
            pltpu.VMEM((length, WB), F32),
            pltpu.VMEM((length, WB), F32),
            pltpu.VMEM((length, WB), F32),
            pltpu.VMEM((length, WB), F32),
            pltpu.VMEM((length, 4 * WB), BF16),
            pltpu.VMEM((length, 128), F32),
            pltpu.VMEM((length, 128), F32),
            pltpu.VMEM((length, 128), F32),
        ],
        compiler_params=params(),
        cost_estimate=cost(3e10, 16e6),
    )(
        r_low, halo, r_low, halo, taps, shift, taps, shift, skip, prm, p, p3, b, c, bt, ct,
        s_in, g_in, dy, y, low[0], high[0], low[1], high[1],
    )


def add(a, b):
    return (a.astype(F32) + b.astype(F32)).astype(BF16)


def swap(a, axis, bit):
    return lax.ppermute(a, axis, [(k, k ^ bit) for k in range(lax.axis_size(axis))])


def hop_to(message, state, hop, upward):
    last = lax.axis_size("seq") - 1
    pair = (hop, hop + 1) if upward else (last - hop, last - hop - 1)
    got = lax.ppermute(message, "seq", [pair])
    return got if state is None else got + state


def message_of(local, decay, state):
    return (local.astype(F32) + decay * state.astype(F32)).astype(BF16)


def pass_along(local, decay, upward, work):
    hops = lax.axis_size("seq") - 1
    state = None
    done = []
    for hop in range(hops):
        message = local if hop == 0 else message_of(local, decay, state)
        state = hop_to(message, state, hop, upward)
        if work:
            item = work[0]()
            work = work[1:]
            state, item = lax.optimization_barrier((state, item))
            done.append(item)
    for item in work:
        done.append(item())
    return state, done


def pieces_kernel(order_ref, left_ref, base_ref, *refs):
    del order_ref
    for m, piece in enumerate(refs[:-1]):

        @pl.when(pl.program_id(0) == m)
        def _(m=m, piece=piece):
            total = base_ref[...] if m == 0 else refs[-1][...]
            refs[-1][...] = total + dot(left_ref[...], piece[...])


def pieces_back_kernel(order_ref, left_ref, *refs):
    del order_ref
    for m, piece in enumerate(refs[:-1]):

        @pl.when(pl.program_id(0) == m)
        def _(piece=piece):
            refs[-1][...] = dot_nt(left_ref[...], piece[...])


def xor_order():
    n = lax.axis_size("fsdp")
    return jnp.bitwise_xor(lax.axis_index("fsdp"), jnp.arange(n)).astype(jnp.int32)


def fixed(shape):
    return pl.BlockSpec(shape, lambda i, order: (0,) * len(shape))


def add_product(base, left, w):
    if not isinstance(w, list):
        return base + dot(left, w)
    return pl.pallas_call(
        pieces_kernel,
        name="add_product",
        grid_spec=pltpu.PrefetchScalarGridSpec(
            num_scalar_prefetch=1,
            grid=(len(w),),
            in_specs=[
                pl.BlockSpec((left.shape[0], w[0].shape[0]), lambda i, order: (0, order[i])),
                fixed(base.shape),
            ]
            + [fixed(w[0].shape)] * len(w),
            out_specs=fixed(base.shape),
        ),
        out_shape=shape_of(base.shape, F32),
        compiler_params=params(),
        cost_estimate=cost(2e9, 10e6),
    )(xor_order(), left, base, *w)


def product_back(left, w):
    if not isinstance(w, list):
        return dot_nt(left, w)
    length = left.shape[0]
    return pl.pallas_call(
        pieces_back_kernel,
        name="product_back",
        grid_spec=pltpu.PrefetchScalarGridSpec(
            num_scalar_prefetch=1,
            grid=(len(w),),
            in_specs=[fixed(left.shape)] + [fixed(w[0].shape)] * len(w),
            out_specs=pl.BlockSpec((length, w[0].shape[0]), lambda i, order: (0, order[i])),
        ),
        out_shape=shape_of((length, len(w) * w[0].shape[0]), F32),
        compiler_params=params(),
        cost_estimate=cost(2e9, 10e6),
    )(xor_order(), left, *w)


def give_kernel(left_ref, right_ref, out_ref):
    out_ref[...] = dot_tn(left_ref[...], right_ref[...]).astype(BF16)


def own_kernel(left_ref, right_ref, got_ref, *out_refs):
    value = dot_tn(left_ref[...], right_ref[...]) + got_ref[...].astype(F32)
    rows = out_refs[0].shape[0]
    for d, out_ref in enumerate(out_refs):
        out_ref[...] = value[d * rows : (d + 1) * rows].astype(BF16)


def shard_columns(left, core):
    n = lax.axis_size("fsdp")
    me = lax.axis_index("fsdp")
    width = left.shape[1] // n
    return jnp.concatenate(
        [
            lax.dynamic_slice_in_dim(left, jnp.bitwise_xor(me, 2 * d + core) * width, width, 1)
            for d in range(n // 2)
        ],
        axis=1,
    )


def product_give(left, right):
    length, rows = left.shape
    columns = right.shape[1]
    block = columns // 2 if columns % 256 == 0 else columns
    return pl.pallas_call(
        give_kernel,
        name="product_give",
        grid=(columns // block,),
        in_specs=[whole((length, rows)), pl.BlockSpec((length, block), lambda i: (0, i))],
        out_specs=pl.BlockSpec((rows, block), lambda i: (0, i)),
        out_shape=shape_of((rows, columns), BF16),
        compiler_params=params(),
        cost_estimate=cost(3e9, 8e6),
    )(left, right)


def product_own(left, right, got):
    chips = lax.axis_size("fsdp") // 2
    length, rows = left.shape
    columns = right.shape[1]
    block = columns // 2 if columns % 256 == 0 else columns
    blocks = lambda height: pl.BlockSpec((height, block), lambda i: (0, i))
    return pl.pallas_call(
        own_kernel,
        name="product_own",
        grid=(columns // block,),
        in_specs=[whole((length, rows)), blocks(length), blocks(rows)],
        out_specs=[blocks(rows // chips)] * chips,
        out_shape=[shape_of((rows // chips, columns), BF16)] * chips,
        compiler_params=params(),
        cost_estimate=cost(3e9, 10e6),
    )(left, right, got)


def send_chips(parts):
    return parts[0], [swap(part, "fsdp", 2 * d) for d, part in enumerate(parts) if d]


def gather_sum(own, got):
    total = own.astype(F32)
    for piece in got:
        total = total + piece.astype(F32)
    return total.astype(BF16)


def tie(*values):
    return lax.optimization_barrier(values)


def seq_first(a):
    odd = lax.axis_index("seq") % 2
    half = a.shape[0] // 2
    keep = lax.dynamic_slice_in_dim(a, odd * half, half, 0)
    give = lax.dynamic_slice_in_dim(a, (1 - odd) * half, half, 0)
    return keep, swap(give, "seq", 1)


def seq_across(keep, got):
    keep = add(keep, got)
    bit = 2
    while 2 * bit < lax.axis_size("seq"):
        keep = add(keep, swap(keep, "seq", bit))
        bit *= 2
    return keep, swap(keep, "seq", bit)


def seq_back(keep, got):
    keep = add(keep, got)
    return keep, swap(keep, "seq", 1)


def seq_join(keep, other):
    odd = lax.axis_index("seq") % 2
    return jnp.where(
        odd == 0, jnp.concatenate([keep, other]), jnp.concatenate([other, keep])
    )


def sum_over(a, *axes):
    for axis in axes:
        bit = 1
        while bit < lax.axis_size(axis):
            a = a + swap(a, axis, bit)
            bit *= 2
    return a


def turn_kernel(*refs):
    out_ref = refs[-1]
    for k in range(len(refs) // 2):
        row = 0
        for ref in refs[2 * k : 2 * k + 2]:
            for j in range(0, ref.shape[1], 128):
                rows = min(128, out_ref.shape[1] - row)
                tile = ref[:, j : j + 128].astype(F32).T
                out_ref[k, row : row + rows, :] = tile[:rows, :]
                row += rows


def in_weight_rows(pieces, in_width):
    flat = [piece for pair in pieces for piece in pair]
    return pl.pallas_call(
        turn_kernel,
        name="in_weight_rows",
        out_shape=shape_of((len(pieces), in_width, flat[0].shape[0]), F32),
        compiler_params=params(),
        cost_estimate=cost(0, 7e6),
    )(*flat)


def on_device(
    hidden_in, cotangent, norm_gain, input_projection_weight, conv_weight, conv_bias, dt_bias,
    a_log, skip, gate_gain, output_projection_weight,
):
    layers, _, in_width = input_projection_weight.shape
    seq_parts = lax.axis_size("seq")
    up = [(z, z + 1) for z in range(seq_parts - 1)]
    down = [(z + 1, z) for z in range(seq_parts - 1)]

    small = [norm_gain, conv_weight, conv_bias, dt_bias, a_log, skip, gate_gain]
    flat = jnp.concatenate([a.reshape(layers, -1) for a in small], axis=1)
    shards = lax.axis_size("fsdp")
    packed = lax.all_gather(flat, "fsdp", axis=0)
    packed = packed.astype(F32)
    unpacked = []
    start = 0
    for a in small:
        width = a[0].size
        piece = packed[:, :, start : start + width].reshape((shards,) + a.shape)
        start += width
        piece = jnp.moveaxis(piece, 0, -2)
        unpacked.append(piece.reshape(a.shape[:-1] + (shards * a.shape[-1],)))
    gains, taps_all, shift_all, bias_all, rate_all, skip_all, gate_all = unpacked

    by_pieces = output_projection_weight.shape[1] % 128 == 0
    weights = []
    for layer in range(layers):
        w = input_projection_weight[layer]
        rest = jnp.concatenate([w[:, DI : DI + CC]] + [w[:, DI + CC :]] * 4, axis=1)
        rest = lax.all_gather(rest, "fsdp", axis=0, tiled=True)
        if layer == 0:
            rest, first_out = tie(rest, output_projection_weight[0])
            if by_pieces:
                near = swap(first_out, "fsdp", 1)
                arrived = [swap(first_out, "fsdp", 2 * d) for d in range(1, shards // 2)]
        weights.append(
            (
                rest,
                lax.all_gather(w[:, :DI], "fsdp", axis=0, tiled=True),
                None
                if layer == 0 and by_pieces
                else lax.all_gather(output_projection_weight[layer], "fsdp", axis=0, tiled=True),
            )
        )

    hidden = hidden_in[0].astype(F32)
    stored = []
    for layer in range(layers):
        w_rest, w_gate, w_out = weights[layer]
        r_in = lax.rsqrt(jnp.mean(hidden * hidden, axis=1, keepdims=True) + EPS)
        normed = (hidden * r_in * gains[layer][None, :]).astype(BF16)
        r_low = dot(normed, w_rest).astype(BF16)
        halo = lax.ppermute(r_low[-HALO:, :CC], "seq", up)
        taps = taps_all[layer]
        shift = shift_all[layer][None, :]
        skip_wide = jnp.repeat(skip_all[layer], P_SIZE)[None, :]
        prm = jnp.zeros((8, 128), F32)
        prm = prm.at[0].set(jnp.tile(bias_all[layer], 4))
        prm = prm.at[1].set(jnp.tile(-jnp.exp(rate_all[layer]), 4))
        f, decay, x, p, p3, b, c, bt, ct = local_state(r_low, halo, taps, shift, prm)
        state = hop_to(f, None, 0, True)
        y = local_scan(x, skip_wide, p3, b, c, bt)
        state, y = tie(state, y)
        if w_out is None:
            y, arrived = tie(y, arrived)
            swapped = [swap(piece, "fsdp", 1) for piece in arrived]
        for hop in range(1, seq_parts - 1):
            state = hop_to(message_of(f, decay[0:1], state), state, hop, True)
            if hop == 1:
                gate = dot(normed, w_gate)
                state, gate = tie(state, gate)
                if w_out is None:
                    gate, swapped = tie(gate, swapped)
                    w_out = [first_out, near]
                    for pair in zip(arrived, swapped):
                        w_out += pair
                    weights[layer] = (w_rest, w_gate, w_out)
        s_in = state
        y, gate_low = gate_forward(y, gate, p, c, s_in, gate_all[layer][None, :])
        stored.append(
            (
                hidden, r_in, normed, r_low, halo, gate, taps, shift, skip_wide, prm, decay, x, p,
                p3, b, c, bt, ct, s_in, y, gate_low,
            )
        )
        hidden = add_product(hidden, gate_low, w_out)
    block_out = hidden.astype(BF16)[None]

    block_out, cotangent = tie(block_out, cotangent)
    grad = cotangent[0].astype(F32)
    big = [None] * layers
    vectors = [None] * layers
    waiting = None
    for layer in reversed(range(layers)):
        (
            hidden, r_in, normed, r_low, halo, gate, taps, shift, skip_wide, prm, decay, x, p,
            p3, b, c, bt, ct, s_in, y, gate_low,
        ) = stored[layer]
        w_rest, w_gate, w_out = weights[layer]
        d_branch = grad.astype(BF16)
        dgn = product_back(d_branch, w_out)
        dgate, dmix, gain_out_grad, g_local = gate_backward(
            y, gate, dgn, p, ct, gate_all[layer][None, :]
        )

        if waiting is not None:
            scattered, g_local = tie(scattered, g_local)
            big[layer + 1] = [lax.psum(a, "seq") for a in scattered]

        normed_give, normed_own = shard_columns(normed, 1), shard_columns(normed, 0)
        inside = lambda first: scan_inside(x, p3, b, c, dmix, first)
        if layer == 0:
            out_give = product_give(shard_columns(gate_low, 1), d_branch)
            state = hop_to(g_local, None, 0, False)
            low = inside(0)
            state, out_give, low, rest_sent = tie(state, out_give, low, rest_sent)
            above = seq_first(gather_sum(rest_mine, rest_sent))
            for hop in range(1, seq_parts - 1):
                state = hop_to(message_of(g_local, decay[0:1], state), state, hop, False)
                if hop == 1:
                    out_got = swap(out_give, "fsdp", 1)
                    gate_give = product_give(normed_give, dgate)
                    high = inside(STEPS // 2)
                    state, out_got, gate_give, high, above = tie(
                        state, out_got, gate_give, high, above
                    )
                    above = seq_across(*above)
                    gate_got = swap(gate_give, "fsdp", 1)
                    out_parts = product_own(shard_columns(gate_low, 0), d_branch, out_got)
                elif hop == 2:
                    out_parts, state = tie(out_parts, state)
                    out_mine, out_sent = send_chips(out_parts)
                    state, gate_got, above = tie(state, gate_got, above)
                    above = seq_back(*above)
                    gate_parts = product_own(normed_own, dgate, gate_got)
                    state, gate_parts = tie(state, gate_parts)
                    gate_mine, gate_sent = send_chips(gate_parts)
        else:
            state, ((out_grad, gate_w_grad), low, high) = pass_along(
                g_local,
                decay[0:1],
                False,
                [
                    lambda: (
                        dot_tn(gate_low, d_branch).astype(BF16),
                        dot_tn(normed, dgate).astype(BF16),
                    ),
                    lambda: inside(0),
                    lambda: inside(STEPS // 2),
                ],
            )
            scattered = [
                lax.psum_scatter(a, "fsdp", scatter_dimension=0, tiled=True)
                for a in (out_grad, gate_w_grad)
            ]
        back = scan_backward(
            r_low, halo, taps, shift, skip_wide, prm, p, p3, b, c, bt, ct, s_in, state, dmix, y,
            low, high,
        )
        if layer == 0:
            back, out_sent, gate_sent, above, big[layer + 1] = tie(
                back, out_sent, gate_sent, above, big[layer + 1]
            )
            big[layer + 1].append(seq_join(*above))
            out_seq = seq_first(gather_sum(out_mine, out_sent))
            gate_sum = gather_sum(gate_mine, gate_sent)
        dv, tail, head, stats, bdv, btail, bhead, bstats, ddt, dtstats = back
        heads_in = lax.ppermute(jnp.concatenate([head, bhead], axis=1), "seq", down)
        tail = jnp.concatenate([tail, btail], axis=1)
        fix = [tail[j : j + 1] for j in range(8)]
        for j in range(3):
            for k in range(j + 1):
                fix[5 + j] = fix[5 + j] + taps[k : k + 1] * heads_in[j - k : j - k + 1]
        d_rest = jnp.concatenate([dv, bdv, ddt], axis=1)
        d_rest = lax.dynamic_update_slice(
            d_rest, jnp.concatenate(fix, axis=0).astype(BF16), (d_rest.shape[0] - 8, 0)
        )
        give = product_give(normed_give, d_rest)
        if layer == 0:
            give, out_seq = tie(give, out_seq)
            out_seq = seq_across(*out_seq)
            gate_seq = seq_first(gate_sum)
        got = swap(give, "fsdp", 1)
        d_normed = dot_nt(dgate, w_gate)
        got, d_normed = tie(got, d_normed)
        if layer > 0:
            parts = product_own(normed_own, d_rest, got)
            parts, d_rest = tie(parts, d_rest)
            rest_mine, rest_sent = send_chips(parts)
        d_normed = d_normed + dot_nt(d_rest, w_rest)
        q = hidden * r_in
        dq = d_normed * gains[layer][None, :]
        gain_in_grad = jnp.sum(d_normed * q, axis=0)
        grad = grad + r_in * (dq - q * jnp.mean(dq * q, axis=1, keepdims=True))
        if layer == 0:
            grad, gain_in_grad, got = tie(grad, gain_in_grad, got)
            parts = product_own(normed_own, d_rest, got)
            parts, out_seq, gate_seq = tie(parts, out_seq, gate_seq)
            rest_mine, rest_sent = send_chips(parts)
            out_seq = seq_back(*out_seq)
            gate_seq = seq_across(*gate_seq)
            out_seq, gate_seq, rest_sent = tie(out_seq, gate_seq, rest_sent)
            gate_seq = seq_back(*gate_seq)
            rest_seq = seq_first(gather_sum(rest_mine, rest_sent))
            rest_seq, gate_seq = tie(rest_seq, gate_seq)
            rest_seq = seq_back(*seq_across(*rest_seq))
            big[layer] = [seq_join(*out_seq), seq_join(*gate_seq), seq_join(*rest_seq)]
        waiting = layer
        stats = jnp.concatenate([stats, bstats], axis=1)
        vectors[layer] = [
            gain_in_grad,
            stats[0:4],
            stats[4],
            dtstats[1, :H],
            dtstats[0, :H],
            stats[5, :DI].reshape(H, P_SIZE).sum(axis=1),
            gain_out_grad[0],
        ]

    rows = []
    for a, member in zip(small, range(len(small))):
        full = jnp.stack([vectors[layer][member] for layer in range(layers)])
        full = full.reshape(a.shape[:-1] + (shards, a.shape[-1]))
        rows.append(jnp.moveaxis(full, -2, 0).reshape(shards, -1))
    vector, rest_sent = tie(jnp.concatenate(rows, axis=1), rest_sent)
    summed = sum_over(vector, "fsdp", "seq")
    mine = lax.dynamic_index_in_dim(summed, lax.axis_index("fsdp"), 0, keepdims=False)
    outs = []
    start = 0
    for a in small:
        outs.append(mine[start : start + a.size].reshape(a.shape))
        start += a.size
    in_w = in_weight_rows([big[k][1:] for k in range(layers)], in_width)
    in_w = jnp.swapaxes(in_w, 1, 2)
    out_w = jnp.stack([big[k][0] for k in range(layers)]).astype(F32)
    return (
        block_out, grad[None], outs[0], in_w, outs[1], outs[2], outs[3], outs[4], outs[5],
        outs[6], out_w,
    )


def solution(mesh):
    tokens = P("fsdp", "seq", None)
    vector = P(None, "fsdp")
    matrix = P(None, "fsdp", None)
    channels = P(None, None, "fsdp")
    return jax.shard_map(
        on_device,
        mesh=mesh,
        in_specs=(
            tokens, tokens, vector, matrix, channels, vector, vector, vector, vector, vector,
            matrix,
        ),
        out_specs=(
            tokens, tokens, vector, matrix, channels, vector, vector, vector, vector, vector,
            matrix,
        ),
        check_vma=False,
    )
```

```python
import functools

import jax
import jax.numpy as jnp
from jax import lax
from jax.experimental import pallas as pl
from jax.experimental.pallas import tpu as pltpu
from jax.sharding import PartitionSpec as P

H = 32
P_SIZE = 64
N = 128
D = 1024
DI = 2048
CC = DI + 2 * N
T = 128
WB = 256
HB = WB // P_SIZE
STEPS = DI // WB
HALO = 16
F32 = jnp.float32
BF16 = jnp.bfloat16
EPS = 1e-05
VMEM_LIMIT = 50 * 1024 * 1024

L_STEP, L_CUM, L_CUMF, L_SIG = 0, 32, 64, 96


def dot(a, b):
    return jnp.dot(a, b, preferred_element_type=F32)


def dot_nt(a, b):
    return lax.dot_general(a, b, (((1,), (1,)), ((), ())), preferred_element_type=F32)


def dot_tn(a, b):
    return lax.dot_general(a, b, (((0,), (0,)), ((), ())), preferred_element_type=F32)


def sigmoid(v):
    return 0.5 * jnp.tanh(0.5 * v) + 0.5


def lane_iota(rows, lanes=128):
    return lax.broadcasted_iota(jnp.int32, (rows, lanes), 1)


def row_iota(rows, lanes=128):
    return lax.broadcasted_iota(jnp.int32, (rows, lanes), 0)


def parts_of(packed):
    high = packed.astype(BF16)
    rest = packed - high.astype(F32)
    middle = rest.astype(BF16)
    return jnp.concatenate([high, middle, (rest - middle.astype(F32)).astype(BF16)], axis=1)


def pick(first, rows, lanes, shift):
    row = jnp.bitwise_and(row_iota(rows, lanes), 127)
    head = lax.shift_right_logical(lane_iota(rows, lanes), shift)
    return jnp.where(row == first + head, 1.0, 0.0).astype(BF16)


def head_lanes(first, i):
    return pick(first + HB * i, 384, WB, 6)


def head_tiles(first, i):
    return pick(first + HB * i, 384, HB * 128, 7)


def widen(tiles):
    left = lane_iota(tiles.shape[0]) < P_SIZE
    tile = lambda h: tiles[:, h * 128 : (h + 1) * 128]
    return jnp.concatenate(
        [jnp.where(left, tile(2 * p), tile(2 * p + 1)) for p in range(HB // 2)], axis=1
    )


def halves(tile, axis_rows=True):
    left = lane_iota(tile.shape[0]) < P_SIZE
    zero = jnp.zeros_like(tile)
    return jnp.concatenate([jnp.where(left, tile, zero), jnp.where(left, zero, tile)], axis=0)


def head_rows(heads, i):
    lane = jnp.bitwise_and(lane_iota(16, 384), 127)
    sel = jnp.where(lane == L_CUM + HB * i + row_iota(16, 384), 1.0, 0.0).astype(BF16)
    return dot_nt(sel, heads)


def fill(ext, halo_ref, v_ref):
    ext[0:HALO, :] = halo_ref[...].astype(F32)
    ext[HALO:, :] = v_ref[...].astype(F32)


def conv_block(ext, taps_ref, shift_ref, c):
    total = shift_ref[0:1, :] + taps_ref[0:1, :] * ext[pl.ds(HALO - 3 + c * T, T), :]
    for k in range(1, 4):
        total = total + taps_ref[k : k + 1, :] * ext[pl.ds(HALO - 3 + k + c * T, T), :]
    return total


def state_kernel(
    v_ref, halo_ref, bc_ref, bchalo_ref, dt_ref, taps_ref, shift_ref, bctaps_ref, bcshift_ref,
    prm_ref, f_ref, tot_ref, x_ref, p_ref, p3_ref, b_ref, c_ref, bt_ref, ct_ref, ext, sumw,
    dtw, wxw,
):
    i = pl.program_id(0)
    blocks = v_ref.shape[0] // T

    @pl.when(i == 0)
    def _():
        fill(ext, bchalo_ref, bc_ref)
        lane = lane_iota(T)
        tril = (row_iota(T) >= lane).astype(F32)
        offset = jnp.zeros((1, 128), F32)
        for c in range(blocks):
            rows = pl.ds(c * T, T)
            conv = conv_block(ext, bctaps_ref, bcshift_ref, c)
            act = conv * sigmoid(conv)
            b_ref[rows, :] = act[:, :N].astype(BF16)
            c_ref[rows, :] = act[:, N:].astype(BF16)
            bt_ref[:, rows] = act[:, :N].T.astype(BF16)
            ct_ref[:, rows] = act[:, N:].T.astype(BF16)
            z = dt_ref[rows, :].astype(F32) + prm_ref[0:1, :]
            step = jnp.maximum(z, 0.0) + jnp.log1p(jnp.exp(-jnp.abs(z)))
            decay = step * prm_ref[1:2, :]
            cum = lax.dot_general(
                tril, decay, (((1,), (0,)), ((), ())),
                precision=lax.Precision.HIGHEST, preferred_element_type=F32,
            )
            cumf = cum + offset
            offset = cumf[T - 1 : T, :]
            packed = jnp.where(
                lane < L_CUM, step,
                jnp.where(lane < L_CUMF, cum, jnp.where(lane < L_SIG, cumf, 1.0 / (1.0 + jnp.exp(-z)))),
            )
            p_ref[rows, :] = packed
            p3_ref[rows, :] = parts_of(packed)

    fill(ext, halo_ref, v_ref)
    steps = head_lanes(L_STEP, i)
    sums = head_lanes(L_CUMF, i)
    heads = p3_ref[...]
    sumw[...] = dot(heads, sums)
    dtw[...] = dot(heads, steps)
    tot = sumw[blocks * T - 8 :, :][7:8, :]
    for c in range(blocks):
        rows = pl.ds(c * T, T)
        conv = conv_block(ext, taps_ref, shift_ref, c)
        x = conv * sigmoid(conv)
        x_ref[rows, :] = x
        wxw[rows, :] = (x * (jnp.exp(tot - sumw[rows, :]) * dtw[rows, :])).astype(BF16)
    f_ref[...] = dot(bt_ref[...], wxw[...]).astype(BF16)
    tot_ref[...] = jnp.broadcast_to(jnp.exp(tot), (8, WB))


def scan_kernel(
    x_ref, skip_ref, p3_ref, b_ref, c_ref, bt_ref, y_ref, cb, cumw, dtw,
):
    i = pl.program_id(0)
    blocks = x_ref.shape[0] // T

    @pl.when(i == 0)
    def _():
        causal = row_iota(T) >= lane_iota(T)
        for c in range(blocks):
            rows = pl.ds(c * T, T)
            cb[c] = jnp.where(causal, dot_nt(c_ref[rows, :], b_ref[rows, :]), 0.0)

    steps = head_lanes(L_STEP, i)
    sums = head_tiles(L_CUM, i)
    cumw[...] = dot(p3_ref[...], sums)
    dtw[...] = dot(p3_ref[...], steps)
    turned_all = head_rows(p3_ref[...], i)
    state = None
    for c in range(blocks):
        rows = pl.ds(c * T, T)
        x = x_ref[rows, :]
        cums = cumw[rows, :]
        turned = turned_all[:, c * T : (c + 1) * T]
        xd = x * dtw[rows, :]
        parts = []
        for p in range(HB // 2):
            weights = []
            for h in (2 * p, 2 * p + 1):
                across = turned[h : h + 1, :]
                e = jnp.exp(jnp.minimum(cums[:, h * 128 : (h + 1) * 128] - across, 0.0))
                weights.append((e * cb[c]).astype(BF16))
            parts.append(
                dot(
                    jnp.concatenate(weights, axis=1),
                    halves(xd[:, p * 128 : (p + 1) * 128]).astype(BF16),
                )
            )
        y = jnp.concatenate(parts, axis=1) + skip_ref[0:1, :] * x
        cumx = widen(cums)
        if state is not None:
            y = y + jnp.exp(cumx) * dot(c_ref[rows, :], state.astype(BF16))
        y_ref[rows, :] = y
        if c < blocks - 1:
            tot = cumx[T - 1 : T, :]
            fresh = dot(bt_ref[:, rows], (jnp.exp(tot - cumx) * xd).astype(BF16))
            state = fresh if state is None else state * jnp.exp(tot) + fresh


def grow_factors(p_ref, sel):
    lane = lane_iota(p_ref.shape[0])
    inside = jnp.logical_and(lane >= L_CUMF, lane < L_SIG)
    grow = jnp.where(inside, jnp.exp(jnp.where(inside, p_ref[...], 0.0)), 0.0)
    high = grow.astype(BF16)
    low = (grow - high.astype(F32)).astype(BF16)
    return dot(jnp.concatenate([high, low], axis=1), sel[...])


def gate_kernel(y_ref, gate_ref, p_ref, c_ref, s_ref, gain_ref, out_y_ref, out_ref, sel):
    @pl.when(pl.program_id(0) == 0)
    def _():
        sel[...] = pick(L_CUMF, 256, DI, 6)

    grow = grow_factors(p_ref, sel)
    y = y_ref[...] + grow * dot(c_ref[...], s_ref[...])
    out_y_ref[...] = y
    mixed = y.astype(BF16).astype(F32)
    gate = gate_ref[...]
    gated = mixed * (gate * sigmoid(gate))
    r = lax.rsqrt(jnp.mean(gated * gated, axis=1, keepdims=True) + EPS)
    out_ref[...] = (gated * r * gain_ref[0:1, :]).astype(BF16)


def gate_back_kernel(
    y_ref, gate_ref, dgn_ref, p_ref, ct_ref, gain_ref, dgate_ref, dmix_ref, gg_ref, g_ref, acc,
    sel,
):
    i = pl.program_id(0)

    @pl.when(i == 0)
    def _():
        sel[...] = pick(L_CUMF, 256, DI, 6)
        acc[...] = jnp.zeros_like(acc)
        gg_ref[...] = jnp.zeros_like(gg_ref)

    mixed = y_ref[...].astype(BF16).astype(F32)
    gate = gate_ref[...]
    sig = sigmoid(gate)
    silu = gate * sig
    gated = mixed * silu
    r = lax.rsqrt(jnp.mean(gated * gated, axis=1, keepdims=True) + EPS)
    q = gated * r
    dgn = dgn_ref[...]
    gg_ref[...] += jnp.broadcast_to(jnp.sum(dgn * q, axis=0, keepdims=True), gg_ref.shape)
    dq = dgn * gain_ref[0:1, :]
    dgated = r * (dq - q * jnp.mean(dq * q, axis=1, keepdims=True))
    dgate_ref[...] = (dgated * mixed * (sig * (1.0 + gate * (1.0 - sig)))).astype(BF16)
    dmix = (dgated * silu).astype(BF16)
    dmix_ref[...] = dmix
    grow = grow_factors(p_ref, sel)
    acc[...] += dot(ct_ref[...], (grow * dmix.astype(F32)).astype(BF16))

    @pl.when(i == pl.num_programs(0) - 1)
    def _():
        g_ref[...] = acc[...].astype(BF16)


def conv_back(ext, dext, taps_ref, dv_ref, tail_ref, head_ref, stats_ref, blocks):
    early = dext[0:8, :]
    before = ext[HALO - 8 : HALO, :]
    sums = []
    for k in range(5):
        sums.append(jnp.zeros((1, WB), F32))
        for j in range(3 - k):
            sums[k] = sums[k] + early[j : j + 1, :] * before[5 + k + j : 6 + k + j, :]
    for c in range(blocks):
        v = ext[pl.ds(HALO + c * T, T), :]
        total = None
        for k in (3, 2, 1, 0):
            d = dext[pl.ds(c * T + 3 - k, T), :]
            total = taps_ref[k : k + 1, :] * d if total is None else total + taps_ref[k : k + 1, :] * d
            sums[k] = sums[k] + jnp.sum(d * v, axis=0, keepdims=True)
            if k == 3:
                sums[4] = sums[4] + jnp.sum(d, axis=0, keepdims=True)
        dv_ref[pl.ds(c * T, T), :] = total.astype(BF16)
        if c == blocks - 1:
            tail_ref[...] = total[T - 8 :, :]
    head_ref[...] = dext[0:8, :]
    for k in range(5):
        stats_ref[k : k + 1, :] = sums[k]


def back_inside_kernel(
    x_ref, p3_ref, b_ref, c_ref, dy_ref, dxd_ref, dcbt_ref, cbt, cumw, dtw, first,
):
    i = pl.program_id(0) + first
    blocks = x_ref.shape[0] // T

    @pl.when(pl.program_id(0) == 0)
    def _():
        causal = row_iota(T) <= lane_iota(T)
        for c in range(blocks):
            rows = pl.ds(c * T, T)
            cbt[c] = jnp.where(causal, dot_nt(b_ref[rows, :], c_ref[rows, :]), 0.0)
        dcbt_ref[...] = jnp.zeros_like(dcbt_ref)

    steps = head_lanes(L_STEP, i)
    sums = head_tiles(L_CUM, i)
    cumw[...] = dot(p3_ref[...], sums)
    dtw[...] = dot(p3_ref[...], steps)
    turned_all = head_rows(p3_ref[...], i)
    for c in range(blocks):
        rows = pl.ds(c * T, T)
        cums = cumw[rows, :]
        turned = turned_all[:, c * T : (c + 1) * T]
        xd = x_ref[rows, :] * dtw[rows, :]
        dyb = dy_ref[rows, :]
        dy = dyb.astype(F32)
        dcb = jnp.zeros((T, T), F32)
        for p in range(HB // 2):
            lanes = slice(p * 128, (p + 1) * 128)
            dm = dot_nt(halves(xd[:, lanes]).astype(BF16), dyb[:, lanes])
            weights = []
            for j in range(2):
                h = 2 * p + j
                across = turned[h : h + 1, :]
                e = jnp.exp(jnp.minimum(across - cums[:, h * 128 : (h + 1) * 128], 0.0))
                weights.append((e * cbt[c]).astype(BF16))
                dcb = dcb + dm[j * T : (j + 1) * T, :] * e
            dxd_ref[rows, lanes] = dot(
                jnp.concatenate(weights, axis=1), halves(dy[:, lanes]).astype(BF16)
            )
        dcbt_ref[c] += dcb


def back_kernel(
    v_ref, halo_ref, bc_ref, bchalo_ref, taps_ref, shift_ref, bctaps_ref, bcshift_ref, skip_ref,
    prm_ref, p_ref, p3_ref, b_ref, c_ref, bt_ref, ct_ref, s_ref, gin_ref, dy_ref, y_ref,
    inside_low_ref, inside_high_ref, low_ref, high_ref,
    dv_ref, tail_ref, head_ref, stats_ref, bdv_ref, btail_ref, bhead_ref, bstats_ref,
    ddt_ref, dtstats_ref,
    ext, dext, convs, sigs, cumw, dtw, prods, acc, dbacc, dcacc,
):
    i = pl.program_id(0)
    blocks = v_ref.shape[0] // T
    length = blocks * T

    @pl.when(i == 0)
    def _():
        acc[...] = jnp.zeros_like(acc)
        dbacc[...] = jnp.zeros_like(dbacc)
        dcacc[...] = jnp.zeros_like(dcacc)

    fill(ext, halo_ref, v_ref)
    dext[length:, :] = jnp.zeros((8, WB), F32)
    steps = head_lanes(L_STEP, i)
    sums = head_lanes(L_CUM, i)
    cumw[...] = dot(p3_ref[...], sums)
    dtw[...] = dot(p3_ref[...], steps)
    states = [s_ref[...].astype(F32)]
    for c in range(blocks):
        rows = pl.ds(c * T, T)
        conv = conv_block(ext, taps_ref, shift_ref, c)
        sig = sigmoid(conv)
        convs[rows, :] = conv
        sigs[rows, :] = sig
        cumx, dt = cumw[rows, :], dtw[rows, :]
        tot = cumx[T - 1 : T, :]
        wx = (jnp.exp(tot - cumx) * (conv * sig * dt)).astype(BF16)
        states.append(states[-1] * jnp.exp(tot) + dot(bt_ref[:, rows], wx))

    ch = lax.shift_right_logical(row_iota(WB), 6)
    seg1 = (lane_iota(WB) == HB * i + ch).astype(BF16)
    seg2 = (lane_iota(WB) == 32 + HB * i + ch).astype(BF16)
    final = row_iota(T, WB) == T - 1
    lower = jnp.full((T, WB), i, jnp.int32) < STEPS // 2
    grad = gin_ref[...].astype(F32)
    skip_sum = jnp.zeros((1, WB), F32)
    for c in reversed(range(blocks)):
        rows = pl.ds(c * T, T)
        conv, sig = convs[rows, :], sigs[rows, :]
        x = conv * sig
        cumx, dt = cumw[rows, :], dtw[rows, :]
        tot = cumx[T - 1 : T, :]
        xd = x * dt
        xdb = xd.astype(BF16)
        dyb = dy_ref[rows, :]
        dy = dyb.astype(F32)
        gb = grad.astype(BF16)
        w = jnp.exp(tot - cumx)
        inside = jnp.where(lower, inside_low_ref[rows, :], inside_high_ref[rows, :])
        dxd = inside + w * dot(b_ref[rows, :], gb)
        ey = (jnp.exp(cumx) * dy).astype(BF16)
        wx = (w * xd).astype(BF16)
        dcacc[rows, :] += dot_nt(ey, states[c].astype(BF16))
        dbacc[rows, :] += dot_nt(wx, gb)
        bound = jnp.sum(grad * states[c + 1], axis=0, keepdims=True)
        skip = skip_ref[0:1, :]
        p1 = dy * (y_ref[rows, :] - skip * x) - xdb.astype(F32) * dxd
        p1 = p1 + jnp.where(final, bound, 0.0)
        p2 = x * dxd
        p1h = p1.astype(BF16)
        p2h = p2.astype(BF16)
        sides = (p1h, (p1 - p1h.astype(F32)).astype(BF16), p2h, (p2 - p2h.astype(F32)).astype(BF16))
        for k, side in enumerate(sides):
            prods[rows, k * WB : (k + 1) * WB] = side
        skip_sum = skip_sum + jnp.sum(x * dy, axis=0, keepdims=True)
        dx = dt * dxd + skip * dy
        dext[rows, :] = dx * (sig * (1.0 + conv * (1.0 - sig)))
        grad = grad * jnp.exp(tot) + dot(ct_ref[:, rows], ey)
    acc[...] += dot(prods[...], jnp.concatenate([seg1, seg1, seg2, seg2], axis=0))
    conv_back(ext, dext, taps_ref, dv_ref, tail_ref, head_ref, stats_ref, blocks)
    stats_ref[5:6, :] = skip_sum

    @pl.when(i == pl.num_programs(0) - 1)
    def _():
        fill(ext, bchalo_ref, bc_ref)
        triu = (row_iota(T) <= lane_iota(T)).astype(F32)
        rate = prm_ref[1:2, :]
        rate_sum = jnp.zeros((1, 128), F32)
        bias_sum = jnp.zeros((1, 128), F32)
        for c in range(blocks):
            rows = pl.ds(c * T, T)
            causal = row_iota(T) <= lane_iota(T)
            m = jnp.where(causal, low_ref[c] + high_ref[c], 0.0).astype(BF16)
            db = dbacc[rows, :] + dot(m, c_ref[rows, :])
            dc = dcacc[rows, :] + dot_tn(m, b_ref[rows, :])
            conv = conv_block(ext, bctaps_ref, bcshift_ref, c)
            sig = sigmoid(conv)
            dext[rows, :] = jnp.concatenate([db, dc], axis=1) * (
                sig * (1.0 + conv * (1.0 - sig))
            )
            a = acc[rows, :]
            ddecay = lax.dot_general(
                triu, a, (((1,), (0,)), ((), ())),
                precision=lax.Precision.HIGHEST, preferred_element_type=F32,
            )
            packed = p_ref[rows, :]
            rate_sum = rate_sum + jnp.sum(packed * ddecay, axis=0, keepdims=True)
            dz = (pltpu.roll(a, 96, 1) + rate * ddecay) * pltpu.roll(packed, 32, 1)
            ddt_ref[rows, :] = jnp.where(lane_iota(T) < H, dz, 0.0).astype(BF16)
            bias_sum = bias_sum + jnp.sum(dz, axis=0, keepdims=True)
        conv_back(ext, dext, bctaps_ref, bdv_ref, btail_ref, bhead_ref, bstats_ref, blocks)
        dtstats_ref[0:1, :] = rate_sum * rate
        dtstats_ref[1:2, :] = bias_sum


def whole(shape):
    return pl.BlockSpec(shape, lambda i: (0,) * len(shape))


def wide(rows):
    return pl.BlockSpec((rows, WB), lambda i: (0, i))


def bc_block(rows):
    return pl.BlockSpec((rows, WB), lambda i: (0, STEPS))


def shape_of(shape, dtype):
    return jax.ShapeDtypeStruct(shape, dtype)


def params():
    return pltpu.CompilerParams(vmem_limit_bytes=VMEM_LIMIT)


def cost(flops, moved):
    return pl.CostEstimate(flops=int(flops), bytes_accessed=int(moved), transcendentals=0)


def local_state(r_low, halo, taps, shift, prm):
    length = r_low.shape[0]
    return pl.pallas_call(
        state_kernel,
        name="local_state",
        grid=(STEPS,),
        in_specs=[
            wide(length), wide(HALO), bc_block(length), bc_block(HALO),
            pl.BlockSpec((length, 128), lambda i: (0, CC // 128)),
            wide(4), wide(1), bc_block(4), bc_block(1), whole((8, 128)),
        ],
        out_specs=[
            wide(N), wide(8), wide(length), whole((length, 128)), whole((length, 384)),
            whole((length, N)), whole((length, N)), whole((N, length)), whole((N, length)),
        ],
        out_shape=[
            shape_of((N, DI), BF16), shape_of((8, DI), F32), shape_of((length, DI), F32),
            shape_of((length, 128), F32), shape_of((length, 384), BF16),
            shape_of((length, N), BF16), shape_of((length, N), BF16),
            shape_of((N, length), BF16), shape_of((N, length), BF16),
        ],
        scratch_shapes=[
            pltpu.VMEM((HALO + length, WB), F32), pltpu.VMEM((length, WB), F32),
            pltpu.VMEM((length, WB), F32), pltpu.VMEM((length, WB), BF16),
        ],
        compiler_params=params(),
        cost_estimate=cost(4e9, 8e6),
    )(r_low, halo, r_low, halo, r_low, taps, shift, taps, shift, prm)


def local_scan(x, skip, p3, b, c, bt):
    length = x.shape[0]
    return pl.pallas_call(
        scan_kernel,
        name="local_scan",
        grid=(STEPS,),
        in_specs=[
            wide(length), wide(1), whole((length, 384)),
            whole((length, N)), whole((length, N)), whole((N, length)),
        ],
        out_specs=wide(length),
        out_shape=shape_of((length, DI), F32),
        scratch_shapes=[
            pltpu.VMEM((length // T, T, T), F32), pltpu.VMEM((length, HB * 128), F32),
            pltpu.VMEM((length, WB), F32),
        ],
        compiler_params=params(),
        cost_estimate=cost(1.5e10, 8e6),
    )(x, skip, p3, b, c, bt)


def gate_forward(y, gate, p, c, s_in, gain):
    length = y.shape[0]
    rows = lambda width: pl.BlockSpec((T, width), lambda i: (i, 0))
    return pl.pallas_call(
        gate_kernel,
        name="gate_forward",
        grid=(length // T,),
        in_specs=[rows(DI), rows(DI), rows(128), rows(N), whole((N, DI)), whole((1, DI))],
        out_specs=[rows(DI), rows(DI)],
        out_shape=[shape_of((length, DI), F32), shape_of((length, DI), BF16)],
        scratch_shapes=[pltpu.VMEM((256, DI), BF16)],
        compiler_params=params(),
        cost_estimate=cost(5e9, 15e6),
    )(y, gate, p, c, s_in, gain)


def gate_backward(y, gate, dgn, p, ct, gain):
    length = y.shape[0]
    rows = lambda width: pl.BlockSpec((T, width), lambda i: (i, 0))
    return pl.pallas_call(
        gate_back_kernel,
        name="gate_backward",
        grid=(length // T,),
        in_specs=[
            rows(DI), rows(DI), rows(DI), rows(128),
            pl.BlockSpec((N, T), lambda i: (0, i)), whole((1, DI)),
        ],
        out_specs=[rows(DI), rows(DI), whole((8, DI)), whole((N, DI))],
        out_shape=[
            shape_of((length, DI), BF16), shape_of((length, DI), BF16),
            shape_of((8, DI), F32), shape_of((N, DI), BF16),
        ],
        scratch_shapes=[pltpu.VMEM((N, DI), F32), pltpu.VMEM((256, DI), BF16)],
        compiler_params=params(),
        cost_estimate=cost(1e10, 17e6),
    )(y, gate, dgn, p, ct, gain)


def scan_inside(x, p3, b, c, dy, first):
    length = x.shape[0]
    blocks = length // T
    wide_from = lambda rows: pl.BlockSpec((rows, WB), lambda i: (0, i + first))
    return pl.pallas_call(
        functools.partial(back_inside_kernel, first=first),
        name="scan_inside",
        grid=(STEPS // 2,),
        in_specs=[
            wide_from(length), whole((length, 384)), whole((length, N)),
            whole((length, N)), wide_from(length),
        ],
        out_specs=[wide(length), whole((blocks, T, T))],
        out_shape=[shape_of((length, DI // 2), F32), shape_of((blocks, T, T), F32)],
        scratch_shapes=[
            pltpu.VMEM((blocks, T, T), F32), pltpu.VMEM((length, HB * 128), F32),
            pltpu.VMEM((length, WB), F32),
        ],
        compiler_params=params(),
        cost_estimate=cost(1e10, 6e6),
    )(x, p3, b, c, dy)


def scan_backward(
    r_low, halo, taps, shift, skip, prm, p, p3, b, c, bt, ct, s_in, g_in, dy, y, low, high
):
    length = r_low.shape[0]
    blocks = length // T
    return pl.pallas_call(
        back_kernel,
        name="scan_backward",
        grid=(STEPS,),
        in_specs=[
            wide(length), wide(HALO), bc_block(length), bc_block(HALO),
            wide(4), wide(1), bc_block(4), bc_block(1), wide(1), whole((8, 128)),
            whole((length, 128)), whole((length, 384)), whole((length, N)), whole((length, N)),
            whole((N, length)), whole((N, length)), wide(N), wide(N), wide(length), wide(length),
            pl.BlockSpec((length, WB), lambda i: (0, jnp.minimum(i, STEPS // 2 - 1))),
            pl.BlockSpec((length, WB), lambda i: (0, jnp.maximum(i - STEPS // 2, 0))),
            whole((blocks, T, T)), whole((blocks, T, T)),
        ],
        out_specs=[
            wide(length), wide(8), wide(8), wide(8),
            whole((length, WB)), whole((8, WB)), whole((8, WB)), whole((8, WB)),
            whole((length, 128)), whole((8, 128)),
        ],
        out_shape=[
            shape_of((length, DI), BF16), shape_of((8, DI), F32), shape_of((8, DI), F32),
            shape_of((8, DI), F32),
            shape_of((length, WB), BF16), shape_of((8, WB), F32), shape_of((8, WB), F32),
            shape_of((8, WB), F32),
            shape_of((length, 128), BF16), shape_of((8, 128), F32),
        ],
        scratch_shapes=[
            pltpu.VMEM((HALO + length, WB), F32),
            pltpu.VMEM((length + 8, WB), F32),
            pltpu.VMEM((length, WB), F32),
            pltpu.VMEM((length, WB), F32),
            pltpu.VMEM((length, WB), F32),
            pltpu.VMEM((length, WB), F32),
            pltpu.VMEM((length, 4 * WB), BF16),
            pltpu.VMEM((length, 128), F32),
            pltpu.VMEM((length, 128), F32),
            pltpu.VMEM((length, 128), F32),
        ],
        compiler_params=params(),
        cost_estimate=cost(3e10, 16e6),
    )(
        r_low, halo, r_low, halo, taps, shift, taps, shift, skip, prm, p, p3, b, c, bt, ct,
        s_in, g_in, dy, y, low[0], high[0], low[1], high[1],
    )


def add(a, b):
    return (a.astype(F32) + b.astype(F32)).astype(BF16)


def swap(a, axis, bit):
    return lax.ppermute(a, axis, [(k, k ^ bit) for k in range(lax.axis_size(axis))])


def hop_to(message, state, hop, upward):
    last = lax.axis_size("seq") - 1
    pair = (hop, hop + 1) if upward else (last - hop, last - hop - 1)
    got = lax.ppermute(message, "seq", [pair])
    return got if state is None else got + state


def message_of(local, decay, state):
    return (local.astype(F32) + decay * state.astype(F32)).astype(BF16)


def pass_along(local, decay, upward, work):
    hops = lax.axis_size("seq") - 1
    state = None
    done = []
    for hop in range(hops):
        message = local if hop == 0 else message_of(local, decay, state)
        state = hop_to(message, state, hop, upward)
        if work:
            item = work[0]()
            work = work[1:]
            state, item = lax.optimization_barrier((state, item))
            done.append(item)
    for item in work:
        done.append(item())
    return state, done


def pieces_kernel(order_ref, left_ref, base_ref, *refs):
    del order_ref
    for m, piece in enumerate(refs[:-1]):

        @pl.when(pl.program_id(0) == m)
        def _(m=m, piece=piece):
            total = base_ref[...] if m == 0 else refs[-1][...]
            refs[-1][...] = total + dot(left_ref[...], piece[...])


def pieces_back_kernel(order_ref, left_ref, *refs):
    del order_ref
    for m, piece in enumerate(refs[:-1]):

        @pl.when(pl.program_id(0) == m)
        def _(piece=piece):
            refs[-1][...] = dot_nt(left_ref[...], piece[...])


def xor_order():
    n = lax.axis_size("fsdp")
    return jnp.bitwise_xor(lax.axis_index("fsdp"), jnp.arange(n)).astype(jnp.int32)


def fixed(shape):
    return pl.BlockSpec(shape, lambda i, order: (0,) * len(shape))


def add_product(base, left, w):
    if not isinstance(w, list):
        return base + dot(left, w)
    return pl.pallas_call(
        pieces_kernel,
        name="add_product",
        grid_spec=pltpu.PrefetchScalarGridSpec(
            num_scalar_prefetch=1,
            grid=(len(w),),
            in_specs=[
                pl.BlockSpec((left.shape[0], w[0].shape[0]), lambda i, order: (0, order[i])),
                fixed(base.shape),
            ]
            + [fixed(w[0].shape)] * len(w),
            out_specs=fixed(base.shape),
        ),
        out_shape=shape_of(base.shape, F32),
        compiler_params=params(),
        cost_estimate=cost(2e9, 10e6),
    )(xor_order(), left, base, *w)


def product_back(left, w):
    if not isinstance(w, list):
        return dot_nt(left, w)
    length = left.shape[0]
    return pl.pallas_call(
        pieces_back_kernel,
        name="product_back",
        grid_spec=pltpu.PrefetchScalarGridSpec(
            num_scalar_prefetch=1,
            grid=(len(w),),
            in_specs=[fixed(left.shape)] + [fixed(w[0].shape)] * len(w),
            out_specs=pl.BlockSpec((length, w[0].shape[0]), lambda i, order: (0, order[i])),
        ),
        out_shape=shape_of((length, len(w) * w[0].shape[0]), F32),
        compiler_params=params(),
        cost_estimate=cost(2e9, 10e6),
    )(xor_order(), left, *w)


def give_kernel(left_ref, right_ref, out_ref):
    out_ref[...] = dot_tn(left_ref[...], right_ref[...]).astype(BF16)


def own_kernel(left_ref, right_ref, got_ref, *out_refs):
    value = dot_tn(left_ref[...], right_ref[...]) + got_ref[...].astype(F32)
    rows = out_refs[0].shape[0]
    for d, out_ref in enumerate(out_refs):
        out_ref[...] = value[d * rows : (d + 1) * rows].astype(BF16)


def shard_columns(left, core):
    n = lax.axis_size("fsdp")
    me = lax.axis_index("fsdp")
    width = left.shape[1] // n
    return jnp.concatenate(
        [
            lax.dynamic_slice_in_dim(left, jnp.bitwise_xor(me, 2 * d + core) * width, width, 1)
            for d in range(n // 2)
        ],
        axis=1,
    )


def product_give(left, right):
    length, rows = left.shape
    columns = right.shape[1]
    block = columns // 2 if columns % 256 == 0 else columns
    return pl.pallas_call(
        give_kernel,
        name="product_give",
        grid=(columns // block,),
        in_specs=[whole((length, rows)), pl.BlockSpec((length, block), lambda i: (0, i))],
        out_specs=pl.BlockSpec((rows, block), lambda i: (0, i)),
        out_shape=shape_of((rows, columns), BF16),
        compiler_params=params(),
        cost_estimate=cost(3e9, 8e6),
    )(left, right)


def product_own(left, right, got):
    chips = lax.axis_size("fsdp") // 2
    length, rows = left.shape
    columns = right.shape[1]
    block = columns // 2 if columns % 256 == 0 else columns
    blocks = lambda height: pl.BlockSpec((height, block), lambda i: (0, i))
    return pl.pallas_call(
        own_kernel,
        name="product_own",
        grid=(columns // block,),
        in_specs=[whole((length, rows)), blocks(length), blocks(rows)],
        out_specs=[blocks(rows // chips)] * chips,
        out_shape=[shape_of((rows // chips, columns), BF16)] * chips,
        compiler_params=params(),
        cost_estimate=cost(3e9, 10e6),
    )(left, right, got)


def send_chips(parts):
    return parts[0], [swap(part, "fsdp", 2 * d) for d, part in enumerate(parts) if d]


def gather_sum(own, got):
    total = own.astype(F32)
    for piece in got:
        total = total + piece.astype(F32)
    return total.astype(BF16)


def tie(*values):
    return lax.optimization_barrier(values)


def seq_first(a):
    odd = lax.axis_index("seq") % 2
    half = a.shape[0] // 2
    keep = lax.dynamic_slice_in_dim(a, odd * half, half, 0)
    give = lax.dynamic_slice_in_dim(a, (1 - odd) * half, half, 0)
    return keep, swap(give, "seq", 1)


def seq_across(keep, got):
    keep = add(keep, got)
    bit = 2
    while 2 * bit < lax.axis_size("seq"):
        keep = add(keep, swap(keep, "seq", bit))
        bit *= 2
    return keep, swap(keep, "seq", bit)


def seq_back(keep, got):
    keep = add(keep, got)
    return keep, swap(keep, "seq", 1)


def seq_join(keep, other):
    odd = lax.axis_index("seq") % 2
    return jnp.where(
        odd == 0, jnp.concatenate([keep, other]), jnp.concatenate([other, keep])
    )


def sum_over(a, *axes):
    for axis in axes:
        bit = 1
        while bit < lax.axis_size(axis):
            a = a + swap(a, axis, bit)
            bit *= 2
    return a


def turn_kernel(*refs):
    out_ref = refs[-1]
    for k in range(len(refs) // 2):
        row = 0
        for ref in refs[2 * k : 2 * k + 2]:
            for j in range(0, ref.shape[1], 128):
                rows = min(128, out_ref.shape[1] - row)
                tile = ref[:, j : j + 128].astype(F32).T
                out_ref[k, row : row + rows, :] = tile[:rows, :]
                row += rows


def in_weight_rows(pieces, in_width):
    flat = [piece for pair in pieces for piece in pair]
    return pl.pallas_call(
        turn_kernel,
        name="in_weight_rows",
        out_shape=shape_of((len(pieces), in_width, flat[0].shape[0]), F32),
        compiler_params=params(),
        cost_estimate=cost(0, 7e6),
    )(*flat)


def on_device(
    hidden_in, cotangent, norm_gain, input_projection_weight, conv_weight, conv_bias, dt_bias,
    a_log, skip, gate_gain, output_projection_weight,
):
    layers, _, in_width = input_projection_weight.shape
    seq_parts = lax.axis_size("seq")
    up = [(z, z + 1) for z in range(seq_parts - 1)]
    down = [(z + 1, z) for z in range(seq_parts - 1)]

    small = [norm_gain, conv_weight, conv_bias, dt_bias, a_log, skip, gate_gain]
    flat = jnp.concatenate([a.reshape(layers, -1) for a in small], axis=1)
    shards = lax.axis_size("fsdp")
    packed = lax.all_gather(flat, "fsdp", axis=0)
    packed = packed.astype(F32)
    unpacked = []
    start = 0
    for a in small:
        width = a[0].size
        piece = packed[:, :, start : start + width].reshape((shards,) + a.shape)
        start += width
        piece = jnp.moveaxis(piece, 0, -2)
        unpacked.append(piece.reshape(a.shape[:-1] + (shards * a.shape[-1],)))
    gains, taps_all, shift_all, bias_all, rate_all, skip_all, gate_all = unpacked

    by_pieces = output_projection_weight.shape[1] % 128 == 0
    weights = []
    for layer in range(layers):
        w = input_projection_weight[layer]
        rest = jnp.concatenate([w[:, DI : DI + CC]] + [w[:, DI + CC :]] * 4, axis=1)
        rest = lax.all_gather(rest, "fsdp", axis=0, tiled=True)
        if layer == 0:
            rest, first_out = tie(rest, output_projection_weight[0])
            if by_pieces:
                near = swap(first_out, "fsdp", 1)
                arrived = [swap(first_out, "fsdp", 2 * d) for d in range(1, shards // 2)]
        weights.append(
            (
                rest,
                lax.all_gather(w[:, :DI], "fsdp", axis=0, tiled=True),
                None
                if layer == 0 and by_pieces
                else lax.all_gather(output_projection_weight[layer], "fsdp", axis=0, tiled=True),
            )
        )

    hidden = hidden_in[0].astype(F32)
    stored = []
    for layer in range(layers):
        w_rest, w_gate, w_out = weights[layer]
        r_in = lax.rsqrt(jnp.mean(hidden * hidden, axis=1, keepdims=True) + EPS)
        normed = (hidden * r_in * gains[layer][None, :]).astype(BF16)
        r_low = dot(normed, w_rest).astype(BF16)
        halo = lax.ppermute(r_low[-HALO:, :CC], "seq", up)
        taps = taps_all[layer]
        shift = shift_all[layer][None, :]
        skip_wide = jnp.repeat(skip_all[layer], P_SIZE)[None, :]
        prm = jnp.zeros((8, 128), F32)
        prm = prm.at[0].set(jnp.tile(bias_all[layer], 4))
        prm = prm.at[1].set(jnp.tile(-jnp.exp(rate_all[layer]), 4))
        f, decay, x, p, p3, b, c, bt, ct = local_state(r_low, halo, taps, shift, prm)
        state = hop_to(f, None, 0, True)
        y = local_scan(x, skip_wide, p3, b, c, bt)
        state, y = tie(state, y)
        if w_out is None:
            y, arrived = tie(y, arrived)
            swapped = [swap(piece, "fsdp", 1) for piece in arrived]
        for hop in range(1, seq_parts - 1):
            state = hop_to(message_of(f, decay[0:1], state), state, hop, True)
            if hop == 1:
                gate = dot(normed, w_gate)
                state, gate = tie(state, gate)
                if w_out is None:
                    gate, swapped = tie(gate, swapped)
                    w_out = [first_out, near]
                    for pair in zip(arrived, swapped):
                        w_out += pair
                    weights[layer] = (w_rest, w_gate, w_out)
        s_in = state
        y, gate_low = gate_forward(y, gate, p, c, s_in, gate_all[layer][None, :])
        stored.append(
            (
                hidden, r_in, normed, r_low, halo, gate, taps, shift, skip_wide, prm, decay, x, p,
                p3, b, c, bt, ct, s_in, y, gate_low,
            )
        )
        hidden = add_product(hidden, gate_low, w_out)
    block_out = hidden.astype(BF16)[None]

    block_out, cotangent = tie(block_out, cotangent)
    grad = cotangent[0].astype(F32)
    big = [None] * layers
    vectors = [None] * layers
    waiting = None
    for layer in reversed(range(layers)):
        (
            hidden, r_in, normed, r_low, halo, gate, taps, shift, skip_wide, prm, decay, x, p,
            p3, b, c, bt, ct, s_in, y, gate_low,
        ) = stored[layer]
        w_rest, w_gate, w_out = weights[layer]
        d_branch = grad.astype(BF16)
        dgn = product_back(d_branch, w_out)
        dgate, dmix, gain_out_grad, g_local = gate_backward(
            y, gate, dgn, p, ct, gate_all[layer][None, :]
        )

        if waiting is not None:
            scattered, g_local = tie(scattered, g_local)
            big[layer + 1] = [lax.psum(a, "seq") for a in scattered]

        normed_give, normed_own = shard_columns(normed, 1), shard_columns(normed, 0)
        inside = lambda first: scan_inside(x, p3, b, c, dmix, first)
        if layer == 0:
            out_give = product_give(shard_columns(gate_low, 1), d_branch)
            state = hop_to(g_local, None, 0, False)
            low = inside(0)
            state, out_give, low, rest_sent = tie(state, out_give, low, rest_sent)
            above = seq_first(gather_sum(rest_mine, rest_sent))
            for hop in range(1, seq_parts - 1):
                state = hop_to(message_of(g_local, decay[0:1], state), state, hop, False)
                if hop == 1:
                    out_got = swap(out_give, "fsdp", 1)
                    gate_give = product_give(normed_give, dgate)
                    high = inside(STEPS // 2)
                    state, out_got, gate_give, high, above = tie(
                        state, out_got, gate_give, high, above
                    )
                    above = seq_across(*above)
                    gate_got = swap(gate_give, "fsdp", 1)
                    out_parts = product_own(shard_columns(gate_low, 0), d_branch, out_got)
                elif hop == 2:
                    out_parts, state = tie(out_parts, state)
                    out_mine, out_sent = send_chips(out_parts)
                    state, gate_got, above = tie(state, gate_got, above)
                    above = seq_back(*above)
                    gate_parts = product_own(normed_own, dgate, gate_got)
                    state, gate_parts = tie(state, gate_parts)
                    gate_mine, gate_sent = send_chips(gate_parts)
        else:
            state, ((out_grad, gate_w_grad), low, high) = pass_along(
                g_local,
                decay[0:1],
                False,
                [
                    lambda: (
                        dot_tn(gate_low, d_branch).astype(BF16),
                        dot_tn(normed, dgate).astype(BF16),
                    ),
                    lambda: inside(0),
                    lambda: inside(STEPS // 2),
                ],
            )
            scattered = [
                lax.psum_scatter(a, "fsdp", scatter_dimension=0, tiled=True)
                for a in (out_grad, gate_w_grad)
            ]
        back = scan_backward(
            r_low, halo, taps, shift, skip_wide, prm, p, p3, b, c, bt, ct, s_in, state, dmix, y,
            low, high,
        )
        if layer == 0:
            back, out_sent, above, big[layer + 1] = tie(back, out_sent, above, big[layer + 1])
            big[layer + 1].append(seq_join(*above))
            out_seq = seq_first(gather_sum(out_mine, out_sent))
        dv, tail, head, stats, bdv, btail, bhead, bstats, ddt, dtstats = back
        heads_in = lax.ppermute(jnp.concatenate([head, bhead], axis=1), "seq", down)
        tail = jnp.concatenate([tail, btail], axis=1)
        fix = [tail[j : j + 1] for j in range(8)]
        for j in range(3):
            for k in range(j + 1):
                fix[5 + j] = fix[5 + j] + taps[k : k + 1] * heads_in[j - k : j - k + 1]
        d_rest = jnp.concatenate([dv, bdv, ddt], axis=1)
        d_rest = lax.dynamic_update_slice(
            d_rest, jnp.concatenate(fix, axis=0).astype(BF16), (d_rest.shape[0] - 8, 0)
        )
        got = swap(product_give(normed_give, d_rest), "fsdp", 1)
        d_normed = dot_nt(dgate, w_gate)
        got, d_normed = tie(got, d_normed)
        if layer == 0:
            out_seq, d_rest = tie(out_seq, d_rest)
            out_seq = seq_across(*out_seq)
        else:
            parts = product_own(normed_own, d_rest, got)
            parts, d_rest = tie(parts, d_rest)
            rest_mine, rest_sent = send_chips(parts)
        d_normed = d_normed + dot_nt(d_rest, w_rest)
        q = hidden * r_in
        dq = d_normed * gains[layer][None, :]
        gain_in_grad = jnp.sum(d_normed * q, axis=0)
        grad = grad + r_in * (dq - q * jnp.mean(dq * q, axis=1, keepdims=True))
        if layer == 0:
            grad, gain_in_grad, got = tie(grad, gain_in_grad, got)
            parts = product_own(normed_own, d_rest, got)
            parts, gate_sent = tie(parts, gate_sent)
            rest_mine, rest_sent = send_chips(parts)
            gate_seq = seq_first(gather_sum(gate_mine, gate_sent))
            out_seq, gate_seq = tie(out_seq, gate_seq)
            out_seq = seq_back(*out_seq)
            gate_seq = seq_across(*gate_seq)
            out_seq, gate_seq, rest_sent = tie(out_seq, gate_seq, rest_sent)
            rest_seq = seq_first(gather_sum(rest_mine, rest_sent))
            gate_seq = seq_back(*gate_seq)
            rest_seq = seq_back(*seq_across(*rest_seq))
            big[layer] = [seq_join(*out_seq), seq_join(*gate_seq), seq_join(*rest_seq)]
        waiting = layer
        stats = jnp.concatenate([stats, bstats], axis=1)
        vectors[layer] = [
            gain_in_grad,
            stats[0:4],
            stats[4],
            dtstats[1, :H],
            dtstats[0, :H],
            stats[5, :DI].reshape(H, P_SIZE).sum(axis=1),
            gain_out_grad[0],
        ]

    rows = []
    for a, member in zip(small, range(len(small))):
        full = jnp.stack([vectors[layer][member] for layer in range(layers)])
        full = full.reshape(a.shape[:-1] + (shards, a.shape[-1]))
        rows.append(jnp.moveaxis(full, -2, 0).reshape(shards, -1))
    vector, rest_sent = tie(jnp.concatenate(rows, axis=1), rest_sent)
    summed = sum_over(vector, "fsdp", "seq")
    mine = lax.dynamic_index_in_dim(summed, lax.axis_index("fsdp"), 0, keepdims=False)
    outs = []
    start = 0
    for a in small:
        outs.append(mine[start : start + a.size].reshape(a.shape))
        start += a.size
    in_w = in_weight_rows([big[k][1:] for k in range(layers)], in_width)
    in_w = jnp.swapaxes(in_w, 1, 2)
    out_w = jnp.stack([big[k][0] for k in range(layers)]).astype(F32)
    return (
        block_out, grad[None], outs[0], in_w, outs[1], outs[2], outs[3], outs[4], outs[5],
        outs[6], out_w,
    )


def solution(mesh):
    tokens = P("fsdp", "seq", None)
    vector = P(None, "fsdp")
    matrix = P(None, "fsdp", None)
    channels = P(None, None, "fsdp")
    return jax.shard_map(
        on_device,
        mesh=mesh,
        in_specs=(
            tokens, tokens, vector, matrix, channels, vector, vector, vector, vector, vector,
            matrix,
        ),
        out_specs=(
            tokens, tokens, vector, matrix, channels, vector, vector, vector, vector, vector,
            matrix,
        ),
        check_vma=False,
    )
```

```python
import functools

import jax
import jax.numpy as jnp
from jax import lax
from jax.experimental import pallas as pl
from jax.experimental.pallas import tpu as pltpu
from jax.sharding import PartitionSpec as P

H = 32
P_SIZE = 64
N = 128
D = 1024
DI = 2048
CC = DI + 2 * N
T = 128
WB = 256
HB = WB // P_SIZE
STEPS = DI // WB
HALO = 16
F32 = jnp.float32
BF16 = jnp.bfloat16
EPS = 1e-05
VMEM_LIMIT = 50 * 1024 * 1024

L_STEP, L_CUM, L_CUMF, L_SIG = 0, 32, 64, 96


def dot(a, b):
    return jnp.dot(a, b, preferred_element_type=F32)


def dot_nt(a, b):
    return lax.dot_general(a, b, (((1,), (1,)), ((), ())), preferred_element_type=F32)


def dot_tn(a, b):
    return lax.dot_general(a, b, (((0,), (0,)), ((), ())), preferred_element_type=F32)


def sigmoid(v):
    return 0.5 * jnp.tanh(0.5 * v) + 0.5


def lane_iota(rows, lanes=128):
    return lax.broadcasted_iota(jnp.int32, (rows, lanes), 1)


def row_iota(rows, lanes=128):
    return lax.broadcasted_iota(jnp.int32, (rows, lanes), 0)


def parts_of(packed):
    high = packed.astype(BF16)
    rest = packed - high.astype(F32)
    middle = rest.astype(BF16)
    return jnp.concatenate([high, middle, (rest - middle.astype(F32)).astype(BF16)], axis=1)


def pick(first, rows, lanes, shift):
    row = jnp.bitwise_and(row_iota(rows, lanes), 127)
    head = lax.shift_right_logical(lane_iota(rows, lanes), shift)
    return jnp.where(row == first + head, 1.0, 0.0).astype(BF16)


def head_lanes(first, i):
    return pick(first + HB * i, 384, WB, 6)


def head_tiles(first, i):
    return pick(first + HB * i, 384, HB * 128, 7)


def widen(tiles):
    left = lane_iota(tiles.shape[0]) < P_SIZE
    tile = lambda h: tiles[:, h * 128 : (h + 1) * 128]
    return jnp.concatenate(
        [jnp.where(left, tile(2 * p), tile(2 * p + 1)) for p in range(HB // 2)], axis=1
    )


def halves(tile, axis_rows=True):
    left = lane_iota(tile.shape[0]) < P_SIZE
    zero = jnp.zeros_like(tile)
    return jnp.concatenate([jnp.where(left, tile, zero), jnp.where(left, zero, tile)], axis=0)


def head_rows(heads, i):
    lane = jnp.bitwise_and(lane_iota(16, 384), 127)
    sel = jnp.where(lane == L_CUM + HB * i + row_iota(16, 384), 1.0, 0.0).astype(BF16)
    return dot_nt(sel, heads)


def fill(ext, halo_ref, v_ref):
    ext[0:HALO, :] = halo_ref[...].astype(F32)
    ext[HALO:, :] = v_ref[...].astype(F32)


def conv_block(ext, taps_ref, shift_ref, c):
    total = shift_ref[0:1, :] + taps_ref[0:1, :] * ext[pl.ds(HALO - 3 + c * T, T), :]
    for k in range(1, 4):
        total = total + taps_ref[k : k + 1, :] * ext[pl.ds(HALO - 3 + k + c * T, T), :]
    return total


def state_kernel(
    v_ref, halo_ref, bc_ref, bchalo_ref, dt_ref, taps_ref, shift_ref, bctaps_ref, bcshift_ref,
    prm_ref, f_ref, tot_ref, x_ref, p_ref, p3_ref, b_ref, c_ref, bt_ref, ct_ref, ext, sumw,
    dtw, wxw,
):
    i = pl.program_id(0)
    blocks = v_ref.shape[0] // T

    @pl.when(i == 0)
    def _():
        fill(ext, bchalo_ref, bc_ref)
        lane = lane_iota(T)
        tril = (row_iota(T) >= lane).astype(F32)
        offset = jnp.zeros((1, 128), F32)
        for c in range(blocks):
            rows = pl.ds(c * T, T)
            conv = conv_block(ext, bctaps_ref, bcshift_ref, c)
            act = conv * sigmoid(conv)
            b_ref[rows, :] = act[:, :N].astype(BF16)
            c_ref[rows, :] = act[:, N:].astype(BF16)
            bt_ref[:, rows] = act[:, :N].T.astype(BF16)
            ct_ref[:, rows] = act[:, N:].T.astype(BF16)
            z = dt_ref[rows, :].astype(F32) + prm_ref[0:1, :]
            step = jnp.maximum(z, 0.0) + jnp.log1p(jnp.exp(-jnp.abs(z)))
            decay = step * prm_ref[1:2, :]
            cum = lax.dot_general(
                tril, decay, (((1,), (0,)), ((), ())),
                precision=lax.Precision.HIGHEST, preferred_element_type=F32,
            )
            cumf = cum + offset
            offset = cumf[T - 1 : T, :]
            packed = jnp.where(
                lane < L_CUM, step,
                jnp.where(lane < L_CUMF, cum, jnp.where(lane < L_SIG, cumf, 1.0 / (1.0 + jnp.exp(-z)))),
            )
            p_ref[rows, :] = packed
            p3_ref[rows, :] = parts_of(packed)

    fill(ext, halo_ref, v_ref)
    steps = head_lanes(L_STEP, i)
    sums = head_lanes(L_CUMF, i)
    heads = p3_ref[...]
    sumw[...] = dot(heads, sums)
    dtw[...] = dot(heads, steps)
    tot = sumw[blocks * T - 8 :, :][7:8, :]
    for c in range(blocks):
        rows = pl.ds(c * T, T)
        conv = conv_block(ext, taps_ref, shift_ref, c)
        x = conv * sigmoid(conv)
        x_ref[rows, :] = x
        wxw[rows, :] = (x * (jnp.exp(tot - sumw[rows, :]) * dtw[rows, :])).astype(BF16)
    f_ref[...] = dot(bt_ref[...], wxw[...]).astype(BF16)
    tot_ref[...] = jnp.broadcast_to(jnp.exp(tot), (8, WB))


def scan_kernel(
    x_ref, skip_ref, p3_ref, b_ref, c_ref, bt_ref, y_ref, cb, cumw, dtw,
):
    i = pl.program_id(0)
    blocks = x_ref.shape[0] // T

    @pl.when(i == 0)
    def _():
        causal = row_iota(T) >= lane_iota(T)
        for c in range(blocks):
            rows = pl.ds(c * T, T)
            cb[c] = jnp.where(causal, dot_nt(c_ref[rows, :], b_ref[rows, :]), 0.0)

    steps = head_lanes(L_STEP, i)
    sums = head_tiles(L_CUM, i)
    cumw[...] = dot(p3_ref[...], sums)
    dtw[...] = dot(p3_ref[...], steps)
    turned_all = head_rows(p3_ref[...], i)
    state = None
    for c in range(blocks):
        rows = pl.ds(c * T, T)
        x = x_ref[rows, :]
        cums = cumw[rows, :]
        turned = turned_all[:, c * T : (c + 1) * T]
        xd = x * dtw[rows, :]
        parts = []
        for p in range(HB // 2):
            weights = []
            for h in (2 * p, 2 * p + 1):
                across = turned[h : h + 1, :]
                e = jnp.exp(jnp.minimum(cums[:, h * 128 : (h + 1) * 128] - across, 0.0))
                weights.append((e * cb[c]).astype(BF16))
            parts.append(
                dot(
                    jnp.concatenate(weights, axis=1),
                    halves(xd[:, p * 128 : (p + 1) * 128]).astype(BF16),
                )
            )
        y = jnp.concatenate(parts, axis=1) + skip_ref[0:1, :] * x
        cumx = widen(cums)
        if state is not None:
            y = y + jnp.exp(cumx) * dot(c_ref[rows, :], state.astype(BF16))
        y_ref[rows, :] = y
        if c < blocks - 1:
            tot = cumx[T - 1 : T, :]
            fresh = dot(bt_ref[:, rows], (jnp.exp(tot - cumx) * xd).astype(BF16))
            state = fresh if state is None else state * jnp.exp(tot) + fresh


def grow_factors(p_ref, sel):
    lane = lane_iota(p_ref.shape[0])
    inside = jnp.logical_and(lane >= L_CUMF, lane < L_SIG)
    grow = jnp.where(inside, jnp.exp(jnp.where(inside, p_ref[...], 0.0)), 0.0)
    high = grow.astype(BF16)
    low = (grow - high.astype(F32)).astype(BF16)
    return dot(jnp.concatenate([high, low], axis=1), sel[...])


def gate_kernel(y_ref, gate_ref, p_ref, c_ref, s_ref, gain_ref, out_y_ref, out_ref, sel):
    @pl.when(pl.program_id(0) == 0)
    def _():
        sel[...] = pick(L_CUMF, 256, DI, 6)

    grow = grow_factors(p_ref, sel)
    y = y_ref[...] + grow * dot(c_ref[...], s_ref[...])
    out_y_ref[...] = y
    mixed = y.astype(BF16).astype(F32)
    gate = gate_ref[...]
    gated = mixed * (gate * sigmoid(gate))
    r = lax.rsqrt(jnp.mean(gated * gated, axis=1, keepdims=True) + EPS)
    out_ref[...] = (gated * r * gain_ref[0:1, :]).astype(BF16)


def gate_back_kernel(
    y_ref, gate_ref, dgn_ref, p_ref, ct_ref, gain_ref, dgate_ref, dmix_ref, gg_ref, g_ref, acc,
    sel,
):
    i = pl.program_id(0)

    @pl.when(i == 0)
    def _():
        sel[...] = pick(L_CUMF, 256, DI, 6)
        acc[...] = jnp.zeros_like(acc)
        gg_ref[...] = jnp.zeros_like(gg_ref)

    mixed = y_ref[...].astype(BF16).astype(F32)
    gate = gate_ref[...]
    sig = sigmoid(gate)
    silu = gate * sig
    gated = mixed * silu
    r = lax.rsqrt(jnp.mean(gated * gated, axis=1, keepdims=True) + EPS)
    q = gated * r
    dgn = dgn_ref[...]
    gg_ref[...] += jnp.broadcast_to(jnp.sum(dgn * q, axis=0, keepdims=True), gg_ref.shape)
    dq = dgn * gain_ref[0:1, :]
    dgated = r * (dq - q * jnp.mean(dq * q, axis=1, keepdims=True))
    dgate_ref[...] = (dgated * mixed * (sig * (1.0 + gate * (1.0 - sig)))).astype(BF16)
    dmix = (dgated * silu).astype(BF16)
    dmix_ref[...] = dmix
    grow = grow_factors(p_ref, sel)
    acc[...] += dot(ct_ref[...], (grow * dmix.astype(F32)).astype(BF16))

    @pl.when(i == pl.num_programs(0) - 1)
    def _():
        g_ref[...] = acc[...].astype(BF16)


def conv_back(ext, dext, taps_ref, dv_ref, tail_ref, head_ref, stats_ref, blocks):
    early = dext[0:8, :]
    before = ext[HALO - 8 : HALO, :]
    sums = []
    for k in range(5):
        sums.append(jnp.zeros((1, WB), F32))
        for j in range(3 - k):
            sums[k] = sums[k] + early[j : j + 1, :] * before[5 + k + j : 6 + k + j, :]
    for c in range(blocks):
        v = ext[pl.ds(HALO + c * T, T), :]
        total = None
        for k in (3, 2, 1, 0):
            d = dext[pl.ds(c * T + 3 - k, T), :]
            total = taps_ref[k : k + 1, :] * d if total is None else total + taps_ref[k : k + 1, :] * d
            sums[k] = sums[k] + jnp.sum(d * v, axis=0, keepdims=True)
            if k == 3:
                sums[4] = sums[4] + jnp.sum(d, axis=0, keepdims=True)
        dv_ref[pl.ds(c * T, T), :] = total.astype(BF16)
        if c == blocks - 1:
            tail_ref[...] = total[T - 8 :, :]
    head_ref[...] = dext[0:8, :]
    for k in range(5):
        stats_ref[k : k + 1, :] = sums[k]


def back_inside_kernel(
    x_ref, p3_ref, b_ref, c_ref, dy_ref, dxd_ref, dcbt_ref, cbt, cumw, dtw, first,
):
    i = pl.program_id(0) + first
    blocks = x_ref.shape[0] // T

    @pl.when(pl.program_id(0) == 0)
    def _():
        causal = row_iota(T) <= lane_iota(T)
        for c in range(blocks):
            rows = pl.ds(c * T, T)
            cbt[c] = jnp.where(causal, dot_nt(b_ref[rows, :], c_ref[rows, :]), 0.0)
        dcbt_ref[...] = jnp.zeros_like(dcbt_ref)

    steps = head_lanes(L_STEP, i)
    sums = head_tiles(L_CUM, i)
    cumw[...] = dot(p3_ref[...], sums)
    dtw[...] = dot(p3_ref[...], steps)
    turned_all = head_rows(p3_ref[...], i)
    for c in range(blocks):
        rows = pl.ds(c * T, T)
        cums = cumw[rows, :]
        turned = turned_all[:, c * T : (c + 1) * T]
        xd = x_ref[rows, :] * dtw[rows, :]
        dyb = dy_ref[rows, :]
        dy = dyb.astype(F32)
        dcb = jnp.zeros((T, T), F32)
        for p in range(HB // 2):
            lanes = slice(p * 128, (p + 1) * 128)
            dm = dot_nt(halves(xd[:, lanes]).astype(BF16), dyb[:, lanes])
            weights = []
            for j in range(2):
                h = 2 * p + j
                across = turned[h : h + 1, :]
                e = jnp.exp(jnp.minimum(across - cums[:, h * 128 : (h + 1) * 128], 0.0))
                weights.append((e * cbt[c]).astype(BF16))
                dcb = dcb + dm[j * T : (j + 1) * T, :] * e
            dxd_ref[rows, lanes] = dot(
                jnp.concatenate(weights, axis=1), halves(dy[:, lanes]).astype(BF16)
            )
        dcbt_ref[c] += dcb


def back_kernel(
    v_ref, halo_ref, bc_ref, bchalo_ref, taps_ref, shift_ref, bctaps_ref, bcshift_ref, skip_ref,
    prm_ref, p_ref, p3_ref, b_ref, c_ref, bt_ref, ct_ref, s_ref, gin_ref, dy_ref, y_ref,
    inside_low_ref, inside_high_ref, low_ref, high_ref,
    dv_ref, tail_ref, head_ref, stats_ref, bdv_ref, btail_ref, bhead_ref, bstats_ref,
    ddt_ref, dtstats_ref,
    ext, dext, convs, sigs, cumw, dtw, prods, acc, dbacc, dcacc,
):
    i = pl.program_id(0)
    blocks = v_ref.shape[0] // T
    length = blocks * T

    @pl.when(i == 0)
    def _():
        acc[...] = jnp.zeros_like(acc)
        dbacc[...] = jnp.zeros_like(dbacc)
        dcacc[...] = jnp.zeros_like(dcacc)

    fill(ext, halo_ref, v_ref)
    dext[length:, :] = jnp.zeros((8, WB), F32)
    steps = head_lanes(L_STEP, i)
    sums = head_lanes(L_CUM, i)
    cumw[...] = dot(p3_ref[...], sums)
    dtw[...] = dot(p3_ref[...], steps)
    states = [s_ref[...].astype(F32)]
    for c in range(blocks):
        rows = pl.ds(c * T, T)
        conv = conv_block(ext, taps_ref, shift_ref, c)
        sig = sigmoid(conv)
        convs[rows, :] = conv
        sigs[rows, :] = sig
        cumx, dt = cumw[rows, :], dtw[rows, :]
        tot = cumx[T - 1 : T, :]
        wx = (jnp.exp(tot - cumx) * (conv * sig * dt)).astype(BF16)
        states.append(states[-1] * jnp.exp(tot) + dot(bt_ref[:, rows], wx))

    ch = lax.shift_right_logical(row_iota(WB), 6)
    seg1 = (lane_iota(WB) == HB * i + ch).astype(BF16)
    seg2 = (lane_iota(WB) == 32 + HB * i + ch).astype(BF16)
    final = row_iota(T, WB) == T - 1
    lower = jnp.full((T, WB), i, jnp.int32) < STEPS // 2
    grad = gin_ref[...].astype(F32)
    skip_sum = jnp.zeros((1, WB), F32)
    for c in reversed(range(blocks)):
        rows = pl.ds(c * T, T)
        conv, sig = convs[rows, :], sigs[rows, :]
        x = conv * sig
        cumx, dt = cumw[rows, :], dtw[rows, :]
        tot = cumx[T - 1 : T, :]
        xd = x * dt
        xdb = xd.astype(BF16)
        dyb = dy_ref[rows, :]
        dy = dyb.astype(F32)
        gb = grad.astype(BF16)
        w = jnp.exp(tot - cumx)
        inside = jnp.where(lower, inside_low_ref[rows, :], inside_high_ref[rows, :])
        dxd = inside + w * dot(b_ref[rows, :], gb)
        ey = (jnp.exp(cumx) * dy).astype(BF16)
        wx = (w * xd).astype(BF16)
        dcacc[rows, :] += dot_nt(ey, states[c].astype(BF16))
        dbacc[rows, :] += dot_nt(wx, gb)
        bound = jnp.sum(grad * states[c + 1], axis=0, keepdims=True)
        skip = skip_ref[0:1, :]
        p1 = dy * (y_ref[rows, :] - skip * x) - xdb.astype(F32) * dxd
        p1 = p1 + jnp.where(final, bound, 0.0)
        p2 = x * dxd
        p1h = p1.astype(BF16)
        p2h = p2.astype(BF16)
        sides = (p1h, (p1 - p1h.astype(F32)).astype(BF16), p2h, (p2 - p2h.astype(F32)).astype(BF16))
        for k, side in enumerate(sides):
            prods[rows, k * WB : (k + 1) * WB] = side
        skip_sum = skip_sum + jnp.sum(x * dy, axis=0, keepdims=True)
        dx = dt * dxd + skip * dy
        dext[rows, :] = dx * (sig * (1.0 + conv * (1.0 - sig)))
        grad = grad * jnp.exp(tot) + dot(ct_ref[:, rows], ey)
    acc[...] += dot(prods[...], jnp.concatenate([seg1, seg1, seg2, seg2], axis=0))
    conv_back(ext, dext, taps_ref, dv_ref, tail_ref, head_ref, stats_ref, blocks)
    stats_ref[5:6, :] = skip_sum

    @pl.when(i == pl.num_programs(0) - 1)
    def _():
        fill(ext, bchalo_ref, bc_ref)
        triu = (row_iota(T) <= lane_iota(T)).astype(F32)
        rate = prm_ref[1:2, :]
        rate_sum = jnp.zeros((1, 128), F32)
        bias_sum = jnp.zeros((1, 128), F32)
        for c in range(blocks):
            rows = pl.ds(c * T, T)
            causal = row_iota(T) <= lane_iota(T)
            m = jnp.where(causal, low_ref[c] + high_ref[c], 0.0).astype(BF16)
            db = dbacc[rows, :] + dot(m, c_ref[rows, :])
            dc = dcacc[rows, :] + dot_tn(m, b_ref[rows, :])
            conv = conv_block(ext, bctaps_ref, bcshift_ref, c)
            sig = sigmoid(conv)
            dext[rows, :] = jnp.concatenate([db, dc], axis=1) * (
                sig * (1.0 + conv * (1.0 - sig))
            )
            a = acc[rows, :]
            ddecay = lax.dot_general(
                triu, a, (((1,), (0,)), ((), ())),
                precision=lax.Precision.HIGHEST, preferred_element_type=F32,
            )
            packed = p_ref[rows, :]
            rate_sum = rate_sum + jnp.sum(packed * ddecay, axis=0, keepdims=True)
            dz = (pltpu.roll(a, 96, 1) + rate * ddecay) * pltpu.roll(packed, 32, 1)
            ddt_ref[rows, :] = jnp.where(lane_iota(T) < H, dz, 0.0).astype(BF16)
            bias_sum = bias_sum + jnp.sum(dz, axis=0, keepdims=True)
        conv_back(ext, dext, bctaps_ref, bdv_ref, btail_ref, bhead_ref, bstats_ref, blocks)
        dtstats_ref[0:1, :] = rate_sum * rate
        dtstats_ref[1:2, :] = bias_sum


def whole(shape):
    return pl.BlockSpec(shape, lambda i: (0,) * len(shape))


def wide(rows):
    return pl.BlockSpec((rows, WB), lambda i: (0, i))


def bc_block(rows):
    return pl.BlockSpec((rows, WB), lambda i: (0, STEPS))


def shape_of(shape, dtype):
    return jax.ShapeDtypeStruct(shape, dtype)


def params():
    return pltpu.CompilerParams(vmem_limit_bytes=VMEM_LIMIT)


def cost(flops, moved):
    return pl.CostEstimate(flops=int(flops), bytes_accessed=int(moved), transcendentals=0)


def local_state(r_low, halo, taps, shift, prm):
    length = r_low.shape[0]
    return pl.pallas_call(
        state_kernel,
        name="local_state",
        grid=(STEPS,),
        in_specs=[
            wide(length), wide(HALO), bc_block(length), bc_block(HALO),
            pl.BlockSpec((length, 128), lambda i: (0, CC // 128)),
            wide(4), wide(1), bc_block(4), bc_block(1), whole((8, 128)),
        ],
        out_specs=[
            wide(N), wide(8), wide(length), whole((length, 128)), whole((length, 384)),
            whole((length, N)), whole((length, N)), whole((N, length)), whole((N, length)),
        ],
        out_shape=[
            shape_of((N, DI), BF16), shape_of((8, DI), F32), shape_of((length, DI), F32),
            shape_of((length, 128), F32), shape_of((length, 384), BF16),
            shape_of((length, N), BF16), shape_of((length, N), BF16),
            shape_of((N, length), BF16), shape_of((N, length), BF16),
        ],
        scratch_shapes=[
            pltpu.VMEM((HALO + length, WB), F32), pltpu.VMEM((length, WB), F32),
            pltpu.VMEM((length, WB), F32), pltpu.VMEM((length, WB), BF16),
        ],
        compiler_params=params(),
        cost_estimate=cost(4e9, 8e6),
    )(r_low, halo, r_low, halo, r_low, taps, shift, taps, shift, prm)


def local_scan(x, skip, p3, b, c, bt):
    length = x.shape[0]
    return pl.pallas_call(
        scan_kernel,
        name="local_scan",
        grid=(STEPS,),
        in_specs=[
            wide(length), wide(1), whole((length, 384)),
            whole((length, N)), whole((length, N)), whole((N, length)),
        ],
        out_specs=wide(length),
        out_shape=shape_of((length, DI), F32),
        scratch_shapes=[
            pltpu.VMEM((length // T, T, T), F32), pltpu.VMEM((length, HB * 128), F32),
            pltpu.VMEM((length, WB), F32),
        ],
        compiler_params=params(),
        cost_estimate=cost(1.5e10, 8e6),
    )(x, skip, p3, b, c, bt)


def gate_forward(y, gate, p, c, s_in, gain):
    length = y.shape[0]
    rows = lambda width: pl.BlockSpec((T, width), lambda i: (i, 0))
    return pl.pallas_call(
        gate_kernel,
        name="gate_forward",
        grid=(length // T,),
        in_specs=[rows(DI), rows(DI), rows(128), rows(N), whole((N, DI)), whole((1, DI))],
        out_specs=[rows(DI), rows(DI)],
        out_shape=[shape_of((length, DI), F32), shape_of((length, DI), BF16)],
        scratch_shapes=[pltpu.VMEM((256, DI), BF16)],
        compiler_params=params(),
        cost_estimate=cost(5e9, 15e6),
    )(y, gate, p, c, s_in, gain)


def gate_backward(y, gate, dgn, p, ct, gain):
    length = y.shape[0]
    rows = lambda width: pl.BlockSpec((T, width), lambda i: (i, 0))
    return pl.pallas_call(
        gate_back_kernel,
        name="gate_backward",
        grid=(length // T,),
        in_specs=[
            rows(DI), rows(DI), rows(DI), rows(128),
            pl.BlockSpec((N, T), lambda i: (0, i)), whole((1, DI)),
        ],
        out_specs=[rows(DI), rows(DI), whole((8, DI)), whole((N, DI))],
        out_shape=[
            shape_of((length, DI), BF16), shape_of((length, DI), BF16),
            shape_of((8, DI), F32), shape_of((N, DI), BF16),
        ],
        scratch_shapes=[pltpu.VMEM((N, DI), F32), pltpu.VMEM((256, DI), BF16)],
        compiler_params=params(),
        cost_estimate=cost(1e10, 17e6),
    )(y, gate, dgn, p, ct, gain)


def scan_inside(x, p3, b, c, dy, first):
    length = x.shape[0]
    blocks = length // T
    wide_from = lambda rows: pl.BlockSpec((rows, WB), lambda i: (0, i + first))
    return pl.pallas_call(
        functools.partial(back_inside_kernel, first=first),
        name="scan_inside",
        grid=(STEPS // 2,),
        in_specs=[
            wide_from(length), whole((length, 384)), whole((length, N)),
            whole((length, N)), wide_from(length),
        ],
        out_specs=[wide(length), whole((blocks, T, T))],
        out_shape=[shape_of((length, DI // 2), F32), shape_of((blocks, T, T), F32)],
        scratch_shapes=[
            pltpu.VMEM((blocks, T, T), F32), pltpu.VMEM((length, HB * 128), F32),
            pltpu.VMEM((length, WB), F32),
        ],
        compiler_params=params(),
        cost_estimate=cost(1e10, 6e6),
    )(x, p3, b, c, dy)


def scan_backward(
    r_low, halo, taps, shift, skip, prm, p, p3, b, c, bt, ct, s_in, g_in, dy, y, low, high
):
    length = r_low.shape[0]
    blocks = length // T
    return pl.pallas_call(
        back_kernel,
        name="scan_backward",
        grid=(STEPS,),
        in_specs=[
            wide(length), wide(HALO), bc_block(length), bc_block(HALO),
            wide(4), wide(1), bc_block(4), bc_block(1), wide(1), whole((8, 128)),
            whole((length, 128)), whole((length, 384)), whole((length, N)), whole((length, N)),
            whole((N, length)), whole((N, length)), wide(N), wide(N), wide(length), wide(length),
            pl.BlockSpec((length, WB), lambda i: (0, jnp.minimum(i, STEPS // 2 - 1))),
            pl.BlockSpec((length, WB), lambda i: (0, jnp.maximum(i - STEPS // 2, 0))),
            whole((blocks, T, T)), whole((blocks, T, T)),
        ],
        out_specs=[
            wide(length), wide(8), wide(8), wide(8),
            whole((length, WB)), whole((8, WB)), whole((8, WB)), whole((8, WB)),
            whole((length, 128)), whole((8, 128)),
        ],
        out_shape=[
            shape_of((length, DI), BF16), shape_of((8, DI), F32), shape_of((8, DI), F32),
            shape_of((8, DI), F32),
            shape_of((length, WB), BF16), shape_of((8, WB), F32), shape_of((8, WB), F32),
            shape_of((8, WB), F32),
            shape_of((length, 128), BF16), shape_of((8, 128), F32),
        ],
        scratch_shapes=[
            pltpu.VMEM((HALO + length, WB), F32),
            pltpu.VMEM((length + 8, WB), F32),
            pltpu.VMEM((length, WB), F32),
            pltpu.VMEM((length, WB), F32),
            pltpu.VMEM((length, WB), F32),
            pltpu.VMEM((length, WB), F32),
            pltpu.VMEM((length, 4 * WB), BF16),
            pltpu.VMEM((length, 128), F32),
            pltpu.VMEM((length, 128), F32),
            pltpu.VMEM((length, 128), F32),
        ],
        compiler_params=params(),
        cost_estimate=cost(3e10, 16e6),
    )(
        r_low, halo, r_low, halo, taps, shift, taps, shift, skip, prm, p, p3, b, c, bt, ct,
        s_in, g_in, dy, y, low[0], high[0], low[1], high[1],
    )


def add(a, b):
    return (a.astype(F32) + b.astype(F32)).astype(BF16)


def swap(a, axis, bit):
    return lax.ppermute(a, axis, [(k, k ^ bit) for k in range(lax.axis_size(axis))])


def hop_to(message, state, hop, upward):
    last = lax.axis_size("seq") - 1
    pair = (hop, hop + 1) if upward else (last - hop, last - hop - 1)
    got = lax.ppermute(message, "seq", [pair])
    return got if state is None else got + state


def message_of(local, decay, state):
    return (local.astype(F32) + decay * state.astype(F32)).astype(BF16)


def pass_along(local, decay, upward, work):
    hops = lax.axis_size("seq") - 1
    state = None
    done = []
    for hop in range(hops):
        message = local if hop == 0 else message_of(local, decay, state)
        state = hop_to(message, state, hop, upward)
        if work:
            item = work[0]()
            work = work[1:]
            state, item = lax.optimization_barrier((state, item))
            done.append(item)
    for item in work:
        done.append(item())
    return state, done


def pieces_kernel(order_ref, left_ref, base_ref, *refs):
    del order_ref
    for m, piece in enumerate(refs[:-1]):

        @pl.when(pl.program_id(0) == m)
        def _(m=m, piece=piece):
            total = base_ref[...] if m == 0 else refs[-1][...]
            refs[-1][...] = total + dot(left_ref[...], piece[...])


def pieces_back_kernel(order_ref, left_ref, *refs):
    del order_ref
    for m, piece in enumerate(refs[:-1]):

        @pl.when(pl.program_id(0) == m)
        def _(piece=piece):
            refs[-1][...] = dot_nt(left_ref[...], piece[...])


def xor_order():
    n = lax.axis_size("fsdp")
    return jnp.bitwise_xor(lax.axis_index("fsdp"), jnp.arange(n)).astype(jnp.int32)


def fixed(shape):
    return pl.BlockSpec(shape, lambda i, order: (0,) * len(shape))


def add_product(base, left, w):
    if not isinstance(w, list):
        return base + dot(left, w)
    return pl.pallas_call(
        pieces_kernel,
        name="add_product",
        grid_spec=pltpu.PrefetchScalarGridSpec(
            num_scalar_prefetch=1,
            grid=(len(w),),
            in_specs=[
                pl.BlockSpec((left.shape[0], w[0].shape[0]), lambda i, order: (0, order[i])),
                fixed(base.shape),
            ]
            + [fixed(w[0].shape)] * len(w),
            out_specs=fixed(base.shape),
        ),
        out_shape=shape_of(base.shape, F32),
        compiler_params=params(),
        cost_estimate=cost(2e9, 10e6),
    )(xor_order(), left, base, *w)


def product_back(left, w):
    if not isinstance(w, list):
        return dot_nt(left, w)
    length = left.shape[0]
    return pl.pallas_call(
        pieces_back_kernel,
        name="product_back",
        grid_spec=pltpu.PrefetchScalarGridSpec(
            num_scalar_prefetch=1,
            grid=(len(w),),
            in_specs=[fixed(left.shape)] + [fixed(w[0].shape)] * len(w),
            out_specs=pl.BlockSpec((length, w[0].shape[0]), lambda i, order: (0, order[i])),
        ),
        out_shape=shape_of((length, len(w) * w[0].shape[0]), F32),
        compiler_params=params(),
        cost_estimate=cost(2e9, 10e6),
    )(xor_order(), left, *w)


def give_kernel(left_ref, right_ref, out_ref):
    out_ref[...] = dot_tn(left_ref[...], right_ref[...]).astype(BF16)


def own_kernel(left_ref, right_ref, got_ref, *out_refs):
    value = dot_tn(left_ref[...], right_ref[...]) + got_ref[...].astype(F32)
    rows = out_refs[0].shape[0]
    for d, out_ref in enumerate(out_refs):
        out_ref[...] = value[d * rows : (d + 1) * rows].astype(BF16)


def shard_columns(left, core):
    n = lax.axis_size("fsdp")
    me = lax.axis_index("fsdp")
    width = left.shape[1] // n
    return jnp.concatenate(
        [
            lax.dynamic_slice_in_dim(left, jnp.bitwise_xor(me, 2 * d + core) * width, width, 1)
            for d in range(n // 2)
        ],
        axis=1,
    )


def product_give(left, right):
    length, rows = left.shape
    columns = right.shape[1]
    block = columns // 2 if columns % 256 == 0 else columns
    return pl.pallas_call(
        give_kernel,
        name="product_give",
        grid=(columns // block,),
        in_specs=[whole((length, rows)), pl.BlockSpec((length, block), lambda i: (0, i))],
        out_specs=pl.BlockSpec((rows, block), lambda i: (0, i)),
        out_shape=shape_of((rows, columns), BF16),
        compiler_params=params(),
        cost_estimate=cost(3e9, 8e6),
    )(left, right)


def product_own(left, right, got):
    chips = lax.axis_size("fsdp") // 2
    length, rows = left.shape
    columns = right.shape[1]
    block = columns // 2 if columns % 256 == 0 else columns
    blocks = lambda height: pl.BlockSpec((height, block), lambda i: (0, i))
    return pl.pallas_call(
        own_kernel,
        name="product_own",
        grid=(columns // block,),
        in_specs=[whole((length, rows)), blocks(length), blocks(rows)],
        out_specs=[blocks(rows // chips)] * chips,
        out_shape=[shape_of((rows // chips, columns), BF16)] * chips,
        compiler_params=params(),
        cost_estimate=cost(3e9, 10e6),
    )(left, right, got)


def send_chips(parts):
    return parts[0], [swap(part, "fsdp", 2 * d) for d, part in enumerate(parts) if d]


def gather_sum(own, got):
    total = own.astype(F32)
    for piece in got:
        total = total + piece.astype(F32)
    return total.astype(BF16)


def tie(*values):
    return lax.optimization_barrier(values)


def seq_first(a):
    odd = lax.axis_index("seq") % 2
    half = a.shape[0] // 2
    keep = lax.dynamic_slice_in_dim(a, odd * half, half, 0)
    give = lax.dynamic_slice_in_dim(a, (1 - odd) * half, half, 0)
    return keep, swap(give, "seq", 1)


def seq_across(keep, got):
    keep = add(keep, got)
    bit = 2
    while 2 * bit < lax.axis_size("seq"):
        keep = add(keep, swap(keep, "seq", bit))
        bit *= 2
    return keep, swap(keep, "seq", bit)


def seq_back(keep, got):
    keep = add(keep, got)
    return keep, swap(keep, "seq", 1)


def seq_join(keep, other):
    odd = lax.axis_index("seq") % 2
    return jnp.where(
        odd == 0, jnp.concatenate([keep, other]), jnp.concatenate([other, keep])
    )


def sum_over(a, *axes):
    for axis in axes:
        bit = 1
        while bit < lax.axis_size(axis):
            a = a + swap(a, axis, bit)
            bit *= 2
    return a


def turn_kernel(*refs):
    out_ref = refs[-1]
    for k in range(len(refs) // 2):
        row = 0
        for ref in refs[2 * k : 2 * k + 2]:
            for j in range(0, ref.shape[1], 128):
                rows = min(128, out_ref.shape[1] - row)
                tile = ref[:, j : j + 128].astype(F32).T
                out_ref[k, row : row + rows, :] = tile[:rows, :]
                row += rows


def in_weight_rows(pieces, in_width):
    flat = [piece for pair in pieces for piece in pair]
    return pl.pallas_call(
        turn_kernel,
        name="in_weight_rows",
        out_shape=shape_of((len(pieces), in_width, flat[0].shape[0]), F32),
        compiler_params=params(),
        cost_estimate=cost(0, 7e6),
    )(*flat)


def on_device(
    hidden_in, cotangent, norm_gain, input_projection_weight, conv_weight, conv_bias, dt_bias,
    a_log, skip, gate_gain, output_projection_weight,
):
    layers, _, in_width = input_projection_weight.shape
    seq_parts = lax.axis_size("seq")
    up = [(z, z + 1) for z in range(seq_parts - 1)]
    down = [(z + 1, z) for z in range(seq_parts - 1)]

    small = [norm_gain, conv_weight, conv_bias, dt_bias, a_log, skip, gate_gain]
    flat = jnp.concatenate([a.reshape(layers, -1) for a in small], axis=1)
    shards = lax.axis_size("fsdp")
    packed = lax.all_gather(flat, "fsdp", axis=0)
    packed = packed.astype(F32)
    unpacked = []
    start = 0
    for a in small:
        width = a[0].size
        piece = packed[:, :, start : start + width].reshape((shards,) + a.shape)
        start += width
        piece = jnp.moveaxis(piece, 0, -2)
        unpacked.append(piece.reshape(a.shape[:-1] + (shards * a.shape[-1],)))
    gains, taps_all, shift_all, bias_all, rate_all, skip_all, gate_all = unpacked

    by_pieces = output_projection_weight.shape[1] % 128 == 0
    weights = []
    for layer in range(layers):
        w = input_projection_weight[layer]
        rest = jnp.concatenate([w[:, DI : DI + CC]] + [w[:, DI + CC :]] * 4, axis=1)
        rest = lax.all_gather(rest, "fsdp", axis=0, tiled=True)
        if layer == 0:
            rest, first_out = tie(rest, output_projection_weight[0])
            if by_pieces:
                near = swap(first_out, "fsdp", 1)
                arrived = [swap(first_out, "fsdp", 2 * d) for d in range(1, shards // 2)]
        weights.append(
            (
                rest,
                lax.all_gather(w[:, :DI], "fsdp", axis=0, tiled=True),
                None
                if layer == 0 and by_pieces
                else lax.all_gather(output_projection_weight[layer], "fsdp", axis=0, tiled=True),
            )
        )

    hidden = hidden_in[0].astype(F32)
    stored = []
    for layer in range(layers):
        w_rest, w_gate, w_out = weights[layer]
        r_in = lax.rsqrt(jnp.mean(hidden * hidden, axis=1, keepdims=True) + EPS)
        normed = (hidden * r_in * gains[layer][None, :]).astype(BF16)
        r_low = dot(normed, w_rest).astype(BF16)
        halo = lax.ppermute(r_low[-HALO:, :CC], "seq", up)
        taps = taps_all[layer]
        shift = shift_all[layer][None, :]
        skip_wide = jnp.repeat(skip_all[layer], P_SIZE)[None, :]
        prm = jnp.zeros((8, 128), F32)
        prm = prm.at[0].set(jnp.tile(bias_all[layer], 4))
        prm = prm.at[1].set(jnp.tile(-jnp.exp(rate_all[layer]), 4))
        f, decay, x, p, p3, b, c, bt, ct = local_state(r_low, halo, taps, shift, prm)
        state = hop_to(f, None, 0, True)
        y = local_scan(x, skip_wide, p3, b, c, bt)
        state, y = tie(state, y)
        if w_out is None:
            y, arrived = tie(y, arrived)
            swapped = [swap(piece, "fsdp", 1) for piece in arrived]
        for hop in range(1, seq_parts - 1):
            state = hop_to(message_of(f, decay[0:1], state), state, hop, True)
            if hop == 1:
                gate = dot(normed, w_gate)
                state, gate = tie(state, gate)
                if w_out is None:
                    gate, swapped = tie(gate, swapped)
                    w_out = [first_out, near]
                    for pair in zip(arrived, swapped):
                        w_out += pair
                    weights[layer] = (w_rest, w_gate, w_out)
        s_in = state
        y, gate_low = gate_forward(y, gate, p, c, s_in, gate_all[layer][None, :])
        stored.append(
            (
                hidden, r_in, normed, r_low, halo, gate, taps, shift, skip_wide, prm, decay, x, p,
                p3, b, c, bt, ct, s_in, y, gate_low,
            )
        )
        hidden = add_product(hidden, gate_low, w_out)
    block_out = hidden.astype(BF16)[None]

    block_out, cotangent = tie(block_out, cotangent)
    grad = cotangent[0].astype(F32)
    big = [None] * layers
    vectors = [None] * layers
    waiting = None
    for layer in reversed(range(layers)):
        (
            hidden, r_in, normed, r_low, halo, gate, taps, shift, skip_wide, prm, decay, x, p,
            p3, b, c, bt, ct, s_in, y, gate_low,
        ) = stored[layer]
        w_rest, w_gate, w_out = weights[layer]
        d_branch = grad.astype(BF16)
        dgn = product_back(d_branch, w_out)
        dgate, dmix, gain_out_grad, g_local = gate_backward(
            y, gate, dgn, p, ct, gate_all[layer][None, :]
        )

        if waiting is not None:
            scattered, g_local = tie(scattered, g_local)
            big[layer + 1] = [lax.psum(a, "seq") for a in scattered]

        normed_give, normed_own = shard_columns(normed, 1), shard_columns(normed, 0)
        inside = lambda first: scan_inside(x, p3, b, c, dmix, first)
        if layer == 0:
            out_give = product_give(shard_columns(gate_low, 1), d_branch)
            state = hop_to(g_local, None, 0, False)
            low = inside(0)
            state, out_give, low = tie(state, out_give, low)
            for hop in range(1, seq_parts - 1):
                state = hop_to(message_of(g_local, decay[0:1], state), state, hop, False)
                if hop == 1:
                    out_got = swap(out_give, "fsdp", 1)
                    gate_give = product_give(normed_give, dgate)
                    high = inside(STEPS // 2)
                    state, gate_give, high, rest_sent = tie(state, gate_give, high, rest_sent)
                    above = seq_first(gather_sum(rest_mine, rest_sent))
                    gate_got = swap(gate_give, "fsdp", 1)
                    out_parts = product_own(shard_columns(gate_low, 0), d_branch, out_got)
                elif hop == 2:
                    out_parts, state = tie(out_parts, state)
                    out_mine, out_sent = send_chips(out_parts)
                    state, gate_got, above = tie(state, gate_got, above)
                    above = seq_across(*above)
                    gate_parts = product_own(normed_own, dgate, gate_got)
                    state, gate_parts = tie(state, gate_parts)
                    gate_mine, gate_sent = send_chips(gate_parts)
        else:
            state, ((out_grad, gate_w_grad), low, high) = pass_along(
                g_local,
                decay[0:1],
                False,
                [
                    lambda: (
                        dot_tn(gate_low, d_branch).astype(BF16),
                        dot_tn(normed, dgate).astype(BF16),
                    ),
                    lambda: inside(0),
                    lambda: inside(STEPS // 2),
                ],
            )
            scattered = [
                lax.psum_scatter(a, "fsdp", scatter_dimension=0, tiled=True)
                for a in (out_grad, gate_w_grad)
            ]
        back = scan_backward(
            r_low, halo, taps, shift, skip_wide, prm, p, p3, b, c, bt, ct, s_in, state, dmix, y,
            low, high,
        )
        if layer == 0:
            back, out_sent, above, big[layer + 1] = tie(back, out_sent, above, big[layer + 1])
            big[layer + 1].append(seq_join(*seq_back(*above)))
            out_seq = seq_first(gather_sum(out_mine, out_sent))
        dv, tail, head, stats, bdv, btail, bhead, bstats, ddt, dtstats = back
        heads_in = lax.ppermute(jnp.concatenate([head, bhead], axis=1), "seq", down)
        tail = jnp.concatenate([tail, btail], axis=1)
        fix = [tail[j : j + 1] for j in range(8)]
        for j in range(3):
            for k in range(j + 1):
                fix[5 + j] = fix[5 + j] + taps[k : k + 1] * heads_in[j - k : j - k + 1]
        d_rest = jnp.concatenate([dv, bdv, ddt], axis=1)
        d_rest = lax.dynamic_update_slice(
            d_rest, jnp.concatenate(fix, axis=0).astype(BF16), (d_rest.shape[0] - 8, 0)
        )
        got = swap(product_give(normed_give, d_rest), "fsdp", 1)
        d_normed = dot_nt(dgate, w_gate)
        got, d_normed = tie(got, d_normed)
        if layer == 0:
            out_seq, d_rest = tie(out_seq, d_rest)
            out_seq = seq_across(*out_seq)
        else:
            parts = product_own(normed_own, d_rest, got)
            parts, d_rest = tie(parts, d_rest)
            rest_mine, rest_sent = send_chips(parts)
        d_normed = d_normed + dot_nt(d_rest, w_rest)
        q = hidden * r_in
        dq = d_normed * gains[layer][None, :]
        gain_in_grad = jnp.sum(d_normed * q, axis=0)
        grad = grad + r_in * (dq - q * jnp.mean(dq * q, axis=1, keepdims=True))
        if layer == 0:
            grad, gain_in_grad, got = tie(grad, gain_in_grad, got)
            parts = product_own(normed_own, d_rest, got)
            parts, gate_sent = tie(parts, gate_sent)
            rest_mine, rest_sent = send_chips(parts)
            gate_seq = seq_first(gather_sum(gate_mine, gate_sent))
            out_seq, gate_seq = tie(out_seq, gate_seq)
            out_seq = seq_back(*out_seq)
            gate_seq = seq_across(*gate_seq)
            out_seq, gate_seq, rest_sent = tie(out_seq, gate_seq, rest_sent)
            rest_seq = seq_first(gather_sum(rest_mine, rest_sent))
            gate_seq = seq_back(*gate_seq)
            rest_seq = seq_back(*seq_across(*rest_seq))
            big[layer] = [seq_join(*out_seq), seq_join(*gate_seq), seq_join(*rest_seq)]
        waiting = layer
        stats = jnp.concatenate([stats, bstats], axis=1)
        vectors[layer] = [
            gain_in_grad,
            stats[0:4],
            stats[4],
            dtstats[1, :H],
            dtstats[0, :H],
            stats[5, :DI].reshape(H, P_SIZE).sum(axis=1),
            gain_out_grad[0],
        ]

    rows = []
    for a, member in zip(small, range(len(small))):
        full = jnp.stack([vectors[layer][member] for layer in range(layers)])
        full = full.reshape(a.shape[:-1] + (shards, a.shape[-1]))
        rows.append(jnp.moveaxis(full, -2, 0).reshape(shards, -1))
    vector, rest_sent = tie(jnp.concatenate(rows, axis=1), rest_sent)
    summed = sum_over(vector, "fsdp", "seq")
    mine = lax.dynamic_index_in_dim(summed, lax.axis_index("fsdp"), 0, keepdims=False)
    outs = []
    start = 0
    for a in small:
        outs.append(mine[start : start + a.size].reshape(a.shape))
        start += a.size
    in_w = in_weight_rows([big[k][1:] for k in range(layers)], in_width)
    in_w = jnp.swapaxes(in_w, 1, 2)
    out_w = jnp.stack([big[k][0] for k in range(layers)]).astype(F32)
    return (
        block_out, grad[None], outs[0], in_w, outs[1], outs[2], outs[3], outs[4], outs[5],
        outs[6], out_w,
    )


def solution(mesh):
    tokens = P("fsdp", "seq", None)
    vector = P(None, "fsdp")
    matrix = P(None, "fsdp", None)
    channels = P(None, None, "fsdp")
    return jax.shard_map(
        on_device,
        mesh=mesh,
        in_specs=(
            tokens, tokens, vector, matrix, channels, vector, vector, vector, vector, vector,
            matrix,
        ),
        out_specs=(
            tokens, tokens, vector, matrix, channels, vector, vector, vector, vector, vector,
            matrix,
        ),
        check_vma=False,
    )
```
